128 devices in a mesh: row: 16 (over x_hi, y, core), col: 8 (over z, x_lo).
Axes of the slice: x: 4 (x_hi: 2, x_lo: 2; x = x_hi * 2 + x_lo), y: 4, z: 4, core: 2. Of those that a mesh axis runs over, the one named last changes fastest.
Arguments:
- tokens: bfloat16 [16384, 2048], P(('row', 'col')), may hold values from -6 to 6
- doc_lengths: int32 [16, 3], P('row'), may hold values from 0 to 1024, as said below
- input_gain: bfloat16 [2048], replicated, may hold values from 0.25 to 1.75
- input_shift: bfloat16 [2048], replicated, may hold values from -1.75 to 1.75
- post_gain: bfloat16 [2048], replicated, may hold values from 0.25 to 1.75
- post_shift: bfloat16 [2048], replicated, may hold values from -1.75 to 1.75
- qkv_weight: bfloat16 [2048, 6144], P('row', 'col'), may hold values from -0.125 to 0.125
- qkv_bias: bfloat16 [6144], P(('col', 'row')), may hold values from -1.75 to 1.75
- dense_weight: bfloat16 [2048, 2048], P('col', 'row'), may hold values from -1 to 1
- dense_bias: bfloat16 [2048], replicated, may hold values from -1.75 to 1.75
- up_weight: bfloat16 [2048, 8192], P('row', 'col'), may hold values from -0.125 to 0.125
- up_bias: bfloat16 [8192], P(('col', 'row')), may hold values from -3 to 3
- down_weight: bfloat16 [8192, 2048], P('col', 'row'), may hold values from -0.0625 to 0.0625
- down_bias: bfloat16 [2048], replicated, may hold values from -1.75 to 1.75
- cotangent: bfloat16 [16384, 2048], P(('row', 'col')), may hold values from -6 to 6
Outputs:
- layer_out: bfloat16 [16384, 2048], P(('row', 'col'))
- input_grad: bfloat16 [16384, 2048], P(('row', 'col'))
- input_gain_grad: float32 [2048], replicated
- input_shift_grad: float32 [2048], replicated
- post_gain_grad: float32 [2048], replicated
- post_shift_grad: float32 [2048], replicated
- qkv_weight_grad: float32 [2048, 6144], P('row', 'col')
- qkv_bias_grad: float32 [6144], P(('col', 'row'))
- dense_weight_grad: float32 [2048, 2048], P('col', 'row')
- dense_bias_grad: float32 [2048], replicated
- up_weight_grad: float32 [2048, 8192], P('row', 'col')
- up_bias_grad: float32 [8192], P(('col', 'row'))
- down_weight_grad: float32 [8192, 2048], P('col', 'row')
- down_bias_grad: float32 [2048], replicated
The draws below stay inside these ranges and needn't reach their ends.
Inputs may be any that keep to these rules, and one draw needn't show every extreme that they name: `doc_lengths`: each row lists the 3 documents of one group of 1024 tokens in order and sums to 1024; a zero is an empty document. In every row one document begins within the group's first 128 tokens and ends within its last 128.
All inputs are finite; a program needn't handle non-finite values.
Results may differ from the reference program's by a relative error of at most 0.023.
Values may be sent and summed in bfloat16 or wider, within the bound.
No kernel may reach another device: no remote copies, remote signals or barrier semaphores. Data moves between devices by JAX's collectives and lax.ppermute only.
A program may use at most 128 MiB of HBM per device.

```python
import math
import jax
import jax.numpy as jnp
from jax import lax

D = 2048
HEADS = 8
HS = 256
FF = 8192
ROT = 64
TOK_DEV = 128
SEQ_GRP = 3
GROUP_TOK = 1024
GROUPS = 16
TOKENS = 16384


def draw_doc_lengths(key, part):
    key = jax.random.fold_in(key, 7)
    lead_key, front_key, back_key, pick_key = jax.random.split(key, 4)
    leading = jax.random.randint(lead_key, (GROUPS,), 0, SEQ_GRP)
    front_cuts = jax.random.randint(front_key, (GROUPS, SEQ_GRP - 1), 0, TOK_DEV)
    back_cuts = jax.random.randint(back_key, (GROUPS, SEQ_GRP - 1), GROUP_TOK - TOK_DEV + 1, GROUP_TOK + 1)
    slot_index = jnp.arange(SEQ_GRP - 1)
    cut_points = jnp.where(slot_index[None, :] < leading[:, None], front_cuts, back_cuts)
    cut_points = jnp.sort(cut_points, axis=1)
    chosen = jax.random.randint(pick_key, (), 0, GROUPS)
    full_group = (jnp.arange(GROUPS) == chosen)[:, None]
    cut_points = jnp.where(full_group, GROUP_TOK, cut_points).astype(jnp.int32)
    boundary = jnp.concatenate([jnp.zeros((GROUPS, 1), jnp.int32), cut_points, jnp.full((GROUPS, 1), GROUP_TOK, jnp.int32)], axis=1)
    return (boundary[:, 1:] - boundary[:, :-1]).astype(jnp.int32)


def level_of(rng, shape, cuts, smallest, largest):
    level = 1.0
    for position, parts in cuts:
        steps = jax.random.uniform(jax.random.fold_in(jax.random.fold_in(rng, 6), position), (parts,), jnp.float32, smallest / len(cuts), largest / len(cuts))
        level = level * jnp.repeat(jnp.exp(steps), shape[position] // parts).reshape((-1,) + (1,) * (len(shape) - 1 - position))
    return level


def gaussian(own_key, extent, spread, bound, shards=(), kind=jnp.bfloat16):
    values = jax.random.normal(own_key, extent, jnp.float32) * spread
    if len(shards) > 0:
        values = level_of(own_key, extent, shards, -0.22, 0.18) * values
    return jnp.clip(values, min=-bound, max=bound).astype(kind)


def setup_inputs(seed: int = 0) -> dict:
    seeds = jax.random.split(jax.random.key(seed), 16)
    tokens = gaussian(seeds[0], (TOKENS, D), 1.0, 6.0, ((0, 128),))
    doc_lengths = draw_doc_lengths(jax.random.fold_in(seeds[15], 71), 0)
    input_gain = jnp.clip(1.0 + 0.15 * jax.random.normal(seeds[2], (D,), jnp.float32), 0.25, 1.75).astype(jnp.bfloat16)
    input_shift = gaussian(seeds[3], (D,), 0.3, 1.75)
    post_gain = jnp.clip(1.0 + 0.15 * jax.random.normal(seeds[4], (D,), jnp.float32), 0.25, 1.75).astype(jnp.bfloat16)
    post_shift = gaussian(seeds[5], (D,), 0.3, 1.75)
    qkv_weight = gaussian(seeds[6], (D, 3 * D), D ** -0.5, 0.125, ((0, 16), (1, 8)))
    qkv_bias = gaussian(seeds[7], (3 * D,), 0.3, 1.75, ((0, 128),))
    dense_weight = gaussian(seeds[8], (D, D), (max(D // 64, 1)) ** -0.5, 1.0, ((0, 8), (1, 16)))
    dense_bias = gaussian(seeds[9], (D,), 0.3, 1.75)
    up_weight = gaussian(seeds[10], (D, FF), D ** -0.5, 0.125, ((0, 16), (1, 8)))
    up_bias = gaussian(seeds[11], (FF,), 0.5, 3.0, ((0, 128),))
    down_weight = gaussian(seeds[12], (FF, D), FF ** -0.5, 0.0625, ((0, 8), (1, 16)))
    down_bias = gaussian(seeds[13], (D,), 0.3, 1.75)
    cotangent = gaussian(seeds[14], (TOKENS, D), 1.0, 6.0, ((0, 128),))
    return {"tokens": tokens, "doc_lengths": doc_lengths, "input_gain": input_gain, "input_shift": input_shift, "post_gain": post_gain, "post_shift": post_shift, "qkv_weight": qkv_weight, "qkv_bias": qkv_bias, "dense_weight": dense_weight, "dense_bias": dense_bias, "up_weight": up_weight, "up_bias": up_bias, "down_weight": down_weight, "down_bias": down_bias, "cotangent": cotangent}


@jax.custom_vjp
def low(v):
    return lax.optimization_barrier(v.astype(jnp.bfloat16)).astype(jnp.float32)

@jax.custom_vjp
def low_back(v):
    return v

def low_keep(v):
    return (low(v), None)

def low_pass(kept, grad):
    return (grad,)

def back_keep(v):
    return (v, None)

def back_low(kept, grad):
    return (low(grad),)
low.defvjp(low_keep, low_pass)
low_back.defvjp(back_keep, back_low)

def matmul(left, right):
    return jnp.dot(left, right, precision=lax.Precision.HIGHEST, preferred_element_type=jnp.float32)

def layer_norm(tok_rows, gain, shift):
    center_mean = lax.optimization_barrier(jnp.mean(tok_rows, axis=-1, keepdims=True))
    centered = tok_rows - center_mean
    variance = lax.optimization_barrier(jnp.mean(centered * centered, axis=-1, keepdims=True))
    return centered * lax.rsqrt(variance + 1e-05) * gain + shift

def doc_layout(lengths, row_count):
    ends = jnp.cumsum(lengths, dtype=jnp.int32).astype(jnp.int32)
    places = jnp.arange(row_count, dtype=jnp.int32)
    passed = places[:, None] >= ends[None, :]
    doc_ids = lax.optimization_barrier(jnp.sum(passed.astype(jnp.int32), axis=1, dtype=jnp.int32)).astype(jnp.int32)
    begins = lax.optimization_barrier(jnp.sum(jnp.where(passed, lengths[None, :], 0), axis=1, dtype=jnp.int32)).astype(jnp.int32)
    return (doc_ids, places - begins)

def rotary_tables(positions, width):
    half_width = width // 2
    frequency = 1.0 / 10000.0 ** (jnp.arange(half_width, dtype=jnp.float32) * (2.0 / width))
    angles = positions.astype(jnp.float32)[:, None] * frequency[None, :]
    return (jnp.cos(angles)[:, None, :], jnp.sin(angles)[:, None, :])

def rotate(portion, cosine, sine_part):
    half_width = cosine.shape[-1]
    lead_part = portion[..., :half_width]
    tail_part = portion[..., half_width:2 * half_width]
    return jnp.concatenate([lead_part * cosine - tail_part * sine_part, tail_part * cosine + lead_part * sine_part, portion[..., 2 * half_width:]], axis=-1)

def gelu_exact(values):
    return 0.5 * values * (1.0 + lax.erf(values * (1.0 / math.sqrt(2.0))))

def group_forward(tok_rows, lengths, params):
    input_gain, input_shift, post_gain, post_shift, qkv_weight, qkv_bias, dense_weight, dense_bias, up_weight, up_bias, down_weight, down_bias = params
    row_count = tok_rows.shape[0]
    doc_ids, positions = doc_layout(lengths, row_count)
    first_norm = low(layer_norm(tok_rows, input_gain, input_shift))
    second_norm = low(layer_norm(tok_rows, post_gain, post_shift))
    mixture = low_back(matmul(first_norm, qkv_weight) + qkv_bias).reshape(row_count, HEADS, 3, HS)
    cosine, sine_part = rotary_tables(positions, ROT)
    queries = low(rotate(mixture[:, :, 0], cosine, sine_part))
    key_rows = low(rotate(mixture[:, :, 1], cosine, sine_part))
    values = low(mixture[:, :, 2])
    scores = jnp.einsum('qhe,khe->hqk', queries, key_rows, precision=lax.Precision.HIGHEST) * HS ** (-0.5)
    scores = low_back(scores)
    places = jnp.arange(row_count, dtype=jnp.int32)
    allowed = (doc_ids[:, None] == doc_ids[None, :]) & (places[None, :] <= places[:, None])
    scores = jnp.where(allowed[None], scores, -1e+30)
    row_max = lax.optimization_barrier(jnp.max(scores, axis=-1, keepdims=True))
    raised = jnp.exp(scores - row_max)
    soft_weights = raised / lax.optimization_barrier(jnp.sum(raised, axis=-1, keepdims=True))
    probabilities = low(soft_weights)
    attended = jnp.einsum('hqk,khe->qhe', probabilities, values, precision=lax.Precision.HIGHEST)
    attended = low(low_back(attended)).reshape(row_count, HEADS * HS)
    hidden = low_back(matmul(second_norm, up_weight) + up_bias)
    active = low(gelu_exact(hidden))
    return tok_rows + matmul(attended, dense_weight) + dense_bias + matmul(active, down_weight) + down_bias

def reference(tokens, doc_lengths, input_gain, input_shift, post_gain, post_shift, qkv_weight, qkv_bias, dense_weight, dense_bias, up_weight, up_bias, down_weight, down_bias, cotangent):
    params = tuple((member.astype(jnp.float32) for member in (input_gain, input_shift, post_gain, post_shift, qkv_weight, qkv_bias, dense_weight, dense_bias, up_weight, up_bias, down_weight, down_bias)))
    grouped = tokens.astype(jnp.float32).reshape(GROUPS, GROUP_TOK, D)

    def forward(group_rows, weights):

        def one_group(packed):
            return group_forward(packed[0], packed[1], weights)
        return lax.map(jax.checkpoint(one_group), (group_rows, doc_lengths))
    output, pullback = jax.vjp(forward, grouped, params)
    grad_rows, grad_params = pullback(cotangent.astype(jnp.float32).reshape(GROUPS, GROUP_TOK, D))
    g_one, g_two, g_three, g_four, g_five, g_six, g_seven, g_eight, g_nine, g_ten, g_eleven, g_twelve = grad_params
    return (output.reshape(TOKENS, D).astype(jnp.bfloat16), grad_rows.reshape(TOKENS, D).astype(jnp.bfloat16), g_one, g_two, g_three, g_four, g_five, g_six, g_seven, g_eight, g_nine, g_ten, g_eleven, g_twelve)
```

```python
import functools
import itertools
import math

import jax
import jax.numpy as jnp
from jax import lax
from jax.experimental import pallas as pl
from jax.experimental.pallas import tpu as pltpu
from jax.sharding import Mesh
from jax.sharding import PartitionSpec as P

HS = 256
ROT = 64
BLOCK = 256
SIZES = {"xh": 2, "y": 4, "c": 2, "z": 4, "xl": 2}
NAMES = tuple(SIZES)
ROW = ("xh", "y", "c")
COL = ("z", "xl")
F32 = jnp.float32
BF16 = jnp.bfloat16


def hop(value, **deltas):
    axes = tuple(name for name in NAMES if name in deltas)

    def flat(coords):
        index = 0
        for name, place in zip(axes, coords):
            index = index * SIZES[name] + place % SIZES[name]
        return index

    pairs = []
    for coords in itertools.product(*[range(SIZES[name]) for name in axes]):
        moved = [place + deltas[name] for name, place in zip(axes, coords)]
        pairs.append((flat(coords), flat(moved)))
    return lax.ppermute(value, axes if len(axes) > 1 else axes[0], pairs)


def put(buffer, piece, start):
    return lax.dynamic_update_slice_in_dim(buffer, piece, start, 0)


def rows_at(value, start, count):
    return lax.dynamic_slice_in_dim(value, start, count, 0)


def gather_col(piece):
    z, xl = lax.axis_index("z"), lax.axis_index("xl")
    count, width = piece.shape
    other = hop(piece, xl=1)
    pair = jnp.zeros((2 * count, width), piece.dtype)
    pair = put(put(pair, piece, xl * count), other, (1 - xl) * count)
    back = hop(pair, z=1)
    ahead = hop(pair, z=3)
    far_low = hop(back[:count], z=1)
    far_high = hop(ahead[count:], z=3)
    whole = jnp.zeros((8 * count, width), piece.dtype)
    whole = put(whole, pair, z * 2 * count)
    whole = put(whole, back, (z + 3) % 4 * 2 * count)
    whole = put(whole, ahead, (z + 1) % 4 * 2 * count)
    whole = put(whole, far_low, (z + 2) % 4 * 2 * count)
    return put(whole, far_high, (z + 2) % 4 * 2 * count + count)


def scatter_col(whole):
    z, xl = lax.axis_index("z"), lax.axis_index("xl")
    count = whole.shape[0] // 8
    far = rows_at(whole, (z + 2) % 4 * 2 * count, 2 * count)
    up = rows_at(whole, (z + 1) % 4 * 2 * count, 2 * count)
    down = rows_at(whole, (z + 3) % 4 * 2 * count, 2 * count)
    own = rows_at(whole, z * 2 * count, 2 * count)
    low = hop(far[:count], z=1)
    high = hop(far[count:], z=3)
    up = jnp.concatenate([up[:count] + low, up[count:]], 0)
    down = jnp.concatenate([down[:count], down[count:] + high], 0)
    from_back = hop(up, z=1)
    from_ahead = hop(down, z=3)
    total = own.astype(F32) + from_back.astype(F32) + from_ahead.astype(F32)
    sent = rows_at(total, (1 - xl) * count, count).astype(BF16)
    return rows_at(total, xl * count, count) + hop(sent, xl=1).astype(F32)


def gather_row(piece):
    y = lax.axis_index("y")
    count, width = piece.shape
    pair = jnp.concatenate([piece, hop(piece, xh=1)], 0)
    half = jnp.zeros((8 * count, width), piece.dtype)
    half = put(half, pair, y * 2 * count)
    for step in (1, 3, 2):
        half = put(half, hop(pair, y=step), (y - step + 4) % 4 * 2 * count)
    return jnp.concatenate([half, hop(half, c=1)], 0)


def scatter_row(whole):
    y = lax.axis_index("y")
    count = whole.shape[0] // 16
    half = whole[: 8 * count].astype(F32) + hop(whole[8 * count :], c=1).astype(F32)
    half = half.astype(BF16)
    pair = rows_at(half, y * 2 * count, 2 * count).astype(F32)
    for step in (1, 3, 2):
        pair = pair + hop(
            rows_at(half, (y + step) % 4 * 2 * count, 2 * count), y=step
        ).astype(F32)
    return pair[:count] + hop(pair[count:].astype(BF16), xh=1).astype(F32)


def sum_row(value):
    value = value + hop(value, c=1)
    value = value + hop(value, xh=1)
    return value + hop(value, y=1) + hop(value, y=2) + hop(value, y=3)


def sum_col(value):
    value = value + hop(value, xl=1)
    return value + hop(value, z=1) + hop(value, z=2) + hop(value, z=3)


def flips(view):
    core, xh = lax.axis_index("c"), lax.axis_index("xh")
    view = jnp.where(core == 1, view[:, ::-1], view)
    return jnp.where(xh == 1, view[:, :, :, ::-1], view)


def to_own_order(value):
    rows, width = value.shape
    view = value.reshape(rows, 2, 4, 2, width // 16).transpose(0, 3, 2, 1, 4)
    return flips(view).reshape(rows, width)


def from_own_order(value):
    rows, width = value.shape
    view = flips(value.reshape(rows, 2, 4, 2, width // 16))
    return view.transpose(0, 3, 2, 1, 4).reshape(rows, width)


def nt(left, right):
    return lax.dot_general(left, right, (((1,), (1,)), ((), ())), preferred_element_type=F32)


def tn(left, right):
    return lax.dot_general(left, right, (((0,), (0,)), ((), ())), preferred_element_type=F32)


def nn(left, right):
    return jnp.dot(left, right, preferred_element_type=F32)


def turn(part, cosine, sine):
    lane = lax.broadcasted_iota(jnp.int32, part.shape, 1)
    ahead = pltpu.roll(part, 128 - ROT // 2, 1)
    behind = pltpu.roll(part, ROT // 2, 1)
    return part * cosine + jnp.where(lane < ROT // 2, ahead, behind) * sine


def block_allowed(doc_col, doc_row, start, width):
    docs = doc_col[start : start + BLOCK] == doc_row[:, :width]
    row = start + lax.broadcasted_iota(jnp.int32, (BLOCK, width), 0)
    column = lax.broadcasted_iota(jnp.int32, (BLOCK, width), 1)
    return docs & (column <= row)


def attend_kernel(mix_ref, bias_ref, cos_ref, sin_ref, doc_col_ref, doc_row_ref, qkv_ref, out_ref, log_ref):
    rows = mix_ref.shape[0]
    for start in range(0, rows, BLOCK):
        at = pl.ds(start, BLOCK)
        cosine, sine = cos_ref[at, :], sin_ref[at, :]
        for first in (0, HS):
            head = mix_ref[at, first : first + 128] + bias_ref[:, first : first + 128]
            qkv_ref[at, first : first + 128] = turn(head, cosine, sine).astype(BF16)
            rest = mix_ref[at, first + 128 : first + HS] + bias_ref[:, first + 128 : first + HS]
            qkv_ref[at, first + 128 : first + HS] = rest.astype(BF16)
        qkv_ref[at, 2 * HS :] = (mix_ref[at, 2 * HS :] + bias_ref[:, 2 * HS :]).astype(BF16)
    doc_row = doc_row_ref[...]
    doc_col = doc_col_ref[...]
    for start in range(0, rows, BLOCK):
        width = start + BLOCK
        at = pl.ds(start, BLOCK)
        scores = nt(qkv_ref[at, :HS], qkv_ref[:width, HS : 2 * HS]) * HS ** (-0.5)
        scores = jnp.where(block_allowed(doc_col, doc_row, start, width), scores, -1e30)
        top = jnp.max(scores, axis=1, keepdims=True)
        raised = jnp.exp(scores - top)
        total = jnp.sum(raised, axis=1, keepdims=True)
        probabilities = (raised * (1.0 / total)).astype(BF16)
        out_ref[at, :] = nn(probabilities, qkv_ref[:width, 2 * HS :]).astype(BF16)
        log_ref[at, :] = top + jnp.log(total)


def attend_back_kernel(qkv_ref, grad_ref, log_ref, cos_ref, sin_ref, doc_col_ref, doc_row_ref, out_ref, sum_ref, dk_ref, dv_ref):
    rows = qkv_ref.shape[0]
    scaling = HS ** (-0.5)
    doc_row = doc_row_ref[...]
    doc_col = doc_col_ref[...]
    sums = [jnp.zeros((1, HS), F32) for _ in range(3)]

    def finish(value, start, first):
        at = pl.ds(start, BLOCK)
        head = turn(value[:, :128], cos_ref[at, :], -sin_ref[at, :]).astype(BF16)
        rest = value[:, 128:].astype(BF16)
        out_ref[at, first : first + 128] = head
        out_ref[at, first + 128 : first + HS] = rest
        both = jnp.concatenate([head.astype(F32), rest.astype(F32)], 1)
        return jnp.sum(both, axis=0, keepdims=True)

    for start in range(0, rows, BLOCK):
        width = start + BLOCK
        at = pl.ds(start, BLOCK)
        query = qkv_ref[at, :HS]
        grad = grad_ref[at, :]
        scores = nt(query, qkv_ref[:width, HS : 2 * HS]) * scaling
        allowed = block_allowed(doc_col, doc_row, start, width)
        weights = jnp.where(allowed, jnp.exp(scores - log_ref[at, :]), 0.0)
        probabilities = weights.astype(BF16)
        d_probs = nt(grad, qkv_ref[:width, 2 * HS :])
        inner = jnp.sum(weights * d_probs, axis=1, keepdims=True)
        d_scores = (weights * (d_probs - inner)).astype(BF16)
        d_values = tn(probabilities, grad)
        d_keys = tn(d_scores, query) * scaling
        if start:
            dv_ref[:start, :] += d_values[:start]
            dk_ref[:start, :] += d_keys[:start]
        dv_ref[start:width, :] = d_values[start:]
        dk_ref[start:width, :] = d_keys[start:]
        d_query = nn(d_scores, qkv_ref[:width, HS : 2 * HS]) * scaling
        sums[0] = sums[0] + finish(d_query, start, 0)
    for start in range(0, rows, BLOCK):
        at = pl.ds(start, BLOCK)
        sums[1] = sums[1] + finish(dk_ref[at, :], start, HS)
        values = dv_ref[at, :].astype(BF16)
        out_ref[at, 2 * HS :] = values
        sums[2] = sums[2] + jnp.sum(values.astype(F32), axis=0, keepdims=True)
    for part in range(3):
        sum_ref[:, part * HS : (part + 1) * HS] = sums[part]


def vmem_call(kernel, outs, args, scratch=(), flops=0, transcendentals=0):
    spec = pl.BlockSpec(memory_space=pltpu.VMEM)
    moved = sum(math.prod(a.shape) * a.dtype.itemsize for a in (*outs, *args))
    return pl.pallas_call(
        kernel,
        out_shape=outs,
        in_specs=[spec] * len(args),
        out_specs=[spec] * len(outs),
        scratch_shapes=scratch,
        compiler_params=pltpu.CompilerParams(vmem_limit_bytes=40 * 1024 * 1024),
        cost_estimate=pl.CostEstimate(
            flops=flops, bytes_accessed=moved, transcendentals=transcendentals
        ),
    )(*args)


def shape(rows, columns, dtype):
    return jax.ShapeDtypeStruct((rows, columns), dtype)


def attend(mix, bias, cosine, sine, doc_col, doc_row):
    rows = mix.shape[0]
    outs = (shape(rows, 3 * HS, BF16), shape(rows, HS, BF16), shape(rows, 1, F32))
    return vmem_call(
        attend_kernel,
        outs,
        (mix, bias, cosine, sine, doc_col, doc_row),
        flops=4 * rows * rows * HS,
        transcendentals=rows * rows,
    )


def attend_back(qkv, grad, logs, cosine, sine, doc_col, doc_row):
    rows = qkv.shape[0]
    outs = (shape(rows, 3 * HS, BF16), shape(1, 3 * HS, F32))
    return vmem_call(
        attend_back_kernel,
        outs,
        (qkv, grad, logs, cosine, sine, doc_col, doc_row),
        scratch=[pltpu.VMEM((rows, HS), F32), pltpu.VMEM((rows, HS), F32)],
        flops=10 * rows * rows * HS,
        transcendentals=rows * rows,
    )


def doc_layout(lengths, row_count):
    ends = jnp.cumsum(lengths, dtype=jnp.int32)
    places = jnp.arange(row_count, dtype=jnp.int32)
    passed = places[:, None] >= ends[None, :]
    doc_ids = jnp.sum(passed.astype(jnp.int32), axis=1, dtype=jnp.int32)
    begins = jnp.sum(jnp.where(passed, lengths[None, :], 0), axis=1, dtype=jnp.int32)
    return (doc_ids, places - begins)


def rotary_tables(positions):
    half = ROT // 2
    lane = jnp.arange(128, dtype=jnp.int32)
    frequency = 1.0 / 10000.0 ** ((lane % half).astype(F32) * (2.0 / ROT))
    frequency = jnp.where(lane < ROT, frequency, 0.0)
    angles = positions.astype(F32)[:, None] * frequency[None, :]
    sign = jnp.where(lane < half, -1.0, 1.0)
    return (jnp.cos(angles), jnp.sin(angles) * sign[None, :])


def gelu_pair(hidden):
    normal = 0.5 * (1.0 + lax.erf(hidden * (1.0 / math.sqrt(2.0))))
    density = jnp.exp(-0.5 * hidden * hidden) * (1.0 / math.sqrt(2.0 * math.pi))
    return (hidden * normal, normal + hidden * density)


def shards(
    tokens,
    doc_lengths,
    input_gain,
    input_shift,
    post_gain,
    post_shift,
    qkv_weight,
    qkv_bias,
    dense_weight,
    dense_bias,
    up_weight,
    up_bias,
    down_weight,
    down_bias,
    cotangent,
):
    row_index = (lax.axis_index("xh") * 4 + lax.axis_index("y")) * 2 + lax.axis_index("c")
    slice_rows = qkv_weight.shape[0]
    qkv_cols, up_cols = qkv_weight.shape[1], up_weight.shape[1]

    tok_rows = tokens.astype(F32)
    center = jnp.mean(tok_rows, axis=-1, keepdims=True)
    centered = tok_rows - center
    variance = jnp.mean(centered * centered, axis=-1, keepdims=True)
    inverse = lax.rsqrt(variance + 1e-05)
    normal_rows = to_own_order(centered * inverse)
    normal_all = gather_col(normal_rows.astype(BF16))

    def own_slice(vector):
        return rows_at(vector.astype(F32), row_index * slice_rows, slice_rows)[:, None]

    block_a = jnp.concatenate(
        [(qkv_weight.astype(F32) * own_slice(input_gain)).astype(BF16), dense_weight.T], 1
    )
    block_b = jnp.concatenate(
        [(up_weight.astype(F32) * own_slice(post_gain)).astype(BF16), down_weight.T], 1
    )
    full_a = gather_row(block_a)
    cot_rows = to_own_order(cotangent)
    cot_all = gather_col(cot_rows)
    full_b = gather_row(block_b)

    bias_part = jnp.pad(
        jnp.concatenate([qkv_bias, up_bias]).astype(F32)[None], ((0, 0), (0, 16))
    )
    bias_all = sum_row(
        jnp.where(jnp.arange(16)[:, None] == row_index, bias_part, 0.0)
    )
    qkv_bias_all = bias_all[:, : qkv_bias.shape[0]].reshape(1, qkv_cols)
    up_bias_all = bias_all[:, qkv_bias.shape[0] : qkv_bias.shape[0] + up_bias.shape[0]].reshape(
        1, up_cols
    )

    vectors = to_own_order(
        jnp.stack([input_gain, input_shift, post_gain, post_shift]).astype(F32)
    )
    gain_one, shift_one, gain_two, shift_two = (vectors[i : i + 1] for i in range(4))
    qkv_full, dense_full = full_a[:, :qkv_cols], full_a[:, qkv_cols:]
    up_full, down_full = full_b[:, :up_cols], full_b[:, up_cols:]
    ratio_one = jnp.broadcast_to((shift_one / gain_one).astype(BF16), (8, vectors.shape[1]))
    ratio_two = jnp.broadcast_to((shift_two / gain_two).astype(BF16), (8, vectors.shape[1]))
    qkv_bias_all = qkv_bias_all + nn(ratio_one, qkv_full)[:1]
    up_bias_all = up_bias_all + nn(ratio_two, up_full)[:1]

    row_count = normal_all.shape[0]
    doc_ids, positions = doc_layout(doc_lengths[0], row_count)
    cosine, sine = rotary_tables(positions)
    doc_col, doc_row = doc_ids[:, None], doc_ids[None, :]
    mixture = nn(normal_all, qkv_full)
    qkv, attended, logs = attend(mixture, qkv_bias_all, cosine, sine, doc_col, doc_row)
    hidden = nn(normal_all, up_full) + up_bias_all
    active, slope = gelu_pair(hidden)
    active = active.astype(BF16)
    slope = slope.astype(BF16)
    out_part = (nt(attended, dense_full) + nt(active, down_full)).astype(BF16)
    out_sum = scatter_col(out_part)

    d_attended = nn(cot_all, dense_full).astype(BF16)
    d_mixture, qkv_bias_part = attend_back(
        qkv, d_attended, logs, cosine, sine, doc_col, doc_row
    )
    d_hidden = (nn(cot_all, down_full) * slope.astype(F32)).astype(BF16)
    up_bias_part = jnp.sum(d_hidden.astype(F32), axis=0, keepdims=True)
    dense_part = tn(cot_all, attended).astype(BF16)
    down_part = tn(cot_all, active).astype(BF16)
    qkv_raw = tn(normal_all, d_mixture)
    up_raw = tn(normal_all, d_hidden)
    qkv_part = (qkv_raw * gain_one.T + shift_one.T * qkv_bias_part).astype(BF16)
    up_part = (up_raw * gain_two.T + shift_two.T * up_bias_part).astype(BF16)
    grad_a = scatter_row(jnp.concatenate([qkv_part, dense_part], 1))
    grad_b = scatter_row(jnp.concatenate([up_part, down_part], 1))
    u_part = (nt(d_mixture, qkv_full) + nt(d_hidden, up_full)).astype(BF16)
    u_rows = scatter_col(u_part)

    def against(weights, raw, bias_part, gain):
        wide = weights.astype(F32)
        return (
            (jnp.sum(wide * raw, axis=1) / gain[0])[None],
            (jnp.sum(wide * bias_part, axis=1) / gain[0])[None],
        )

    gain_one_part, shift_one_part = against(qkv_full, qkv_raw, qkv_bias_part, gain_one)
    gain_two_part, shift_two_part = against(up_full, up_raw, up_bias_part, gain_two)
    width = vectors.shape[1]
    small = jnp.concatenate(
        [
            gain_one_part,
            shift_one_part,
            gain_two_part,
            shift_two_part,
            jnp.sum(cot_rows.astype(F32), axis=0, keepdims=True),
        ],
        0,
    )
    biases = jnp.concatenate([qkv_bias_part, up_bias_part], 1)
    biases = jnp.pad(biases, ((0, 0), (0, width - biases.shape[1])))
    packed = jnp.concatenate([from_own_order(small), biases, jnp.zeros((2, width), F32)], 0)
    packed = sum_row(packed)
    qkv_bias_total = lax.dynamic_slice_in_dim(
        packed[5], row_index * qkv_bias.shape[0], qkv_bias.shape[0], 0
    )
    up_bias_total = lax.dynamic_slice_in_dim(
        packed[5], qkv_cols + row_index * up_bias.shape[0], up_bias.shape[0], 0
    )
    packed = sum_col(packed)

    layer_out = (
        tok_rows
        + from_own_order(out_sum)
        + dense_bias.astype(F32)
        + down_bias.astype(F32)
    ).astype(BF16)
    u_mean = jnp.mean(u_rows, axis=-1, keepdims=True)
    un_mean = jnp.mean(u_rows * normal_rows, axis=-1, keepdims=True)
    d_tokens = (u_rows - u_mean - normal_rows * un_mean) * inverse
    input_grad = (cotangent.astype(F32) + from_own_order(d_tokens)).astype(BF16)
    return (
        layer_out,
        input_grad,
        packed[0],
        packed[1],
        packed[2],
        packed[3],
        grad_a[:, :qkv_cols],
        qkv_bias_total,
        grad_a[:, qkv_cols:].T,
        packed[4],
        grad_b[:, :up_cols],
        up_bias_total,
        grad_b[:, up_cols:].T,
        packed[4],
    )


def solution(mesh):
    fine = Mesh(mesh.devices.reshape(tuple(SIZES.values())), NAMES)
    everywhere = P(ROW + COL, None)
    return jax.shard_map(
        shards,
        mesh=fine,
        in_specs=(
            everywhere,
            P(ROW, None),
            P(),
            P(),
            P(),
            P(),
            P(ROW, COL),
            P(COL + ROW),
            P(COL, ROW),
            P(),
            P(ROW, COL),
            P(COL + ROW),
            P(COL, ROW),
            P(),
            everywhere,
        ),
        out_specs=(
            everywhere,
            everywhere,
            P(),
            P(),
            P(),
            P(),
            P(ROW, COL),
            P(COL + ROW),
            P(COL, ROW),
            P(),
            P(ROW, COL),
            P(COL + ROW),
            P(COL, ROW),
            P(),
        ),
        check_vma=False,
    )
```

```python
import functools
import itertools
import math

import jax
import jax.numpy as jnp
from jax import lax
from jax.experimental import pallas as pl
from jax.experimental.pallas import tpu as pltpu
from jax.sharding import Mesh
from jax.sharding import PartitionSpec as P

HS = 256
ROT = 64
BLOCK = 256
OFFLOAD = False
SIZES = {"xh": 2, "y": 4, "c": 2, "z": 4, "xl": 2}
NAMES = tuple(SIZES)
ROW = ("xh", "y", "c")
COL = ("z", "xl")
F32 = jnp.float32
BF16 = jnp.bfloat16


def hop(value, **deltas):
    axes = tuple(name for name in NAMES if name in deltas)

    def flat(coords):
        index = 0
        for name, place in zip(axes, coords):
            index = index * SIZES[name] + place % SIZES[name]
        return index

    pairs = []
    for coords in itertools.product(*[range(SIZES[name]) for name in axes]):
        moved = [place + deltas[name] for name, place in zip(axes, coords)]
        pairs.append((flat(coords), flat(moved)))
    return lax.ppermute(value, axes if len(axes) > 1 else axes[0], pairs)


def put(buffer, piece, start):
    return lax.dynamic_update_slice_in_dim(buffer, piece, start, 0)


def rows_at(value, start, count):
    return lax.dynamic_slice_in_dim(value, start, count, 0)


def after(value, *others):
    return lax.optimization_barrier((value, *others))[0]


def all_after(values, others):
    return list(lax.optimization_barrier((*values, *others))[: len(values)])


def assemble(shapes, dtype, moves, scalars):
    names = list(scalars)
    pieces = []
    for piece, *_ in moves:
        if not any(piece is known for known in pieces):
            pieces.append(piece)

    def kernel(scalars_ref, *refs):
        sources, outs = refs[: len(pieces)], refs[len(pieces) :]
        for piece, cut, output, index in moves:
            source = next(r for known, r in zip(pieces, sources) if known is piece)
            place = tuple(scalars_ref[names.index(i)] if isinstance(i, str) else i for i in index)
            outs[output][place] = source[cut]

    args = (jnp.stack(list(scalars.values())).astype(jnp.int32), *pieces)
    outs = tuple(jax.ShapeDtypeStruct(one, dtype) for one in shapes)
    return vmem_call(kernel, outs, args, scalars=1)


def ring_near(pair, axis):
    return [hop(pair, **{axis: 1}), hop(pair, **{axis: 3})]


def ring_far(near, axis):
    back, ahead = near
    return [hop(back[:1], **{axis: 1}), hop(ahead[1:], **{axis: 3})]


RING_PLACES = (
    ("at", (("own", 0), ("other", 1))),
    ("back", (("own", 0), ("other", 1))),
    ("ahead", (("own", 0), ("other", 1))),
    ("far", (("own", 0),)),
    ("far", (("other", 0),)),
)


def places(axis, pair):
    at, own = lax.axis_index(axis), lax.axis_index(pair)
    return {
        "at": at,
        "back": (at + 3) % 4,
        "ahead": (at + 1) % 4,
        "far": (at + 2) % 4,
        "own": own,
        "other": 1 - own,
    }


def rows_of_group(parts):
    count, width = parts[0].shape[1:]
    moves = []
    for part, (place, blocks) in zip(parts, RING_PLACES):
        for pair, number in blocks:
            moves.append((part, (number,), 0, (place, pair)))
    (whole,) = assemble([(4, 2, count, width)], BF16, moves, places("z", "xl"))
    return whole.reshape(8 * count, width)


def rows_of_weight(parts, widths, count):
    height, width = parts[0].shape[1:]
    shapes = [(2, 4, 2, count, part) for part in widths]
    if height > count:
        shapes.append((16, height - count, width))
    scalars = places("y", "xh") | {"core": lax.axis_index("c"), "sibling": 1 - lax.axis_index("c")}
    moves = []
    extras = 0
    for part, (place, blocks) in zip(parts, RING_PLACES):
        for core, value in (("core", part), ("sibling", hop(part, c=1))):
            for pair, number in blocks:
                first = 0
                for output, cols in enumerate(widths):
                    cut = (number, slice(0, count), slice(first, first + cols))
                    moves.append((value, cut, output, (pair, place, core)))
                    first += cols
                if height > count:
                    moves.append((value, (number, slice(count, height)), len(widths), (extras,)))
                    extras += 1
    outs = assemble(shapes, BF16, moves, scalars)
    wholes = [out.reshape(16 * count, cols) for out, cols in zip(outs, widths)]
    return (*wholes, *outs[len(widths) :])


def scatter_col_first(parts):
    return [hop(parts[0], z=1), hop(parts[1], z=3)]


def scatter_col_second(parts, first):
    low, high = first
    up, down = parts[2], parts[3]
    count = low.shape[0]
    up = jnp.concatenate([up[:count] + low, up[count:]], 0)
    down = jnp.concatenate([down[:count], down[count:] + high], 0)
    return [hop(up, z=1), hop(down, z=3)]


def scatter_col_third(parts, second):
    xl = lax.axis_index("xl")
    own = parts[4]
    count = own.shape[0] // 2

    def total(place):
        return sum(rows_at(part, place * count, count).astype(F32) for part in (own, *second))

    return total(xl), hop(total(1 - xl).astype(BF16), xl=1)


def scatter_row_first(sent):
    return hop(sent, c=1)


def scatter_row_second(kept, first, offload):
    y = lax.axis_index("y")
    if offload:
        half = (kept.astype(F32) + first.astype(F32)).astype(BF16)
        return [lax.psum_scatter(half, "y", scatter_dimension=0)]

    def cut(step):
        two = [
            lax.dynamic_index_in_dim(part, (y + step) % 4, 0, keepdims=False).astype(F32)
            for part in (kept, first)
        ]
        return (two[0] + two[1]).astype(BF16)

    return [cut(0)] + [hop(cut(step), y=step) for step in (1, 3, 2)]


def scatter_row_third(second):
    xh = lax.axis_index("xh")
    pair = sum(part.astype(F32) for part in second)
    kept = lax.dynamic_index_in_dim(pair, xh, 0, keepdims=False)
    sent = lax.dynamic_index_in_dim(pair, 1 - xh, 0, keepdims=False).astype(BF16)
    return kept, hop(sent, xh=1)


def sum_row(value):
    value = value + hop(value, c=1)
    value = value + hop(value, xh=1)
    return value + hop(value, y=1) + hop(value, y=2) + hop(value, y=3)


def sum_col(value):
    value = value + hop(value, xl=1)
    return value + hop(value, z=1) + hop(value, z=2) + hop(value, z=3)


def nt(left, right):
    return lax.dot_general(left, right, (((1,), (1,)), ((), ())), preferred_element_type=F32)


def tn(left, right):
    return lax.dot_general(left, right, (((0,), (0,)), ((), ())), preferred_element_type=F32)


def nn(left, right):
    return jnp.dot(left, right, preferred_element_type=F32)


def turn(part, cosine, sine):
    lane = lax.broadcasted_iota(jnp.int32, part.shape, 1)
    ahead = pltpu.roll(part, 128 - ROT // 2, 1)
    behind = pltpu.roll(part, ROT // 2, 1)
    return part * cosine + jnp.where(lane < ROT // 2, ahead, behind) * sine


def block_allowed(doc_col, doc_row, start, width):
    docs = doc_col[start : start + BLOCK] == doc_row[:, :width]
    row = start + lax.broadcasted_iota(jnp.int32, (BLOCK, width), 0)
    column = lax.broadcasted_iota(jnp.int32, (BLOCK, width), 1)
    return docs & (column <= row)


def attend_kernel(mix_ref, bias_ref, cos_ref, sin_ref, doc_col_ref, doc_row_ref, qkv_ref, out_ref, log_ref):
    rows = mix_ref.shape[0]
    for start in range(0, rows, BLOCK):
        at = pl.ds(start, BLOCK)
        cosine, sine = cos_ref[at, :], sin_ref[at, :]
        for first in (0, HS):
            head = mix_ref[at, first : first + 128] + bias_ref[:, first : first + 128]
            qkv_ref[at, first : first + 128] = turn(head, cosine, sine).astype(BF16)
            rest = mix_ref[at, first + 128 : first + HS] + bias_ref[:, first + 128 : first + HS]
            qkv_ref[at, first + 128 : first + HS] = rest.astype(BF16)
        qkv_ref[at, 2 * HS :] = (mix_ref[at, 2 * HS :] + bias_ref[:, 2 * HS :]).astype(BF16)
    doc_row = doc_row_ref[...]
    doc_col = doc_col_ref[...]
    for start in range(0, rows, BLOCK):
        width = start + BLOCK
        at = pl.ds(start, BLOCK)
        scores = nt(qkv_ref[at, :HS], qkv_ref[:width, HS : 2 * HS]) * HS ** (-0.5)
        scores = jnp.where(block_allowed(doc_col, doc_row, start, width), scores, -1e30)
        top = jnp.max(scores, axis=1, keepdims=True)
        raised = jnp.exp(scores - top)
        total = jnp.sum(raised, axis=1, keepdims=True)
        probabilities = (raised * (1.0 / total)).astype(BF16)
        out_ref[at, :] = nn(probabilities, qkv_ref[:width, 2 * HS :]).astype(BF16)
        log_ref[at, :] = top + jnp.log(total)


def attend_back_kernel(qkv_ref, grad_ref, log_ref, cos_ref, sin_ref, doc_col_ref, doc_row_ref, out_ref, sum_ref, dk_ref, dv_ref):
    rows = qkv_ref.shape[0]
    scaling = HS ** (-0.5)
    doc_row = doc_row_ref[...]
    doc_col = doc_col_ref[...]
    sums = [jnp.zeros((1, HS), F32) for _ in range(3)]

    def finish(value, start, first):
        at = pl.ds(start, BLOCK)
        head = turn(value[:, :128], cos_ref[at, :], -sin_ref[at, :]).astype(BF16)
        rest = value[:, 128:].astype(BF16)
        out_ref[at, first : first + 128] = head
        out_ref[at, first + 128 : first + HS] = rest
        both = jnp.concatenate([head.astype(F32), rest.astype(F32)], 1)
        return jnp.sum(both, axis=0, keepdims=True)

    for start in range(0, rows, BLOCK):
        width = start + BLOCK
        at = pl.ds(start, BLOCK)
        query = qkv_ref[at, :HS]
        grad = grad_ref[at, :]
        scores = nt(query, qkv_ref[:width, HS : 2 * HS]) * scaling
        allowed = block_allowed(doc_col, doc_row, start, width)
        weights = jnp.where(allowed, jnp.exp(scores - log_ref[at, :]), 0.0)
        probabilities = weights.astype(BF16)
        d_probs = nt(grad, qkv_ref[:width, 2 * HS :])
        inner = jnp.sum(weights * d_probs, axis=1, keepdims=True)
        d_scores = (weights * (d_probs - inner)).astype(BF16)
        d_values = tn(probabilities, grad)
        d_keys = tn(d_scores, query) * scaling
        if start:
            dv_ref[:start, :] += d_values[:start]
            dk_ref[:start, :] += d_keys[:start]
        dv_ref[start:width, :] = d_values[start:]
        dk_ref[start:width, :] = d_keys[start:]
        d_query = nn(d_scores, qkv_ref[:width, HS : 2 * HS]) * scaling
        sums[0] = sums[0] + finish(d_query, start, 0)
    for start in range(0, rows, BLOCK):
        at = pl.ds(start, BLOCK)
        sums[1] = sums[1] + finish(dk_ref[at, :], start, HS)
        values = dv_ref[at, :].astype(BF16)
        out_ref[at, 2 * HS :] = values
        sums[2] = sums[2] + jnp.sum(values.astype(F32), axis=0, keepdims=True)
    for part in range(3):
        sum_ref[:, part * HS : (part + 1) * HS] = sums[part]


def project_kernel(z_ref, one_ref, two_ref, weight_one_ref, weight_two_ref, low_ref, high_ref, up_ref, down_ref, own_ref, held_ref):
    z = z_ref[0]
    rows, width = held_ref.shape
    part = rows // 4
    for first in range(0, weight_one_ref.shape[0], width):
        at = pl.ds(first, width)
        total = nt(one_ref[...], weight_one_ref[at, :]) + nt(two_ref[...], weight_two_ref[at, :])
        held_ref[...] = total.astype(BF16)

        def cut(step, start, count):
            place = pl.multiple_of((z + step) % 4 * part, part)
            return held_ref[pl.ds(place + start, count), :]

        low_ref[:, first : first + width] = cut(2, 0, part // 2)
        high_ref[:, first : first + width] = cut(2, part // 2, part // 2)
        up_ref[:, first : first + width] = cut(1, 0, part)
        down_ref[:, first : first + width] = cut(3, 0, part)
        own_ref[:, first : first + width] = cut(0, 0, part)


def project(one, two, weight_one, weight_two):
    rows, features = one.shape[0], weight_one.shape[0]
    z = lax.axis_index("z").astype(jnp.int32)[None]
    counts = (rows // 8, rows // 8, rows // 4, rows // 4, rows // 4)
    return vmem_call(
        project_kernel,
        tuple(shape(count, features, BF16) for count in counts),
        (z, one, two, weight_one, weight_two),
        scratch=[pltpu.VMEM((rows, 512), BF16)],
        flops=2 * rows * features * (one.shape[1] + two.shape[1]),
        scalars=1,
    )


def split_cores(core, values, first, sent_ref, kept_ref):
    count, width = sent_ref.shape[2], values.shape[1]
    for y in range(values.shape[0] // (2 * count)):
        zero = values[2 * y * count : (2 * y + 1) * count]
        one = values[(2 * y + 1) * count : (2 * y + 2) * count]
        sent_ref[y, 0, :, first : first + width] = jnp.where(core == 0, one, zero)
        kept_ref[y, 0, :, first : first + width] = jnp.where(core == 0, zero, one)


def back_grads_kernel(core_ref, left_ref, one_ref, two_ref, sent_ref, kept_ref):
    first = 0
    for right_ref in (one_ref, two_ref):
        values = tn(left_ref[...], right_ref[...]).astype(BF16)
        split_cores(core_ref[0], values, first, sent_ref, kept_ref)
        first += right_ref.shape[1]


def in_grads_kernel(core_ref, left_ref, one_ref, two_ref, norm_ref, weight_one_ref, weight_two_ref, bias_ref, sent_ref, kept_ref, sums_ref):
    columns = norm_ref[...].T
    lane = lax.broadcasted_iota(jnp.int32, (columns.shape[0], 128), 1)
    sums = jnp.zeros((columns.shape[0], 128), F32)
    first = 0
    for number, (right_ref, weight_ref) in enumerate(((one_ref, weight_one_ref), (two_ref, weight_two_ref))):
        width = right_ref.shape[1]
        gain, shift = columns[:, 2 * number : 2 * number + 1], columns[:, 2 * number + 1 : 2 * number + 2]
        bias = bias_ref[:, first : first + width]
        raw = tn(left_ref[...], right_ref[...])
        wide = weight_ref[...].astype(F32)
        gain_sum = jnp.sum(wide * raw, axis=1, keepdims=True) / gain
        shift_sum = jnp.sum(wide * bias, axis=1, keepdims=True) / gain
        sums = jnp.where(lane == 2 * number, gain_sum, sums)
        sums = jnp.where(lane == 2 * number + 1, shift_sum, sums)
        values = (raw * gain + shift * bias).astype(BF16)
        split_cores(core_ref[0], values, first, sent_ref, kept_ref)
        first += width
    sums_ref[...] = sums.T[:8]


def weight_grads(left, one, two, extra=None):
    rows, features = left.shape
    count = features // 16
    step = 4 * count
    width = one.shape[1] + two.shape[1]
    core = lax.axis_index("c").astype(jnp.int32)[None]
    whole = lambda a: pl.BlockSpec(a.shape, lambda i: (0,) * a.ndim)
    in_specs = [
        pl.BlockSpec(memory_space=pltpu.SMEM),
        pl.BlockSpec((rows, step), lambda i: (0, i)),
        whole(one),
        whole(two),
    ]
    blocks = jax.ShapeDtypeStruct((4, 2, count, width), BF16)
    block_spec = pl.BlockSpec((2, 1, count, width), lambda i: (i % 2, i // 2, 0, 0))
    outs, out_specs, args = [blocks] * 2, [block_spec] * 2, [core, left, one, two]
    kernel = back_grads_kernel
    if extra is not None:
        kernel = in_grads_kernel
        vectors, weight_one, weight_two, bias = extra
        args += [vectors, weight_one, weight_two, bias]
        in_specs.append(pl.BlockSpec((8, step), lambda i: (0, i)))
        in_specs += [pl.BlockSpec((step, w.shape[1]), lambda i: (i, 0)) for w in (weight_one, weight_two)]
        in_specs.append(whole(bias))
        outs.append(shape(8, features, F32))
        out_specs.append(pl.BlockSpec((8, step), lambda i: (0, i)))
    return pl.pallas_call(
        kernel,
        grid=(features // step,),
        out_shape=tuple(outs),
        in_specs=in_specs,
        out_specs=tuple(out_specs),
        compiler_params=pltpu.CompilerParams(vmem_limit_bytes=48 * 1024 * 1024),
        cost_estimate=pl.CostEstimate(
            flops=2 * rows * features * width,
            bytes_accessed=2 * (rows * (features + width) + features * width),
            transcendentals=0,
        ),
    )(*args)


def prepare_kernel(row_ref, tok_ref, norm_ref, qkv_ref, up_ref, dense_ref, down_ref, bias_ref, normal_ref, in_ref, back_ref):
    tok_rows = tok_ref[...].astype(F32)
    center = jnp.mean(tok_rows, axis=-1, keepdims=True)
    centered = tok_rows - center
    variance = jnp.mean(centered * centered, axis=-1, keepdims=True)
    normal_ref[...] = (centered * lax.rsqrt(variance + 1e-05)).astype(BF16)
    count = qkv_ref.shape[0]
    start = pl.multiple_of(row_ref[0] * count, count)
    square = (count, count)
    diagonal = lax.broadcasted_iota(jnp.int32, square, 0) == lax.broadcasted_iota(jnp.int32, square, 1)

    def column(which):
        lanes = jnp.broadcast_to(norm_ref[which : which + 1, pl.ds(start, count)], square)
        return jnp.sum(jnp.where(diagonal, lanes, 0.0), axis=1, keepdims=True)

    first = 0
    for gain, weight in ((0, qkv_ref), (2, up_ref)):
        width = weight.shape[1]
        wide = weight[...].astype(F32)
        in_ref[:count, first : first + width] = (wide * column(gain)).astype(BF16)
        shifted = jnp.sum(wide * column(gain + 1), axis=0, keepdims=True)
        shifted = shifted + bias_ref[:, first : first + width]
        high = shifted.astype(BF16)
        low = (shifted - high.astype(F32)).astype(BF16)
        line = lax.broadcasted_iota(jnp.int32, (16, width), 0)
        tail = jnp.where(line == 0, high.astype(F32), jnp.where(line == 1, low.astype(F32), 0.0))
        in_ref[count:, first : first + width] = tail.astype(BF16)
        first += width
    first = 0
    for weight in (dense_ref, down_ref):
        height = weight.shape[0]
        back_ref[:, first : first + height] = weight[...].astype(F32).T.astype(BF16)
        first += height


def vmem_call(kernel, outs, args, scratch=(), flops=0, transcendentals=0, scalars=0):
    spec = pl.BlockSpec()
    scalar = pl.BlockSpec(memory_space=pltpu.SMEM)
    moved = sum(math.prod(a.shape) * a.dtype.itemsize for a in (*outs, *args))
    return pl.pallas_call(
        kernel,
        out_shape=outs,
        in_specs=[scalar] * scalars + [spec] * (len(args) - scalars),
        out_specs=[spec] * len(outs),
        scratch_shapes=scratch,
        compiler_params=pltpu.CompilerParams(vmem_limit_bytes=40 * 1024 * 1024),
        cost_estimate=pl.CostEstimate(
            flops=flops, bytes_accessed=moved, transcendentals=transcendentals
        ),
    )(*args)


def shape(rows, columns, dtype):
    return jax.ShapeDtypeStruct((rows, columns), dtype)


def attend(mix, bias, cosine, sine, doc_col, doc_row):
    rows = mix.shape[0]
    outs = (shape(rows, 3 * HS, BF16), shape(rows, HS, BF16), shape(rows, 1, F32))
    return vmem_call(
        attend_kernel,
        outs,
        (mix, bias, cosine, sine, doc_col, doc_row),
        flops=4 * rows * rows * HS,
        transcendentals=rows * rows,
    )


def attend_back(qkv, grad, logs, cosine, sine, doc_col, doc_row):
    rows = qkv.shape[0]
    outs = (shape(rows, 3 * HS, BF16), shape(1, 3 * HS, F32))
    return vmem_call(
        attend_back_kernel,
        outs,
        (qkv, grad, logs, cosine, sine, doc_col, doc_row),
        scratch=[pltpu.VMEM((rows, HS), F32), pltpu.VMEM((rows, HS), F32)],
        flops=10 * rows * rows * HS,
        transcendentals=rows * rows,
    )


def doc_layout(lengths, places):
    first, second = lengths[0], lengths[0] + lengths[1]
    third = second + lengths[2]
    passed = [(places >= end).astype(jnp.int32) for end in (first, second, third)]
    doc_ids = passed[0] + passed[1] + passed[2]
    begins = passed[0] * lengths[0] + passed[1] * lengths[1] + passed[2] * lengths[2]
    return (doc_ids, places - begins)


def rotary_tables(positions):
    half = ROT // 2
    lane = jnp.arange(128, dtype=jnp.int32)
    frequency = 1.0 / 10000.0 ** ((lane % half).astype(F32) * (2.0 / ROT))
    frequency = jnp.where(lane < ROT, frequency, 0.0)
    angles = positions.astype(F32) * frequency[None, :]
    sign = jnp.where(lane < half, -1.0, 1.0)
    return (jnp.cos(angles), jnp.sin(angles) * sign[None, :])


def gelu_pair(hidden):
    normal = 0.5 * (1.0 + lax.erf(hidden * (1.0 / math.sqrt(2.0))))
    density = jnp.exp(-0.5 * hidden * hidden) * (1.0 / math.sqrt(2.0 * math.pi))
    return (hidden * normal, normal + hidden * density)


def shards(
    tokens,
    doc_lengths,
    input_gain,
    input_shift,
    post_gain,
    post_shift,
    qkv_weight,
    qkv_bias,
    dense_weight,
    dense_bias,
    up_weight,
    up_bias,
    down_weight,
    down_bias,
    cotangent,
):
    row_index = (lax.axis_index("xh") * 4 + lax.axis_index("y")) * 2 + lax.axis_index("c")
    slice_rows = qkv_weight.shape[0]
    qkv_cols, up_cols = qkv_weight.shape[1], up_weight.shape[1]

    vectors = jnp.stack([input_gain, input_shift, post_gain, post_shift]).astype(F32)
    gain_one, shift_one, gain_two, shift_two = (vectors[i : i + 1] for i in range(4))
    bias_row = jnp.concatenate(
        [
            lax.dynamic_update_slice(
                jnp.zeros((1, whole), F32), bias.astype(F32)[None], (0, row_index * bias.shape[0])
            )
            for whole, bias in ((qkv_cols, qkv_bias), (up_cols, up_bias))
        ],
        1,
    )
    tok_count, width = tokens.shape
    back_cols = (dense_weight.shape[0], down_weight.shape[0])
    own_normal, block_in, block_back = vmem_call(
        prepare_kernel,
        (
            shape(tok_count, width, BF16),
            shape(slice_rows + 16, qkv_cols + up_cols, BF16),
            shape(slice_rows, sum(back_cols), BF16),
        ),
        (
            row_index.astype(jnp.int32)[None],
            tokens,
            vectors,
            qkv_weight,
            up_weight,
            dense_weight,
            down_weight,
            bias_row,
        ),
        scalars=1,
    )
    def with_other(piece, other):
        return jnp.stack([piece, other])

    cot_near = ring_near(cotangent, "z")
    in_other = hop(block_in, xh=1)
    normal_other = hop(own_normal, xl=1)
    normal_pair, in_pair, cot_own = all_after(
        [with_other(own_normal, normal_other), with_other(block_in, in_other), cotangent], cot_near
    )
    normal_near = ring_near(normal_pair, "z")
    in_near = ring_near(in_pair, "y")
    cot_other = hop(cot_own, xl=1)
    held = all_after([*normal_near, *in_near, block_back, cot_other], [])
    normal_far = ring_far(held[:2], "z")
    in_far = ring_far(held[2:4], "y")
    back_other = hop(held[4], xh=1)
    cot_other, back_pair = all_after(
        [held[5], with_other(block_back, back_other)], [*normal_far, *in_far]
    )
    back_near = ring_near(back_pair, "y")
    cot_other_near = ring_near(cot_other, "z")
    qkv_full, up_full, extra = rows_of_weight(
        [in_pair, *in_near, *in_far], (qkv_cols, up_cols), slice_rows
    )
    normal_all = rows_of_group([normal_pair, *normal_near, *normal_far])
    held = all_after([*back_near, cot_near[0]], cot_other_near)
    back_far = ring_far(held[:2], "y")
    cot_far = hop(held[2], z=1)
    cot_far_other = hop(cot_far, xl=1)
    dense_full, down_full = rows_of_weight([back_pair, *back_near, *back_far], back_cols, slice_rows)
    cot_parts = [
        cotangent,
        cot_other,
        cot_near[0],
        cot_other_near[0],
        cot_near[1],
        cot_other_near[1],
        cot_far,
        cot_far_other,
    ]
    cot_places = [(at, pair) for at in ("at", "back", "ahead", "far") for pair in ("own", "other")]
    (cot_all,) = assemble(
        [(4, 2, tok_count, width)],
        BF16,
        [(part, (slice(None),), 0, place) for part, place in zip(cot_parts, cot_places)],
        places("z", "xl"),
    )
    cot_all = cot_all.reshape(8 * tok_count, width)
    bias_all = jnp.sum(extra.astype(F32), axis=(0, 1))[None]
    qkv_bias_all, up_bias_all = bias_all[:, :qkv_cols], bias_all[:, qkv_cols:]

    row_count = normal_all.shape[0]
    doc_col, positions = doc_layout(doc_lengths[0], jnp.arange(row_count, dtype=jnp.int32)[:, None])
    doc_row, _ = doc_layout(doc_lengths[0], jnp.arange(row_count, dtype=jnp.int32)[None, :])
    cosine, sine = rotary_tables(positions)
    mixture = nn(normal_all, qkv_full)
    qkv, attended, logs = attend(mixture, qkv_bias_all, cosine, sine, doc_col, doc_row)
    hidden = nn(normal_all, up_full) + up_bias_all
    active, slope = gelu_pair(hidden)
    active = active.astype(BF16)
    slope = slope.astype(BF16)
    out_parts = project(attended, active, dense_full, down_full)
    out_first = scatter_col_first(out_parts)

    back_sent, back_kept = weight_grads(cot_all, attended, active)
    back_first = scatter_row_first(back_sent)
    cot_all = after(cot_all, back_sent)
    d_attended = nn(cot_all, dense_full).astype(BF16)
    d_active = nn(cot_all, down_full)
    d_hidden = (d_active * slope.astype(F32)).astype(BF16)
    d_attended, d_hidden = all_after([d_attended, d_hidden], [back_first, *out_first])
    out_second = scatter_col_second(out_parts, out_first)
    back_second = scatter_row_second(back_kept, back_first, OFFLOAD)
    d_mixture, qkv_bias_part = attend_back(
        qkv, d_attended, logs, cosine, sine, doc_col, doc_row
    )
    up_bias_part = jnp.sum(d_hidden.astype(F32), axis=0, keepdims=True)
    u_parts = project(d_mixture, d_hidden, qkv_full, up_full)
    u_parts = all_after(u_parts, out_second)
    u_first = scatter_col_first(u_parts)
    d_mixture, d_hidden = all_after([d_mixture, d_hidden], [u_parts[0]])
    biases = jnp.concatenate([qkv_bias_part, up_bias_part], 1)
    in_sent, in_kept, sums = weight_grads(
        normal_all,
        d_mixture,
        d_hidden,
        (jnp.pad(vectors, ((0, 4), (0, 0))), qkv_full, up_full, biases),
    )
    in_sent, sums = all_after([in_sent, sums], back_second)
    in_first = scatter_row_first(in_sent)
    out_kept, out_got = scatter_col_third(out_parts, out_second)
    back_rest, back_got = scatter_row_third(back_second)

    cot_sum = jnp.sum(cotangent.astype(F32), axis=0, keepdims=True)
    biases = jnp.pad(biases, ((0, 0), (0, width - biases.shape[1])))
    line = jnp.arange(8)[:, None]
    packed = jnp.where(line == 4, cot_sum, jnp.where(line == 5, biases, sums))
    packed = after(packed, *u_first, in_first)
    u_second = scatter_col_second(u_parts, u_first)
    in_second = scatter_row_second(in_kept, in_first, OFFLOAD)
    packed = sum_row(packed)
    qkv_bias_total = lax.dynamic_slice_in_dim(
        packed[5], row_index * qkv_bias.shape[0], qkv_bias.shape[0], 0
    )
    up_bias_total = lax.dynamic_slice_in_dim(
        packed[5], qkv_cols + row_index * up_bias.shape[0], up_bias.shape[0], 0
    )
    packed = sum_col(packed)
    *u_second, first_in_second = all_after([*u_second, in_second[0]], [packed])
    in_second = [first_in_second, *in_second[1:]]
    u_kept, u_got = scatter_col_third(u_parts, u_second)
    in_rest, in_got = scatter_row_third(in_second)
    back_total = back_rest + back_got.astype(F32)
    in_total = in_rest + in_got.astype(F32)
    u_rows = u_kept + u_got.astype(F32)

    tok_rows = tokens.astype(F32)
    layer_out = (
        tok_rows
        + (out_kept + out_got.astype(F32))
        + dense_bias.astype(F32)
        + down_bias.astype(F32)
    ).astype(BF16)
    center = jnp.mean(tok_rows, axis=-1, keepdims=True)
    centered = tok_rows - center
    variance = jnp.mean(centered * centered, axis=-1, keepdims=True)
    inverse = lax.rsqrt(variance + 1e-05)
    normal_rows = centered * inverse
    u_mean = jnp.mean(u_rows, axis=-1, keepdims=True)
    un_mean = jnp.mean(u_rows * normal_rows, axis=-1, keepdims=True)
    d_tokens = (u_rows - u_mean - normal_rows * un_mean) * inverse
    input_grad = (cotangent.astype(F32) + d_tokens).astype(BF16)
    return (
        layer_out,
        input_grad,
        packed[0],
        packed[1],
        packed[2],
        packed[3],
        in_total[:, :qkv_cols],
        qkv_bias_total,
        back_total[:, : back_cols[0]].T,
        packed[4],
        in_total[:, qkv_cols:],
        up_bias_total,
        back_total[:, back_cols[0] :].T,
        packed[4],
    )


def solution(mesh):
    fine = Mesh(mesh.devices.reshape(tuple(SIZES.values())), NAMES)
    everywhere = P(ROW + COL, None)
    return jax.shard_map(
        shards,
        mesh=fine,
        in_specs=(
            everywhere,
            P(ROW, None),
            P(),
            P(),
            P(),
            P(),
            P(ROW, COL),
            P(COL + ROW),
            P(COL, ROW),
            P(),
            P(ROW, COL),
            P(COL + ROW),
            P(COL, ROW),
            P(),
            everywhere,
        ),
        out_specs=(
            everywhere,
            everywhere,
            P(),
            P(),
            P(),
            P(),
            P(ROW, COL),
            P(COL + ROW),
            P(COL, ROW),
            P(),
            P(ROW, COL),
            P(COL + ROW),
            P(COL, ROW),
            P(),
        ),
        check_vma=False,
    )
```

```python
import functools
import itertools
import math

import jax
import jax.numpy as jnp
from jax import lax
from jax.experimental import pallas as pl
from jax.experimental.pallas import tpu as pltpu
from jax.sharding import Mesh
from jax.sharding import PartitionSpec as P

HS = 256
ROT = 64
BLOCK = 256
SIZES = {"xh": 2, "y": 4, "c": 2, "z": 4, "xl": 2}
NAMES = tuple(SIZES)
ROW = ("xh", "y", "c")
COL = ("z", "xl")
F32 = jnp.float32
BF16 = jnp.bfloat16


def light():
    return pl.CostEstimate(flops=1, bytes_accessed=1, transcendentals=0)


def hop(value, **deltas):
    axes = tuple(name for name in NAMES if name in deltas)

    def flat(coords):
        index = 0
        for name, place in zip(axes, coords):
            index = index * SIZES[name] + place % SIZES[name]
        return index

    pairs = []
    for coords in itertools.product(*[range(SIZES[name]) for name in axes]):
        moved = [place + deltas[name] for name, place in zip(axes, coords)]
        pairs.append((flat(coords), flat(moved)))
    return lax.ppermute(value, axes if len(axes) > 1 else axes[0], pairs)


def put(buffer, piece, start):
    return lax.dynamic_update_slice_in_dim(buffer, piece, start, 0)


def rows_at(value, start, count):
    return lax.dynamic_slice_in_dim(value, start, count, 0)


def after(value, *others):
    return lax.optimization_barrier((value, *others))[0]


def all_after(values, others):
    return list(lax.optimization_barrier((*values, *others))[: len(values)])


def ring_near(pair, axis):
    return [hop(pair, **{axis: 1}), hop(pair, **{axis: 3})]


def ring_far(near, axis):
    back, ahead = near
    return [hop(back[:1], **{axis: 1}), hop(ahead[1:], **{axis: 3})]


def places(axis, pair):
    at, own = lax.axis_index(axis), lax.axis_index(pair)
    return {
        "at": at,
        "back": (at + 3) % 4,
        "ahead": (at + 1) % 4,
        "far": (at + 2) % 4,
        "own": own,
        "other": 1 - own,
    }


def group_kernel(count, places_ref, *refs):
    *sources, out_ref, turned_ref = refs
    number = 0
    for source in sources:
        pieces = [source[i] for i in range(source.shape[0])] if len(source.shape) == 3 else [source[...]]
        for piece in pieces:
            start = pl.multiple_of(places_ref[number] * count, count)
            out_ref[pl.ds(start, count), :] = piece
            turned_ref[:, pl.ds(start, count)] = piece.astype(F32).T.astype(BF16)
            number += 1


def rows_of_group(parts, order):
    count, width = parts[0].shape[-2:]
    at = places("z", "xl")
    index = jnp.stack([at[place] * 2 + at[pair] for place, pair in order]).astype(jnp.int32)
    outs = (shape(8 * count, width, BF16), shape(width, 8 * count, BF16))
    return vmem_call(functools.partial(group_kernel, count), outs, (index, *parts), scalars=1)


def gather_row_near(pair):
    return lax.all_gather(pair, ("y", "c"), axis=0)


def scatter_col_first(parts):
    return [hop(parts[0], z=1), hop(parts[1], z=3)]


def scatter_col_second(parts, first):
    low, high = first
    up, down = parts[2], parts[3]
    count = low.shape[0]
    up = jnp.concatenate([up[:count] + low, up[count:]], 0)
    down = jnp.concatenate([down[:count], down[count:] + high], 0)
    return [hop(up, z=1), hop(down, z=3)]


def scatter_col_third(parts, second):
    xl = lax.axis_index("xl")
    own = parts[4]
    count = own.shape[0] // 2

    def total(place):
        return sum(rows_at(part, place * count, count).astype(F32) for part in (own, *second))

    return total(xl), hop(total(1 - xl).astype(BF16), xl=1)


def scatter_row_near(blocks):
    return lax.psum_scatter(blocks.reshape(8, *blocks.shape[2:]), ("y", "c"), scatter_dimension=0)


def scatter_row_far(pair):
    xh = lax.axis_index("xh")
    kept = lax.dynamic_index_in_dim(pair, xh, 0, keepdims=False)
    sent = lax.dynamic_index_in_dim(pair, 1 - xh, 0, keepdims=False)
    return kept, hop(sent, xh=1)


def sum_row(value):
    value = value + hop(value, c=1)
    value = value + hop(value, xh=1)
    return value + hop(value, y=1) + hop(value, y=2) + hop(value, y=3)


def sum_col(value):
    value = value + hop(value, xl=1)
    return value + hop(value, z=1) + hop(value, z=2) + hop(value, z=3)


def nt(left, right):
    return lax.dot_general(left, right, (((1,), (1,)), ((), ())), preferred_element_type=F32)


def tn(left, right):
    return lax.dot_general(left, right, (((0,), (0,)), ((), ())), preferred_element_type=F32)


def nn(left, right):
    return jnp.dot(left, right, preferred_element_type=F32)


def turn(part, cosine, sine):
    lane = lax.broadcasted_iota(jnp.int32, part.shape, 1)
    ahead = pltpu.roll(part, 128 - ROT // 2, 1)
    behind = pltpu.roll(part, ROT // 2, 1)
    return part * cosine + jnp.where(lane < ROT // 2, ahead, behind) * sine


def block_allowed(doc_col, doc_row, start, width):
    docs = doc_col[start : start + BLOCK] == doc_row[:, :width]
    row = start + lax.broadcasted_iota(jnp.int32, (BLOCK, width), 0)
    column = lax.broadcasted_iota(jnp.int32, (BLOCK, width), 1)
    return docs & (column <= row)


def attend_kernel(mix_ref, cos_ref, sin_ref, doc_col_ref, doc_row_ref, qkv_ref, out_ref, log_ref):
    rows = mix_ref.shape[0]
    for start in range(0, rows, BLOCK):
        at = pl.ds(start, BLOCK)
        cosine, sine = cos_ref[at, :], sin_ref[at, :]
        for first in (0, HS):
            head = mix_ref[at, first : first + 128]
            qkv_ref[at, first : first + 128] = turn(head, cosine, sine).astype(BF16)
            qkv_ref[at, first + 128 : first + HS] = mix_ref[at, first + 128 : first + HS].astype(BF16)
        qkv_ref[at, 2 * HS :] = mix_ref[at, 2 * HS :].astype(BF16)
    doc_row = doc_row_ref[...]
    doc_col = doc_col_ref[...]
    for start in range(0, rows, BLOCK):
        width = start + BLOCK
        at = pl.ds(start, BLOCK)
        scores = nt(qkv_ref[at, :HS], qkv_ref[:width, HS : 2 * HS]) * HS ** (-0.5)
        scores = jnp.where(block_allowed(doc_col, doc_row, start, width), scores, -1e30)
        top = jnp.max(scores, axis=1, keepdims=True)
        raised = jnp.exp(scores - top)
        total = jnp.sum(raised, axis=1, keepdims=True)
        probabilities = (raised * (1.0 / total)).astype(BF16)
        out_ref[at, :] = nn(probabilities, qkv_ref[:width, 2 * HS :]).astype(BF16)
        log_ref[at, :] = top + jnp.log(total)


def attend_back_kernel(qkv_ref, grad_ref, log_ref, cos_ref, sin_ref, doc_col_ref, doc_row_ref, out_ref, sum_ref, dk_ref, dv_ref):
    rows = qkv_ref.shape[0]
    scaling = HS ** (-0.5)
    doc_row = doc_row_ref[...]
    doc_col = doc_col_ref[...]
    sums = [jnp.zeros((1, HS), F32) for _ in range(3)]

    def finish(value, start, first):
        at = pl.ds(start, BLOCK)
        head = turn(value[:, :128], cos_ref[at, :], -sin_ref[at, :]).astype(BF16)
        rest = value[:, 128:].astype(BF16)
        out_ref[at, first : first + 128] = head
        out_ref[at, first + 128 : first + HS] = rest
        both = jnp.concatenate([head.astype(F32), rest.astype(F32)], 1)
        return jnp.sum(both, axis=0, keepdims=True)

    for start in range(0, rows, BLOCK):
        width = start + BLOCK
        at = pl.ds(start, BLOCK)
        query = qkv_ref[at, :HS]
        grad = grad_ref[at, :]
        scores = nt(query, qkv_ref[:width, HS : 2 * HS]) * scaling
        allowed = block_allowed(doc_col, doc_row, start, width)
        weights = jnp.where(allowed, jnp.exp(scores - log_ref[at, :]), 0.0)
        probabilities = weights.astype(BF16)
        d_probs = nt(grad, qkv_ref[:width, 2 * HS :])
        inner = jnp.sum(weights * d_probs, axis=1, keepdims=True)
        d_scores = (weights * (d_probs - inner)).astype(BF16)
        d_values = tn(probabilities, grad)
        d_keys = tn(d_scores, query) * scaling
        if start:
            dv_ref[:start, :] += d_values[:start]
            dk_ref[:start, :] += d_keys[:start]
        dv_ref[start:width, :] = d_values[start:]
        dk_ref[start:width, :] = d_keys[start:]
        d_query = nn(d_scores, qkv_ref[:width, HS : 2 * HS]) * scaling
        sums[0] = sums[0] + finish(d_query, start, 0)
    for start in range(0, rows, BLOCK):
        at = pl.ds(start, BLOCK)
        sums[1] = sums[1] + finish(dk_ref[at, :], start, HS)
        values = dv_ref[at, :].astype(BF16)
        out_ref[at, 2 * HS :] = values
        sums[2] = sums[2] + jnp.sum(values.astype(F32), axis=0, keepdims=True)
    for part in range(3):
        sum_ref[:, part * HS : (part + 1) * HS] = sums[part]


PART = 256


def whole_spec(array):
    return pl.BlockSpec(array.shape, lambda i: (0,) * array.ndim)


def columns_spec(rows, first=0, last=None):
    if last is None:
        return pl.BlockSpec((rows, PART), lambda i: (0, i + first))
    return pl.BlockSpec((rows, PART), lambda i: (0, jnp.clip(i + first, 0, last)))


def grid_call(kernel, steps, outs, out_specs, args, in_specs, scratch=()):
    return pl.pallas_call(
        kernel,
        grid=(steps,),
        out_shape=tuple(outs),
        in_specs=in_specs,
        out_specs=tuple(out_specs),
        scratch_shapes=scratch,
        compiler_params=pltpu.CompilerParams(vmem_limit_bytes=48 * 1024 * 1024),
        cost_estimate=light(),
    )(*args)


def project_kernel(z_ref, one_ref, two_ref, weight_ref, low_ref, high_ref, up_ref, down_ref, own_ref, both_ref, held_ref):
    z = z_ref[0]
    part = held_ref.shape[0] // 4

    @pl.when(pl.program_id(0) == 0)
    def _():
        both_ref[:, : one_ref.shape[1]] = one_ref[...]
        both_ref[:, one_ref.shape[1] :] = two_ref[...]

    block = weight_ref[...].reshape(-1, weight_ref.shape[-1])
    held_ref[...] = nt(both_ref[...], block).astype(BF16)

    def cut(step, start, count):
        place = pl.multiple_of((z + step) % 4 * part, part)
        return held_ref[pl.ds(place + start, count), :]

    low_ref[...] = cut(2, 0, part // 2)
    high_ref[...] = cut(2, part // 2, part // 2)
    up_ref[...] = cut(1, 0, part)
    down_ref[...] = cut(3, 0, part)
    own_ref[...] = cut(0, 0, part)


def project(one, two, weights):
    rows, width = one.shape[0], one.shape[1] + two.shape[1]
    if weights.ndim == 2:
        features = weights.shape[0]
        step = features // 4
        weight_spec = pl.BlockSpec((step, width), lambda i: (i, 0))
    else:
        features = math.prod(weights.shape[:3])
        step = features // 4
        weight_spec = pl.BlockSpec(
            (weights.shape[0] // 2, 1, *weights.shape[2:]), lambda i: (i % 2, i // 2, 0, 0)
        )
    z = lax.axis_index("z").astype(jnp.int32)[None]
    counts = (rows // 8, rows // 8, rows // 4, rows // 4, rows // 4)
    return grid_call(
        project_kernel,
        4,
        [shape(count, features, BF16) for count in counts],
        [pl.BlockSpec((count, step), lambda i: (0, i)) for count in counts],
        (z, one, two, weights),
        [pl.BlockSpec(memory_space=pltpu.SMEM), whole_spec(one), whole_spec(two), weight_spec],
        scratch=[pltpu.VMEM((rows, width), BF16), pltpu.VMEM((rows, step), BF16)],
    )


CHUNK = 256


def put_rows(out_ref, start, values):
    count = out_ref.shape[3]
    for row in range(start, start + values.shape[0], count):
        xh, y, core = row // (8 * count), row // (2 * count) % 4, row // count % 2
        out_ref[y, core, xh] = values[row - start : row - start + count]


def back_grads_kernel(split, turned_ref, one_ref, two_ref, out_ref):
    def step(right_ref):
        put_rows(out_ref, 0, nn(turned_ref[...], right_ref[...]).astype(BF16))

    @pl.when(pl.program_id(0) < split)
    def _():
        step(one_ref)

    @pl.when(pl.program_id(0) >= split)
    def _():
        step(two_ref)


def in_grads_kernel(split, turned_ref, one_ref, two_ref, norm_ref, weight_ref, bias_ref, out_ref, sums_ref, held_ref):
    features = turned_ref.shape[0]

    @pl.when(pl.program_id(0) == 0)
    def _():
        held_ref[...] = jnp.zeros_like(held_ref)

    def step(right_ref, first):
        bias = bias_ref[...]
        for start in range(0, features, CHUNK):
            at = slice(start, start + CHUNK)
            raw = nn(turned_ref[at, :], right_ref[...])
            wide = weight_ref[at, :].astype(F32)
            gain_part, shift_part = wide * raw, wide * bias
            held_ref[first, at, :] += gain_part[:, :128] + gain_part[:, 128:]
            held_ref[first + 1, at, :] += shift_part[:, :128] + shift_part[:, 128:]
            put_rows(out_ref, start, raw.astype(BF16))

    @pl.when(pl.program_id(0) < split)
    def _():
        step(one_ref, 0)

    @pl.when(pl.program_id(0) >= split)
    def _():
        step(two_ref, 2)

    @pl.when(pl.program_id(0) == pl.num_programs(0) - 1)
    def _():
        for number in range(4):
            total = jnp.sum(held_ref[number].T, axis=0, keepdims=True)
            gain = number // 2 * 2
            sums_ref[number : number + 1, :] = total / norm_ref[gain : gain + 1, :]
        sums_ref[4:, :] = jnp.zeros((4, features), F32)


def weight_grads(turned, one, two, extra=None):
    features, rows = turned.shape
    count = features // 16
    split, steps = one.shape[1] // PART, (one.shape[1] + two.shape[1]) // PART
    args = [turned, one, two]
    in_specs = [
        whole_spec(turned),
        columns_spec(rows, 0, split - 1),
        columns_spec(rows, -split, steps - split - 1),
    ]
    outs = [jax.ShapeDtypeStruct((4, 2, 2, count, steps * PART), BF16)]
    out_specs = [pl.BlockSpec((4, 2, 2, count, PART), lambda i: (0, 0, 0, 0, i))]
    kernel, scratch = back_grads_kernel, []
    if extra is not None:
        kernel = in_grads_kernel
        vectors, weights, bias = extra
        args += [vectors, weights, bias]
        in_specs += [whole_spec(vectors), columns_spec(features), columns_spec(1)]
        outs.append(shape(8, features, F32))
        out_specs.append(whole_spec(outs[-1]))
        scratch = [pltpu.VMEM((4, features, 128), F32)]
    kernel = functools.partial(kernel, split)
    return grid_call(kernel, steps, outs, out_specs, args, in_specs, scratch=scratch)


def gelu_pair(hidden):
    normal = 0.5 * (1.0 + lax.erf(hidden * (1.0 / math.sqrt(2.0))))
    density = jnp.exp(-0.5 * hidden * hidden) * (1.0 / math.sqrt(2.0 * math.pi))
    return (hidden * normal, normal + hidden * density)


def forward_kernel(split, normal_ref, weight_ref, extra_ref, mix_ref, active_ref, slope_ref, bias_ref):
    count = extra_ref.shape[1]
    step = pl.program_id(0)

    @pl.when(step == 0)
    def _():
        total = jnp.zeros((32, 128), F32)
        for place in range(extra_ref.shape[0] // count):
            total = total + extra_ref[place * count : place * count + 32, :].astype(F32)
        lines = (mix_ref.shape[0] // 1024) * 14
        for line in range(lines):
            both = total[line : line + 1] + total[lines + line : lines + line + 1]
            bias_ref[line // 2 : line // 2 + 1, 128 * (line % 2) : 128 * (line % 2 + 1)] = both

    bias = bias_ref[pl.ds(step, 1), :]

    @pl.when(step < split)
    def _():
        mix_ref[...] = nn(normal_ref[...], weight_ref[...]) + bias

    @pl.when(step >= split)
    def _():
        rows = normal_ref.shape[0]
        for start in range(0, rows, 256):
            at = slice(start, start + 256)
            active, slope = gelu_pair(nn(normal_ref[at, :], weight_ref[...]) + bias)
            active_ref[at, :] = active.astype(BF16)
            slope_ref[at, :] = slope.astype(BF16)


def forward(normal, weights, qkv_cols, up_cols):
    rows, features = normal.shape
    split, steps = qkv_cols // PART, (qkv_cols + up_cols) // PART
    outs = [shape(rows, qkv_cols, F32), shape(rows, up_cols, BF16), shape(rows, up_cols, BF16)]
    late = columns_spec(rows, -split, steps - split - 1)
    extra_place = weights.shape[1] // 128 - 1
    return grid_call(
        functools.partial(forward_kernel, split),
        steps,
        outs,
        [columns_spec(rows, 0, split - 1), late, late],
        (normal, weights, weights),
        [
            whole_spec(normal),
            columns_spec(features),
            pl.BlockSpec((features, 128), lambda i: (0, extra_place)),
        ],
        scratch=[pltpu.VMEM((8, PART), F32)],
    )


def backward_kernel(split, cot_ref, weight_ref, slope_ref, att_ref, hid_ref, sum_ref):
    def product():
        half = cot_ref.shape[1] // 2
        parts = [weight_ref[:, xh].reshape(half, -1) for xh in range(2)]
        return nn(cot_ref[:, :half], parts[0]) + nn(cot_ref[:, half:], parts[1])

    @pl.when(pl.program_id(0) < split)
    def _():
        att_ref[...] = product().astype(BF16)

    @pl.when(pl.program_id(0) >= split)
    def _():
        value = (product() * slope_ref[...].astype(F32)).astype(BF16)
        hid_ref[...] = value
        sum_ref[...] = jnp.sum(value.astype(F32), axis=0, keepdims=True)


def backward(cot, weights, slope, dense_cols, down_cols):
    rows, features = cot.shape
    split, steps = dense_cols // PART, (dense_cols + down_cols) // PART
    outs = [shape(rows, dense_cols, BF16), shape(rows, down_cols, BF16), shape(1, down_cols, F32)]
    return grid_call(
        functools.partial(backward_kernel, split),
        steps,
        outs,
        [
            columns_spec(rows, 0, split - 1),
            columns_spec(rows, -split, steps - split - 1),
            columns_spec(1, -split, steps - split - 1),
        ],
        (cot, weights, slope),
        [
            whole_spec(cot),
            pl.BlockSpec((*weights.shape[:3], PART), lambda i: (0, 0, 0, i)),
            columns_spec(rows, -split, steps - split - 1),
        ],
    )


def finish_back_kernel(kept_ref, got_ref, dense_ref, down_ref):
    total = kept_ref[...].astype(F32) + got_ref[...].astype(F32)
    first = dense_ref.shape[0]
    dense_ref[...] = total[:, :first].T
    down_ref[...] = total[:, first:].T


def finish_in_kernel(row_ref, kept_ref, got_ref, norm_ref, bias_ref, qkv_ref, up_ref):
    total = kept_ref[...].astype(F32) + got_ref[...].astype(F32)

    def column(which):
        return own_column(row_ref, norm_ref, which, total.shape[0])

    first = 0
    for number, out_ref in enumerate((qkv_ref, up_ref)):
        at = slice(first, first + out_ref.shape[1])
        out_ref[...] = total[:, at] * column(2 * number) + column(2 * number + 1) * bias_ref[:, at]
        first += out_ref.shape[1]


def input_grad_kernel(tok_ref, cot_ref, kept_ref, got_ref, out_ref):
    tok_rows = tok_ref[...].astype(F32)
    center = jnp.mean(tok_rows, axis=-1, keepdims=True)
    centered = tok_rows - center
    variance = jnp.mean(centered * centered, axis=-1, keepdims=True)
    inverse = lax.rsqrt(variance + 1e-05)
    normal = centered * inverse
    u_rows = kept_ref[...] + got_ref[...].astype(F32)
    u_mean = jnp.mean(u_rows, axis=-1, keepdims=True)
    un_mean = jnp.mean(u_rows * normal, axis=-1, keepdims=True)
    d_rows = (u_rows - u_mean - normal * un_mean) * inverse
    out_ref[...] = (cot_ref[...].astype(F32) + d_rows).astype(BF16)


def own_column(row_ref, norm_ref, which, count):
    start = pl.multiple_of(row_ref[0] * count, count)
    square = (count, count)
    diagonal = lax.broadcasted_iota(jnp.int32, square, 0) == lax.broadcasted_iota(jnp.int32, square, 1)
    lanes = norm_ref[which : which + 1, pl.ds(start, count)].astype(F32)
    return jnp.sum(jnp.where(diagonal, jnp.broadcast_to(lanes, square), 0.0), axis=1, keepdims=True)


def prepare_kernel(row_ref, tok_ref, gain_one_ref, shift_one_ref, gain_two_ref, shift_two_ref, qkv_ref, up_ref, dense_ref, down_ref, qkv_bias_ref, up_bias_ref, normal_ref, out_ref, back_ref):
    tok_rows = tok_ref[...].astype(F32)
    center = jnp.mean(tok_rows, axis=-1, keepdims=True)
    centered = tok_rows - center
    variance = jnp.mean(centered * centered, axis=-1, keepdims=True)
    normal_ref[...] = (centered * lax.rsqrt(variance + 1e-05)).astype(BF16)
    count = qkv_ref.shape[0]

    def placed(bias_ref, width):
        own = bias_ref[...].astype(F32)
        rest = jnp.zeros((1, width - own.shape[1]), F32)
        wide = jnp.broadcast_to(jnp.concatenate([own, rest], 1), (8, width))
        return pltpu.roll(wide, row_ref[0] * own.shape[1], 1)[:1]

    lines = []
    first = 0
    for gain, shift, weight, bias in (
        (gain_one_ref, shift_one_ref, qkv_ref, qkv_bias_ref),
        (gain_two_ref, shift_two_ref, up_ref, up_bias_ref),
    ):
        width = weight.shape[1]
        wide = weight[...].astype(F32)
        out_ref[:, first : first + width] = (wide * own_column(row_ref, gain, 0, count)).astype(BF16)
        shifted = jnp.sum(wide * own_column(row_ref, shift, 0, count), axis=0, keepdims=True)
        shifted = shifted + placed(bias, width)
        lines += [shifted[:, 128 * i : 128 * (i + 1)] for i in range(width // 128)]
        first += width
    first_back = 0
    for weight in (dense_ref, down_ref):
        width = weight.shape[0]
        back_ref[:, first_back : first_back + width] = weight[...].astype(F32).T.astype(BF16)
        first_back += width
    high = [line.astype(BF16).astype(F32) for line in lines]
    low = [line - part for line, part in zip(lines, high)]
    rest = jnp.zeros((count - 2 * len(lines), 128), F32)
    out_ref[:, first:] = jnp.concatenate([*high, *low, rest], 0).astype(BF16)


def vmem_call(kernel, outs, args, scratch=(), scalars=0, limit=40):
    spec = pl.BlockSpec()
    scalar = pl.BlockSpec(memory_space=pltpu.SMEM)
    return pl.pallas_call(
        kernel,
        out_shape=outs,
        in_specs=[scalar] * scalars + [spec] * (len(args) - scalars),
        out_specs=[spec] * len(outs),
        scratch_shapes=scratch,
        compiler_params=pltpu.CompilerParams(vmem_limit_bytes=limit * 1024 * 1024),
        cost_estimate=light(),
    )(*args)


def shape(rows, columns, dtype):
    return jax.ShapeDtypeStruct((rows, columns), dtype)


def attend(mix, cosine, sine, doc_col, doc_row):
    rows = mix.shape[0]
    outs = (shape(rows, 3 * HS, BF16), shape(rows, HS, BF16), shape(rows, 1, F32))
    return vmem_call(
        attend_kernel,
        outs,
        (mix, cosine, sine, doc_col, doc_row),
    )


def attend_back(qkv, grad, logs, cosine, sine, doc_col, doc_row):
    rows = qkv.shape[0]
    outs = (shape(rows, 3 * HS, BF16), shape(1, 3 * HS, F32))
    return vmem_call(
        attend_back_kernel,
        outs,
        (qkv, grad, logs, cosine, sine, doc_col, doc_row),
        scratch=[pltpu.VMEM((rows, HS), F32), pltpu.VMEM((rows, HS), F32)],
    )


def doc_layout(lengths, places):
    first, second = lengths[0], lengths[0] + lengths[1]
    third = second + lengths[2]
    passed = [(places >= end).astype(jnp.int32) for end in (first, second, third)]
    doc_ids = passed[0] + passed[1] + passed[2]
    begins = passed[0] * lengths[0] + passed[1] * lengths[1] + passed[2] * lengths[2]
    return (doc_ids, places - begins)


def rotary_tables(positions):
    half = ROT // 2
    lane = jnp.arange(128, dtype=jnp.int32)
    frequency = 1.0 / 10000.0 ** ((lane % half).astype(F32) * (2.0 / ROT))
    frequency = jnp.where(lane < ROT, frequency, 0.0)
    angles = positions.astype(F32) * frequency[None, :]
    sign = jnp.where(lane < half, -1.0, 1.0)
    return (jnp.cos(angles), jnp.sin(angles) * sign[None, :])


def shards(
    tokens,
    doc_lengths,
    input_gain,
    input_shift,
    post_gain,
    post_shift,
    qkv_weight,
    qkv_bias,
    dense_weight,
    dense_bias,
    up_weight,
    up_bias,
    down_weight,
    down_bias,
    cotangent,
):
    row_index = (lax.axis_index("xh") * 4 + lax.axis_index("y")) * 2 + lax.axis_index("c")
    slice_rows = qkv_weight.shape[0]
    qkv_cols, up_cols = qkv_weight.shape[1], up_weight.shape[1]

    tok_count, width = tokens.shape
    back_cols = (dense_weight.shape[0], down_weight.shape[0])
    own_normal, block, block_back = vmem_call(
        prepare_kernel,
        (
            shape(tok_count, width, BF16),
            shape(slice_rows, qkv_cols + up_cols + 128, BF16),
            shape(slice_rows, sum(back_cols), BF16),
        ),
        (
            row_index.astype(jnp.int32)[None],
            tokens,
            input_gain[None],
            input_shift[None],
            post_gain[None],
            post_shift[None],
            qkv_weight,
            up_weight,
            dense_weight,
            down_weight,
            qkv_bias[None],
            up_bias[None],
        ),
        scalars=1,
        limit=60,
    )
    weights = lax.all_gather(block, ROW, axis=0, tiled=True)
    in_cols = qkv_cols + up_cols

    row_count = 8 * tok_count
    doc_col, positions = doc_layout(doc_lengths[0], jnp.arange(row_count, dtype=jnp.int32)[:, None])
    doc_row, _ = doc_layout(doc_lengths[0], jnp.arange(row_count, dtype=jnp.int32)[None, :])
    tables = (*rotary_tables(positions), doc_col, doc_row)

    cot_near = ring_near(cotangent, "z")
    normal_other = hop(own_normal, xl=1)
    normal_pair, cot_own, back_own, *tables = all_after(
        [jnp.stack([own_normal, normal_other]), cotangent, block_back, *tables], cot_near
    )
    normal_near = ring_near(normal_pair, "z")
    cot_other = hop(cot_own, xl=1)
    back_other = hop(back_own, xh=1)
    held = all_after([*normal_near, cot_other, back_other], [])
    normal_far = ring_far(held[:2], "z")
    cot_other_near = ring_near(held[2], "z")
    xh = lax.axis_index("xh")
    back_pair = [jnp.where(xh == first, block_back, held[3]) for first in range(2)]
    back_weights = gather_row_near(jnp.stack(back_pair))
    order = [(at, pair) for at in ("at", "back", "ahead", "far") for pair in ("own", "other")]
    normal_all, normal_turned = rows_of_group([normal_pair, *normal_near, *normal_far], order)
    held = all_after([cot_near[0], cot_other_near[1]], [normal_all])
    cot_far = [hop(held[0], z=1), hop(held[1], z=3)]

    mixture, active, slope = forward(normal_all, weights, qkv_cols, up_cols)
    mixture, *cot_far = all_after([mixture, *cot_far], [])
    qkv, attended, logs = attend(mixture, *tables)
    cot_parts = [
        cotangent,
        cot_other,
        cot_near[0],
        cot_other_near[0],
        cot_near[1],
        cot_other_near[1],
        *cot_far,
    ]
    cot_all, cot_turned = rows_of_group(cot_parts, order)
    (back_grads,) = weight_grads(cot_turned, attended, active)
    back_sum = scatter_row_near(back_grads)
    attended, active = all_after([attended, active], [back_grads])
    out_parts = project(attended, active, back_weights)
    out_first = scatter_col_first(out_parts)

    cot_all = after(cot_all, out_parts[0])
    d_attended, d_hidden, up_bias_part = backward(cot_all, back_weights, slope, *back_cols)
    d_attended, d_hidden, *out_first = all_after([d_attended, d_hidden, *out_first], [])
    out_second = scatter_col_second(out_parts, out_first)
    d_mixture, qkv_bias_part = attend_back(qkv, d_attended, logs, *tables)
    biases = jnp.concatenate([qkv_bias_part, up_bias_part], 1)
    vectors = jnp.stack([input_gain, input_shift, post_gain, post_shift]).astype(F32)
    padded = jnp.pad(vectors, ((0, 4), (0, 0)))
    in_grads, sums = weight_grads(normal_turned, d_mixture, d_hidden, (padded, weights, biases))
    in_grads, sums, d_mixture, d_hidden, *out_second = all_after(
        [in_grads, sums, d_mixture, d_hidden, *out_second], []
    )
    back_kept, back_got = scatter_row_far(after(back_sum, sums))
    in_pair = scatter_row_near(in_grads)
    out_kept, out_got = scatter_col_third(out_parts, out_second)
    u_parts = project(d_mixture, d_hidden, weights)
    u_first = scatter_col_first(u_parts)

    def flat(kept, got):
        return (kept.reshape(slice_rows, -1), got.reshape(slice_rows, -1))

    dense_total, down_total = vmem_call(
        finish_back_kernel,
        tuple(shape(cols, slice_rows, F32) for cols in back_cols),
        flat(back_kept, back_got),
    )
    layer_out = (
        tokens.astype(F32)
        + (out_kept + out_got.astype(F32))
        + dense_bias.astype(F32)
        + down_bias.astype(F32)
    ).astype(BF16)

    cot_sum = jnp.sum(cotangent.astype(F32), axis=0, keepdims=True)
    biases = jnp.pad(biases, ((0, 0), (0, width - biases.shape[1])))
    line = jnp.arange(8)[:, None]
    packed = jnp.where(line == 4, cot_sum, jnp.where(line == 5, biases, sums))
    packed = sum_row(after(packed, u_parts[0]))
    qkv_bias_total = lax.dynamic_slice_in_dim(
        packed[5], row_index * qkv_bias.shape[0], qkv_bias.shape[0], 0
    )
    up_bias_total = lax.dynamic_slice_in_dim(
        packed[5], qkv_cols + row_index * up_bias.shape[0], up_bias.shape[0], 0
    )
    u_first = all_after(u_first, [packed, dense_total, down_total, layer_out])
    u_second = scatter_col_second(u_parts, u_first)
    bias_total = packed[5:6]
    packed = sum_col(packed)
    in_kept, in_got = scatter_row_far(in_pair)
    *u_second, in_got = all_after([*u_second, in_got], [])
    u_kept, u_got = scatter_col_third(u_parts, u_second)
    qkv_total, up_total = vmem_call(
        finish_in_kernel,
        tuple(shape(slice_rows, cols, F32) for cols in (qkv_cols, up_cols)),
        (row_index.astype(jnp.int32)[None], *flat(in_kept, in_got), padded, bias_total),
        scalars=1,
    )
    (input_grad,) = vmem_call(
        input_grad_kernel,
        (shape(tok_count, width, BF16),),
        (tokens, cotangent, u_kept, u_got),
    )

    return (
        layer_out,
        input_grad,
        packed[0],
        packed[1],
        packed[2],
        packed[3],
        qkv_total,
        qkv_bias_total,
        dense_total,
        packed[4],
        up_total,
        up_bias_total,
        down_total,
        packed[4],
    )


def solution(mesh):
    fine = Mesh(mesh.devices.reshape(tuple(SIZES.values())), NAMES)
    everywhere = P(ROW + COL, None)
    return jax.shard_map(
        shards,
        mesh=fine,
        in_specs=(
            everywhere,
            P(ROW, None),
            P(),
            P(),
            P(),
            P(),
            P(ROW, COL),
            P(COL + ROW),
            P(COL, ROW),
            P(),
            P(ROW, COL),
            P(COL + ROW),
            P(COL, ROW),
            P(),
            everywhere,
        ),
        out_specs=(
            everywhere,
            everywhere,
            P(),
            P(),
            P(),
            P(),
            P(ROW, COL),
            P(COL + ROW),
            P(COL, ROW),
            P(),
            P(ROW, COL),
            P(COL + ROW),
            P(COL, ROW),
            P(),
        ),
        check_vma=False,
    )
```

```python
import functools
import itertools
import math

import jax
import jax.numpy as jnp
from jax import lax
from jax.experimental import pallas as pl
from jax.experimental.pallas import tpu as pltpu
from jax.sharding import Mesh
from jax.sharding import PartitionSpec as P

HS = 256
ROT = 64
BLOCK = 256
SIZES = {"xh": 2, "y": 4, "c": 2, "z": 4, "xl": 2}
NAMES = tuple(SIZES)
ROW = ("xh", "y", "c")
COL = ("z", "xl")
F32 = jnp.float32
BF16 = jnp.bfloat16


def light():
    return pl.CostEstimate(flops=1, bytes_accessed=1, transcendentals=0)


def hop(value, **deltas):
    return send(value, tuple(deltas), lambda coords: [c + deltas[name] for name, c in coords.items()])


def swap(value, axis):
    return send(value, (axis,), lambda coords: [coords[axis] ^ 1])


def send(value, names, target):
    axes = tuple(name for name in NAMES if name in names)

    def flat(coords):
        index = 0
        for name, place in zip(axes, coords):
            index = index * SIZES[name] + place % SIZES[name]
        return index

    pairs = []
    for coords in itertools.product(*[range(SIZES[name]) for name in axes]):
        pairs.append((flat(coords), flat(target(dict(zip(axes, coords))))))
    return lax.ppermute(value, axes if len(axes) > 1 else axes[0], pairs)


def rows_at(value, start, count):
    return lax.dynamic_slice_in_dim(value, start, count, 0)


def after(value, *others):
    return lax.optimization_barrier((value, *others))[0]


def all_after(values, others):
    return list(lax.optimization_barrier((*values, *others))[: len(values)])


def ring_near(pair, axis):
    return [hop(pair, **{axis: 1}), hop(pair, **{axis: 3})]


def ring_far(near, axis):
    back, ahead = near
    return [hop(back[:1], **{axis: 1}), hop(ahead[1:], **{axis: 3})]


def places(axis, pair):
    at, own = lax.axis_index(axis), lax.axis_index(pair)
    return {
        "at": at,
        "back": (at + 3) % 4,
        "ahead": (at + 1) % 4,
        "far": (at + 2) % 4,
        "own": own,
        "other": 1 - own,
    }


def group_kernel(count, places_ref, *refs):
    *sources, out_ref = refs
    number = 0
    for source in sources:
        pieces = [source[i] for i in range(source.shape[0])] if len(source.shape) == 3 else [source[...]]
        for piece in pieces:
            start = pl.multiple_of(places_ref[number] * count, count)
            out_ref[pl.ds(start, count), :] = piece
            number += 1


def rows_of_group(parts, order):
    count, width = parts[0].shape[-2:]
    at = places("z", "xl")
    index = jnp.stack([at[place] * 2 + at[pair] for place, pair in order]).astype(jnp.int32)
    outs = (shape(8 * count, width, BF16),)
    (whole,) = vmem_call(functools.partial(group_kernel, count), outs, (index, *parts), scalars=1)
    return whole


def gather_row_near(pair):
    return lax.all_gather(pair, ("y", "c"), axis=0)


def scatter_col_first(far):
    return [hop(far[0], z=1), hop(far[1], z=3)]


def scatter_col_second(near, first):
    low, high = first
    up, down = near[:2]
    count = low.shape[0]
    up = jnp.concatenate([up[:count] + low, up[count:]], 0)
    down = jnp.concatenate([down[:count], down[count:] + high], 0)
    return [hop(up, z=1), hop(down, z=3)]


def scatter_col_third(near, second):
    xl = lax.axis_index("xl")
    own = near[2]
    count = own.shape[0] // 2

    def total(place):
        return sum(rows_at(part, place * count, count).astype(F32) for part in (own, *second))

    return total(xl), hop(total(1 - xl).astype(BF16), xl=1)


def scatter_row_near(blocks):
    return lax.psum_scatter(blocks.reshape(8, *blocks.shape[2:]), ("y", "c"), scatter_dimension=0)


def scatter_row_far(pair):
    xh = lax.axis_index("xh")
    kept = lax.dynamic_index_in_dim(pair, xh, 0, keepdims=False)
    sent = lax.dynamic_index_in_dim(pair, 1 - xh, 0, keepdims=False)
    return kept, hop(sent, xh=1)


def nt(left, right):
    return lax.dot_general(left, right, (((1,), (1,)), ((), ())), preferred_element_type=F32)


def tn(left, right):
    return lax.dot_general(left, right, (((0,), (0,)), ((), ())), preferred_element_type=F32)


def nn(left, right):
    return jnp.dot(left, right, preferred_element_type=F32)


def turn(part, cosine, sine):
    lane = lax.broadcasted_iota(jnp.int32, part.shape, 1)
    ahead = pltpu.roll(part, 128 - ROT // 2, 1)
    behind = pltpu.roll(part, ROT // 2, 1)
    return part * cosine + jnp.where(lane < ROT // 2, ahead, behind) * sine


def block_allowed(doc_col, doc_row, start, width):
    docs = doc_col[start : start + BLOCK] == doc_row[:, :width]
    row = start + lax.broadcasted_iota(jnp.int32, (BLOCK, width), 0)
    column = lax.broadcasted_iota(jnp.int32, (BLOCK, width), 1)
    return docs & (column <= row)


def attend(mix_ref, cos_ref, sin_ref, doc_col_ref, doc_row_ref, qkv_ref, out_ref, log_ref):
    rows = mix_ref.shape[1]
    for start in range(0, rows, BLOCK):
        at = pl.ds(start, BLOCK)
        cosine, sine = cos_ref[at, :], sin_ref[at, :]
        for part in range(2):
            first = part * HS
            qkv_ref[at, first : first + 128] = turn(mix_ref[part, at, :128], cosine, sine).astype(BF16)
            qkv_ref[at, first + 128 : first + HS] = mix_ref[part, at, 128:].astype(BF16)
        qkv_ref[at, 2 * HS :] = mix_ref[2, at, :].astype(BF16)
    doc_row = doc_row_ref[...]
    doc_col = doc_col_ref[...]
    for start in range(0, rows, BLOCK):
        width = start + BLOCK
        at = pl.ds(start, BLOCK)
        scores = nt(qkv_ref[at, :HS], qkv_ref[:width, HS : 2 * HS]) * HS ** (-0.5)
        scores = jnp.where(block_allowed(doc_col, doc_row, start, width), scores, -1e30)
        top = jnp.max(scores, axis=1, keepdims=True)
        raised = jnp.exp(scores - top)
        total = jnp.sum(raised, axis=1, keepdims=True)
        probabilities = (raised * (1.0 / total)).astype(BF16)
        out_ref[at, :] = nn(probabilities, qkv_ref[:width, 2 * HS :]).astype(BF16)
        log_ref[at, :] = top + jnp.log(total)


def attend_back_kernel(qkv_ref, grad_ref, log_ref, cos_ref, sin_ref, doc_col_ref, doc_row_ref, out_ref, sum_ref, dk_ref, dv_ref):
    rows = qkv_ref.shape[0]
    scaling = HS ** (-0.5)
    doc_row = doc_row_ref[...]
    doc_col = doc_col_ref[...]
    sums = [jnp.zeros((1, HS), F32) for _ in range(3)]

    def finish(value, start, first):
        at = pl.ds(start, BLOCK)
        head = turn(value[:, :128], cos_ref[at, :], -sin_ref[at, :]).astype(BF16)
        rest = value[:, 128:].astype(BF16)
        out_ref[at, first : first + 128] = head
        out_ref[at, first + 128 : first + HS] = rest
        both = jnp.concatenate([head.astype(F32), rest.astype(F32)], 1)
        return jnp.sum(both, axis=0, keepdims=True)

    for start in range(0, rows, BLOCK):
        width = start + BLOCK
        at = pl.ds(start, BLOCK)
        query = qkv_ref[at, :HS]
        grad = grad_ref[at, :]
        scores = nt(query, qkv_ref[:width, HS : 2 * HS]) * scaling
        allowed = block_allowed(doc_col, doc_row, start, width)
        weights = jnp.where(allowed, jnp.exp(scores - log_ref[at, :]), 0.0)
        probabilities = weights.astype(BF16)
        d_probs = nt(grad, qkv_ref[:width, 2 * HS :])
        inner = jnp.sum(weights * d_probs, axis=1, keepdims=True)
        d_scores = (weights * (d_probs - inner)).astype(BF16)
        d_values = tn(probabilities, grad)
        d_keys = tn(d_scores, query) * scaling
        if start:
            dv_ref[:start, :] += d_values[:start]
            dk_ref[:start, :] += d_keys[:start]
        dv_ref[start:width, :] = d_values[start:]
        dk_ref[start:width, :] = d_keys[start:]
        d_query = nn(d_scores, qkv_ref[:width, HS : 2 * HS]) * scaling
        sums[0] = sums[0] + finish(d_query, start, 0)
    for start in range(0, rows, BLOCK):
        at = pl.ds(start, BLOCK)
        sums[1] = sums[1] + finish(dk_ref[at, :], start, HS)
        values = dv_ref[at, :].astype(BF16)
        out_ref[at, 2 * HS :] = values
        sums[2] = sums[2] + jnp.sum(values.astype(F32), axis=0, keepdims=True)
    for part in range(3):
        sum_ref[:, part * HS : (part + 1) * HS] = sums[part]


PART = 256


def whole_spec(array):
    return pl.BlockSpec(array.shape, lambda i: (0,) * array.ndim)


def columns_spec(rows, first=0, last=None):
    if last is None:
        return pl.BlockSpec((rows, PART), lambda i: (0, i + first))
    return pl.BlockSpec((rows, PART), lambda i: (0, jnp.clip(i + first, 0, last)))


def grid_call(kernel, steps, outs, out_specs, args, in_specs, scratch=()):
    return pl.pallas_call(
        kernel,
        grid=(steps,),
        out_shape=tuple(outs),
        in_specs=in_specs,
        out_specs=tuple(out_specs),
        scratch_shapes=scratch,
        compiler_params=pltpu.CompilerParams(vmem_limit_bytes=48 * 1024 * 1024),
        cost_estimate=light(),
    )(*args)


def project_kernel(steps, z_ref, one_ref, two_ref, weight_ref, *refs):
    *out_refs, both_ref = refs
    part = one_ref.shape[0] // 4

    @pl.when(pl.program_id(0) == 0)
    def _():
        for number, step in enumerate(steps):
            rows = pl.ds(pl.multiple_of((z_ref[0] + step) % 4 * part, part), part)
            at = slice(number * part, (number + 1) * part)
            both_ref[at, : one_ref.shape[1]] = one_ref[rows, :]
            both_ref[at, one_ref.shape[1] :] = two_ref[rows, :]

    block = weight_ref[...].reshape(-1, weight_ref.shape[-1])
    total = nt(both_ref[...], block).astype(BF16)
    first = 0
    for out_ref in out_refs:
        out_ref[...] = total[first : first + out_ref.shape[0]]
        first += out_ref.shape[0]


def project(one, two, weights, steps, counts):
    rows, width = one.shape[0], one.shape[1] + two.shape[1]
    if weights.ndim == 2:
        features = weights.shape[0]
        step = features // 4
        weight_spec = pl.BlockSpec((step, width), lambda i: (i, 0))
    else:
        features = math.prod(weights.shape[:3])
        step = features // 4
        weight_spec = pl.BlockSpec(
            (weights.shape[0] // 2, 1, *weights.shape[2:]), lambda i: (i % 2, i // 2, 0, 0)
        )
    z = lax.axis_index("z").astype(jnp.int32)[None]
    return grid_call(
        functools.partial(project_kernel, steps),
        4,
        [shape(count, features, BF16) for count in counts],
        [pl.BlockSpec((count, step), lambda i: (0, i)) for count in counts],
        (z, one, two, weights),
        [pl.BlockSpec(memory_space=pltpu.SMEM), whole_spec(one), whole_spec(two), weight_spec],
        scratch=[pltpu.VMEM((sum(counts), width), BF16)],
    )


def project_far(one, two, weights):
    eighth = one.shape[0] // 8
    return project(one, two, weights, (2,), (eighth, eighth))


def project_near(one, two, weights):
    quarter = one.shape[0] // 4
    return project(one, two, weights, (1, 3, 0), (quarter, quarter, quarter))


def back_grads_kernel(left_ref, one_ref, two_ref, out_ref):
    block = out_ref.shape[:-1]
    first = 0
    for right_ref in (one_ref, two_ref):
        width = right_ref.shape[1]
        values = tn(left_ref[...], right_ref[...]).astype(BF16)
        out_ref[..., first : first + width] = values.reshape(*block, width)
        first += width


def in_grads_kernel(left_ref, one_ref, two_ref, norm_ref, weight_ref, bias_ref, out_ref, sums_ref):
    block = out_ref.shape[:-1]
    first = 0
    rows = []
    for number, right_ref in enumerate((one_ref, two_ref)):
        gain_sum = shift_sum = jnp.zeros((left_ref.shape[1], 128), F32)
        for part in range(0, right_ref.shape[1], PART):
            at = slice(first + part, first + part + PART)
            raw = tn(left_ref[...], right_ref[:, part : part + PART])
            wide = weight_ref[:, at].astype(F32)
            gain_part, shift_part = wide * raw, wide * bias_ref[:, at]
            gain_sum = gain_sum + gain_part[:, :128] + gain_part[:, 128:]
            shift_sum = shift_sum + shift_part[:, :128] + shift_part[:, 128:]
            out_ref[..., at] = raw.astype(BF16).reshape(*block, PART)
        gain = norm_ref[2 * number : 2 * number + 1, :]
        rows += [jnp.sum(part.T, axis=0, keepdims=True) / gain for part in (gain_sum, shift_sum)]
        first += right_ref.shape[1]
    sums_ref[...] = jnp.concatenate([*rows, jnp.zeros((4, left_ref.shape[1]), F32)], 0)


def weight_grads(left, one, two, extra=None):
    rows, features = left.shape
    count = features // 16
    step = 4 * count
    width = one.shape[1] + two.shape[1]
    args = [left, one, two]
    in_specs = [pl.BlockSpec((rows, step), lambda i: (0, i)), whole_spec(one), whole_spec(two)]
    outs = [jax.ShapeDtypeStruct((4, 2, 2, count, width), BF16)]
    out_specs = [pl.BlockSpec((2, 2, 1, count, width), lambda i: (i % 2, 0, i // 2, 0, 0))]
    kernel = back_grads_kernel
    if extra is not None:
        kernel = in_grads_kernel
        vectors, weights, bias = extra
        args += [vectors, weights, bias]
        in_specs += [
            pl.BlockSpec((vectors.shape[0], step), lambda i: (0, i)),
            pl.BlockSpec((step, width), lambda i: (i, 0)),
            whole_spec(bias),
        ]
        outs.append(shape(8, features, F32))
        out_specs.append(pl.BlockSpec((8, step), lambda i: (0, i)))
    return grid_call(kernel, features // step, outs, out_specs, args, in_specs)


def gelu_pair(hidden):
    normal = 0.5 * (1.0 + lax.erf(hidden * (1.0 / math.sqrt(2.0))))
    density = jnp.exp(-0.5 * hidden * hidden) * (1.0 / math.sqrt(2.0 * math.pi))
    return (hidden * normal, normal + hidden * density)


def forward_kernel(split, normal_ref, weight_ref, extra_ref, cos_ref, sin_ref, doc_col_ref, doc_row_ref, qkv_ref, att_ref, log_ref, active_ref, slope_ref, bias_ref, mix_ref):
    count = extra_ref.shape[1]
    step = pl.program_id(0)

    @pl.when(step == 0)
    def _():
        total = jnp.zeros((32, 128), F32)
        for place in range(extra_ref.shape[0] // count):
            total = total + extra_ref[place * count : place * count + 32, :].astype(F32)
        lines = 14
        for line in range(lines):
            both = total[line : line + 1] + total[lines + line : lines + line + 1]
            bias_ref[line // 2 : line // 2 + 1, 128 * (line % 2) : 128 * (line % 2 + 1)] = both

    bias = bias_ref[pl.ds(step, 1), :]

    @pl.when(step < split)
    def _():
        mix_ref[step] = nn(normal_ref[...], weight_ref[...]) + bias

    @pl.when(step == split)
    def _():
        attend(mix_ref, cos_ref, sin_ref, doc_col_ref, doc_row_ref, qkv_ref, att_ref, log_ref)

    @pl.when(step >= split)
    def _():
        rows = normal_ref.shape[0]
        for start in range(0, rows, 256):
            at = slice(start, start + 256)
            active, slope = gelu_pair(nn(normal_ref[at, :], weight_ref[...]) + bias)
            active_ref[at, :] = active.astype(BF16)
            slope_ref[at, :] = slope.astype(BF16)


def forward(normal, weights, qkv_cols, up_cols, tables):
    rows, features = normal.shape
    split, steps = qkv_cols // PART, (qkv_cols + up_cols) // PART
    early = [shape(rows, qkv_cols, BF16), shape(rows, HS, BF16), shape(rows, 1, F32)]
    late = columns_spec(rows, -split, steps - split - 1)
    extra_place = weights.shape[1] // 128 - 1
    return grid_call(
        functools.partial(forward_kernel, split),
        steps,
        early + [shape(rows, up_cols, BF16)] * 2,
        [whole_spec(out) for out in early] + [late, late],
        (normal, weights, weights, *tables),
        [
            whole_spec(normal),
            columns_spec(features),
            pl.BlockSpec((features, 128), lambda i: (0, extra_place)),
            *[whole_spec(table) for table in tables],
        ],
        scratch=[pltpu.VMEM((8, PART), F32), pltpu.VMEM((split, rows, PART), F32)],
    )


def backward_kernel(split, cot_ref, weight_ref, slope_ref, att_ref, hid_ref, sum_ref):
    def product():
        half = cot_ref.shape[1] // 2
        parts = [weight_ref[:, xh].reshape(half, -1) for xh in range(2)]
        return nn(cot_ref[:, :half], parts[0]) + nn(cot_ref[:, half:], parts[1])

    @pl.when(pl.program_id(0) < split)
    def _():
        att_ref[...] = product().astype(BF16)

    @pl.when(pl.program_id(0) >= split)
    def _():
        value = (product() * slope_ref[...].astype(F32)).astype(BF16)
        hid_ref[...] = value
        sum_ref[...] = jnp.sum(value.astype(F32), axis=0, keepdims=True)


def backward(cot, weights, slope, dense_cols, down_cols):
    rows, features = cot.shape
    split, steps = dense_cols // PART, (dense_cols + down_cols) // PART
    outs = [shape(rows, dense_cols, BF16), shape(rows, down_cols, BF16), shape(1, down_cols, F32)]
    return grid_call(
        functools.partial(backward_kernel, split),
        steps,
        outs,
        [
            columns_spec(rows, 0, split - 1),
            columns_spec(rows, -split, steps - split - 1),
            columns_spec(1, -split, steps - split - 1),
        ],
        (cot, weights, slope),
        [
            whole_spec(cot),
            pl.BlockSpec((*weights.shape[:3], PART), lambda i: (0, 0, 0, i)),
            columns_spec(rows, -split, steps - split - 1),
        ],
    )


def finish_back_kernel(kept_ref, got_ref, dense_ref, down_ref):
    total = kept_ref[...].astype(F32) + got_ref[...].astype(F32)
    first = dense_ref.shape[0]
    dense_ref[...] = total[:, :first].T
    down_ref[...] = total[:, first:].T


def finish_in_kernel(row_ref, kept_ref, got_ref, norm_ref, bias_ref, qkv_ref, up_ref):
    total = kept_ref[...].astype(F32) + got_ref[...].astype(F32)

    def column(which):
        return own_column(row_ref, norm_ref, which, total.shape[0])

    first = 0
    for number, out_ref in enumerate((qkv_ref, up_ref)):
        at = slice(first, first + out_ref.shape[1])
        out_ref[...] = total[:, at] * column(2 * number) + column(2 * number + 1) * bias_ref[:, at]
        first += out_ref.shape[1]


def input_grad_kernel(tok_ref, cot_ref, kept_ref, got_ref, out_ref):
    tok_rows = tok_ref[...].astype(F32)
    center = jnp.mean(tok_rows, axis=-1, keepdims=True)
    centered = tok_rows - center
    variance = jnp.mean(centered * centered, axis=-1, keepdims=True)
    inverse = lax.rsqrt(variance + 1e-05)
    normal = centered * inverse
    u_rows = kept_ref[...] + got_ref[...].astype(F32)
    u_mean = jnp.mean(u_rows, axis=-1, keepdims=True)
    un_mean = jnp.mean(u_rows * normal, axis=-1, keepdims=True)
    d_rows = (u_rows - u_mean - normal * un_mean) * inverse
    out_ref[...] = (cot_ref[...].astype(F32) + d_rows).astype(BF16)


def own_column(row_ref, norm_ref, which, count):
    start = pl.multiple_of(row_ref[0] * count, count)
    square = (count, count)
    diagonal = lax.broadcasted_iota(jnp.int32, square, 0) == lax.broadcasted_iota(jnp.int32, square, 1)
    lanes = norm_ref[which : which + 1, pl.ds(start, count)].astype(F32)
    return jnp.sum(jnp.where(diagonal, jnp.broadcast_to(lanes, square), 0.0), axis=1, keepdims=True)


def prepare_kernel(row_ref, tok_ref, norm_ref, qkv_ref, up_ref, dense_ref, down_ref, qkv_bias_ref, up_bias_ref, normal_ref, out_ref, back_ref):
    tok_rows = tok_ref[...].astype(F32)
    center = jnp.mean(tok_rows, axis=-1, keepdims=True)
    centered = tok_rows - center
    variance = jnp.mean(centered * centered, axis=-1, keepdims=True)
    normal_ref[...] = (centered * lax.rsqrt(variance + 1e-05)).astype(BF16)
    count = qkv_ref.shape[0]

    def placed(bias_ref, width):
        own = bias_ref[...].astype(F32)
        rest = jnp.zeros((1, width - own.shape[1]), F32)
        wide = jnp.broadcast_to(jnp.concatenate([own, rest], 1), (8, width))
        return pltpu.roll(wide, row_ref[0] * own.shape[1], 1)[:1]

    lines = []
    first = 0
    for number, weight, bias in ((0, qkv_ref, qkv_bias_ref), (2, up_ref, up_bias_ref)):
        width = weight.shape[1]
        wide = weight[...].astype(F32)
        out_ref[:, first : first + width] = (wide * own_column(row_ref, norm_ref, number, count)).astype(BF16)
        shifted = jnp.sum(wide * own_column(row_ref, norm_ref, number + 1, count), axis=0, keepdims=True)
        shifted = shifted + placed(bias, width)
        lines += [shifted[:, 128 * i : 128 * (i + 1)] for i in range(width // 128)]
        first += width
    first_back = 0
    for weight in (dense_ref, down_ref):
        width = weight.shape[0]
        back_ref[:, first_back : first_back + width] = weight[...].astype(F32).T.astype(BF16)
        first_back += width
    high = [line.astype(BF16).astype(F32) for line in lines]
    low = [line - part for line, part in zip(lines, high)]
    rest = jnp.zeros((count - 2 * len(lines), 128), F32)
    out_ref[:, first:] = jnp.concatenate([*high, *low, rest], 0).astype(BF16)


def vmem_call(kernel, outs, args, scratch=(), scalars=0, limit=40):
    spec = pl.BlockSpec()
    scalar = pl.BlockSpec(memory_space=pltpu.SMEM)
    return pl.pallas_call(
        kernel,
        out_shape=outs,
        in_specs=[scalar] * scalars + [spec] * (len(args) - scalars),
        out_specs=[spec] * len(outs),
        scratch_shapes=scratch,
        compiler_params=pltpu.CompilerParams(vmem_limit_bytes=limit * 1024 * 1024),
        cost_estimate=light(),
    )(*args)


def shape(rows, columns, dtype):
    return jax.ShapeDtypeStruct((rows, columns), dtype)


def attend_back(qkv, grad, logs, cosine, sine, doc_col, doc_row):
    rows = qkv.shape[0]
    outs = (shape(rows, 3 * HS, BF16), shape(1, 3 * HS, F32))
    return vmem_call(
        attend_back_kernel,
        outs,
        (qkv, grad, logs, cosine, sine, doc_col, doc_row),
        scratch=[pltpu.VMEM((rows, HS), F32), pltpu.VMEM((rows, HS), F32)],
    )


def doc_layout(lengths, places):
    first, second = lengths[0], lengths[0] + lengths[1]
    third = second + lengths[2]
    passed = [(places >= end).astype(jnp.int32) for end in (first, second, third)]
    doc_ids = passed[0] + passed[1] + passed[2]
    begins = passed[0] * lengths[0] + passed[1] * lengths[1] + passed[2] * lengths[2]
    return (doc_ids, places - begins)


def rotary_tables(positions):
    half = ROT // 2
    lane = jnp.arange(128, dtype=jnp.int32)
    frequency = 1.0 / 10000.0 ** ((lane % half).astype(F32) * (2.0 / ROT))
    frequency = jnp.where(lane < ROT, frequency, 0.0)
    angles = positions.astype(F32) * frequency[None, :]
    sign = jnp.where(lane < half, -1.0, 1.0)
    return (jnp.cos(angles), jnp.sin(angles) * sign[None, :])


def shards(
    tokens,
    doc_lengths,
    input_gain,
    input_shift,
    post_gain,
    post_shift,
    qkv_weight,
    qkv_bias,
    dense_weight,
    dense_bias,
    up_weight,
    up_bias,
    down_weight,
    down_bias,
    cotangent,
):
    row_index = (lax.axis_index("xh") * 4 + lax.axis_index("y")) * 2 + lax.axis_index("c")
    slice_rows = qkv_weight.shape[0]
    qkv_cols, up_cols = qkv_weight.shape[1], up_weight.shape[1]

    tok_count, width = tokens.shape
    vectors = jnp.concatenate([input_gain, input_shift, post_gain, post_shift]).astype(F32).reshape(4, width)
    back_cols = (dense_weight.shape[0], down_weight.shape[0])
    own_normal, block, block_back = vmem_call(
        prepare_kernel,
        (
            shape(tok_count, width, BF16),
            shape(slice_rows, qkv_cols + up_cols + 128, BF16),
            shape(slice_rows, sum(back_cols), BF16),
        ),
        (
            row_index.astype(jnp.int32)[None],
            tokens,
            vectors,
            qkv_weight,
            up_weight,
            dense_weight,
            down_weight,
            qkv_bias[None],
            up_bias[None],
        ),
        scalars=1,
        limit=60,
    )
    weights = lax.all_gather(block, ROW, axis=0, tiled=True)
    in_cols = qkv_cols + up_cols

    row_count = 8 * tok_count
    doc_col, positions = doc_layout(doc_lengths[0], jnp.arange(row_count, dtype=jnp.int32)[:, None])
    doc_row, _ = doc_layout(doc_lengths[0], jnp.arange(row_count, dtype=jnp.int32)[None, :])
    tables = (*rotary_tables(positions), doc_col, doc_row)

    cot_near = ring_near(cotangent, "z")
    normal_other = hop(own_normal, xl=1)
    normal_pair, cot_own, back_own, *tables = all_after(
        [jnp.stack([own_normal, normal_other]), cotangent, block_back, *tables], cot_near
    )
    normal_near = ring_near(normal_pair, "z")
    cot_other = hop(cot_own, xl=1)
    back_other = hop(back_own, xh=1)
    held = all_after([*normal_near, cot_other, back_other], [])
    normal_far = ring_far(held[:2], "z")
    cot_other_near = ring_near(held[2], "z")
    xh = lax.axis_index("xh")
    back_pair = [jnp.where(xh == first, block_back, held[3]) for first in range(2)]
    back_weights = gather_row_near(jnp.stack(back_pair))
    order = [(at, pair) for at in ("at", "back", "ahead", "far") for pair in ("own", "other")]
    normal_all = rows_of_group([normal_pair, *normal_near, *normal_far], order)
    held = all_after([cot_near[0], cot_other_near[1]], [normal_all])
    cot_far = [hop(held[0], z=1), hop(held[1], z=3)]

    qkv, attended, logs, active, slope = forward(normal_all, weights, qkv_cols, up_cols, tables)
    qkv, *cot_far = all_after([qkv, *cot_far], [])
    cot_parts = [
        cotangent,
        cot_other,
        cot_near[0],
        cot_other_near[0],
        cot_near[1],
        cot_other_near[1],
        *cot_far,
    ]
    cot_all = rows_of_group(cot_parts, order)
    (back_grads,) = weight_grads(cot_all, attended, active)
    back_pair = scatter_row_near(back_grads)
    attended, active = all_after([attended, active], [back_grads])
    out_far = project_far(attended, active, back_weights)
    out_first = scatter_col_first(out_far)
    attended, active = all_after([attended, active], [out_far[0]])
    out_near = project_near(attended, active, back_weights)

    cot_all = after(cot_all, out_near[0])
    d_attended, d_hidden, up_bias_part = backward(cot_all, back_weights, slope, *back_cols)
    d_attended, d_hidden, *out_first = all_after([d_attended, d_hidden, *out_first], [])
    out_second = scatter_col_second(out_near, out_first)
    d_mixture, qkv_bias_part = attend_back(qkv, d_attended, logs, *tables)
    biases = jnp.concatenate([qkv_bias_part, up_bias_part], 1)
    in_grads, sums = weight_grads(normal_all, d_mixture, d_hidden, (vectors, weights, biases))
    in_grads, sums, d_mixture, d_hidden, *out_second = all_after(
        [in_grads, sums, d_mixture, d_hidden, *out_second], []
    )
    in_pair = scatter_row_near(in_grads)

    cot_sum = jnp.sum(cotangent.astype(F32), axis=0, keepdims=True)
    biases = jnp.pad(biases, ((0, 0), (0, width - biases.shape[1])))
    line = jnp.arange(8)[:, None]
    packed = jnp.where(line == 4, cot_sum, jnp.where(line == 5, biases, sums))
    packed = packed + hop(packed, c=1)
    packed, d_mixture, d_hidden, back_pair = all_after([packed, d_mixture, d_hidden, back_pair], [])
    packed = packed + hop(packed, xh=1)
    back_kept, back_got = scatter_row_far(back_pair)
    u_far = project_far(d_mixture, d_hidden, weights)
    packed, d_mixture, d_hidden, *u_far = all_after([packed, d_mixture, d_hidden, *u_far], [])
    u_first = scatter_col_first(u_far)
    packed = packed + jnp.where(line == 5, 0.0, hop(packed, xl=1))
    u_near = project_near(d_mixture, d_hidden, weights)
    packed, back_got, *held = all_after([packed, back_got, *out_second, *u_near, *u_first], [])
    out_second, u_near, u_first = held[:2], held[2:5], held[5:]
    u_second = scatter_col_second(u_near, u_first)
    out_kept, out_got = scatter_col_third(out_near, out_second)
    packed = packed + swap(packed, "y")
    packed = packed + hop(packed, y=2)
    bias_total = packed[5:6]
    qkv_bias_total = lax.dynamic_slice_in_dim(
        packed[5], row_index * qkv_bias.shape[0], qkv_bias.shape[0], 0
    )
    up_bias_total = lax.dynamic_slice_in_dim(
        packed[5], qkv_cols + row_index * up_bias.shape[0], up_bias.shape[0], 0
    )
    in_kept, in_got = scatter_row_far(after(in_pair, packed))
    packed, in_got, out_got, *u_second = all_after([packed, in_got, out_got, *u_second], [])
    u_kept, u_got = scatter_col_third(u_near, u_second)
    packed = packed + swap(packed, "z")
    packed = packed + hop(packed, z=2)

    def flat(kept, got):
        return (kept.reshape(slice_rows, -1), got.reshape(slice_rows, -1))

    dense_total, down_total = vmem_call(
        finish_back_kernel,
        tuple(shape(cols, slice_rows, F32) for cols in back_cols),
        flat(back_kept, back_got),
    )
    layer_out = (
        tokens.astype(F32)
        + (out_kept + out_got.astype(F32))
        + dense_bias.astype(F32)
        + down_bias.astype(F32)
    ).astype(BF16)
    qkv_total, up_total = vmem_call(
        finish_in_kernel,
        tuple(shape(slice_rows, cols, F32) for cols in (qkv_cols, up_cols)),
        (row_index.astype(jnp.int32)[None], *flat(in_kept, in_got), vectors, bias_total),
        scalars=1,
    )
    (input_grad,) = vmem_call(
        input_grad_kernel,
        (shape(tok_count, width, BF16),),
        (tokens, cotangent, u_kept, u_got),
    )

    return (
        layer_out,
        input_grad,
        packed[0],
        packed[1],
        packed[2],
        packed[3],
        qkv_total,
        qkv_bias_total,
        dense_total,
        packed[4],
        up_total,
        up_bias_total,
        down_total,
        packed[4],
    )


def solution(mesh):
    fine = Mesh(mesh.devices.reshape(tuple(SIZES.values())), NAMES)
    everywhere = P(ROW + COL, None)
    return jax.shard_map(
        shards,
        mesh=fine,
        in_specs=(
            everywhere,
            P(ROW, None),
            P(),
            P(),
            P(),
            P(),
            P(ROW, COL),
            P(COL + ROW),
            P(COL, ROW),
            P(),
            P(ROW, COL),
            P(COL + ROW),
            P(COL, ROW),
            P(),
            everywhere,
        ),
        out_specs=(
            everywhere,
            everywhere,
            P(),
            P(),
            P(),
            P(),
            P(ROW, COL),
            P(COL + ROW),
            P(COL, ROW),
            P(),
            P(ROW, COL),
            P(COL + ROW),
            P(COL, ROW),
            P(),
        ),
        check_vma=False,
    )
```

```python
import functools
import itertools
import math

import jax
import jax.numpy as jnp
from jax import lax
from jax.experimental import pallas as pl
from jax.experimental.pallas import tpu as pltpu
from jax.sharding import Mesh
from jax.sharding import PartitionSpec as P

HS = 256
ROT = 64
BLOCK = 256
SIZES = {"xh": 2, "y": 4, "c": 2, "z": 4, "xl": 2}
NAMES = tuple(SIZES)
ROW = ("xh", "y", "c")
COL = ("z", "xl")
F32 = jnp.float32
BF16 = jnp.bfloat16


def light():
    return pl.CostEstimate(flops=1, bytes_accessed=1, transcendentals=0)


def hop(value, **deltas):
    return send(value, tuple(deltas), lambda coords: [c + deltas[name] for name, c in coords.items()])


def swap(value, axis):
    return send(value, (axis,), lambda coords: [coords[axis] ^ 1])


def send(value, names, target):
    axes = tuple(name for name in NAMES if name in names)

    def flat(coords):
        index = 0
        for name, place in zip(axes, coords):
            index = index * SIZES[name] + place % SIZES[name]
        return index

    pairs = []
    for coords in itertools.product(*[range(SIZES[name]) for name in axes]):
        pairs.append((flat(coords), flat(target(dict(zip(axes, coords))))))
    return lax.ppermute(value, axes if len(axes) > 1 else axes[0], pairs)


def rows_at(value, start, count):
    return lax.dynamic_slice_in_dim(value, start, count, 0)


def after(value, *others):
    return lax.optimization_barrier((value, *others))[0]


def all_after(values, others):
    return list(lax.optimization_barrier((*values, *others))[: len(values)])


def ring_near(pair, axis):
    return [hop(pair, **{axis: 1}), hop(pair, **{axis: 3})]


def places(axis, pair):
    at, own = lax.axis_index(axis), lax.axis_index(pair)
    return {
        "at": at,
        "back": (at + 3) % 4,
        "ahead": (at + 1) % 4,
        "far": (at + 2) % 4,
        "own": own,
        "other": 1 - own,
    }


def group_kernel(count, places_ref, *refs):
    *sources, out_ref = refs
    for number, source in enumerate(sources):
        start = pl.multiple_of(places_ref[number] * count, count)
        out_ref[pl.ds(start, count), :] = source[...]


def rows_of_group(blocks):
    count, width = blocks["at", "own"].shape
    at = places("z", "xl")
    index = jnp.stack([at[place] * 2 + at[pair] for place, pair in blocks]).astype(jnp.int32)
    outs = (shape(8 * count, width, BF16),)
    kernel = functools.partial(group_kernel, count)
    (whole,) = vmem_call(kernel, outs, (index, *blocks.values()), scalars=1, limit=60)
    return whole


def gather_row_near(pair):
    return lax.all_gather(pair, ("y", "c"), axis=0)


def scatter_col_first(far):
    return [hop(far[0], z=1), hop(far[1], z=3)]


def scatter_col_second(near, first):
    low, high = first
    up, down = near[:2]
    count = low.shape[0]
    up = jnp.concatenate([up[:count] + low, up[count:]], 0)
    down = jnp.concatenate([down[:count], down[count:] + high], 0)
    return [hop(up, z=1), hop(down, z=3)]


def scatter_col_early(near):
    return [hop(near[1], z=1), hop(near[2], z=3)]


def scatter_col_late(near, first):
    return [hop(near[0] + first[0], z=1), hop(near[3] + first[1], z=3)]


def scatter_col_third(own, parts):
    mine = lax.axis_index("xl") == 0
    count = own.shape[0] // 2
    halves = [
        sum(part.astype(F32) for part in (own[place * count : (place + 1) * count], *got))
        for place, got in enumerate(parts)
    ]
    kept, sent = jnp.where(mine, halves[0], halves[1]), jnp.where(mine, halves[1], halves[0])
    return kept, hop(sent.astype(BF16), xl=1)


def scatter_row_near(blocks):
    return lax.psum_scatter(blocks.reshape(8, *blocks.shape[2:]), ("y", "c"), scatter_dimension=0)


def scatter_row_far(pair):
    xh = lax.axis_index("xh")
    kept = lax.dynamic_index_in_dim(pair, xh, 0, keepdims=False)
    sent = lax.dynamic_index_in_dim(pair, 1 - xh, 0, keepdims=False)
    return kept, hop(sent, xh=1)


def nt(left, right):
    return lax.dot_general(left, right, (((1,), (1,)), ((), ())), preferred_element_type=F32)


def tn(left, right):
    return lax.dot_general(left, right, (((0,), (0,)), ((), ())), preferred_element_type=F32)


def nn(left, right):
    return jnp.dot(left, right, preferred_element_type=F32)


def turn(part, cosine, sine):
    lane = lax.broadcasted_iota(jnp.int32, part.shape, 1)
    ahead = pltpu.roll(part, 128 - ROT // 2, 1)
    behind = pltpu.roll(part, ROT // 2, 1)
    return part * cosine + jnp.where(lane < ROT // 2, ahead, behind) * sine


def block_allowed(doc_col, doc_row, start, width):
    docs = doc_col[start : start + BLOCK] == doc_row[:, :width]
    row = start + lax.broadcasted_iota(jnp.int32, (BLOCK, width), 0)
    column = lax.broadcasted_iota(jnp.int32, (BLOCK, width), 1)
    return docs & (column <= row)


def attend(mix_ref, cos_ref, sin_ref, doc_col_ref, doc_row_ref, qkv_ref, out_ref, log_ref):
    rows = mix_ref.shape[1]
    for start in range(0, rows, BLOCK):
        at = pl.ds(start, BLOCK)
        cosine, sine = cos_ref[at, :], sin_ref[at, :]
        for part in range(2):
            first = part * HS
            qkv_ref[at, first : first + 128] = turn(mix_ref[part, at, :128], cosine, sine).astype(BF16)
            qkv_ref[at, first + 128 : first + HS] = mix_ref[part, at, 128:].astype(BF16)
        qkv_ref[at, 2 * HS :] = mix_ref[2, at, :].astype(BF16)
    doc_row = doc_row_ref[...]
    doc_col = doc_col_ref[...]
    for start in range(0, rows, BLOCK):
        width = start + BLOCK
        at = pl.ds(start, BLOCK)
        scores = nt(qkv_ref[at, :HS], qkv_ref[:width, HS : 2 * HS]) * HS ** (-0.5)
        scores = jnp.where(block_allowed(doc_col, doc_row, start, width), scores, -1e30)
        top = jnp.max(scores, axis=1, keepdims=True)
        raised = jnp.exp(scores - top)
        total = jnp.sum(raised, axis=1, keepdims=True)
        probabilities = (raised * (1.0 / total)).astype(BF16)
        out_ref[at, :] = nn(probabilities, qkv_ref[:width, 2 * HS :]).astype(BF16)
        log_ref[at, :] = top + jnp.log(total)


def attend_back_kernel(qkv_ref, grad_ref, log_ref, cos_ref, sin_ref, doc_col_ref, doc_row_ref, out_ref, sum_ref, dk_ref, dv_ref):
    rows = qkv_ref.shape[0]
    scaling = HS ** (-0.5)
    doc_row = doc_row_ref[...]
    doc_col = doc_col_ref[...]
    sums = [jnp.zeros((1, HS), F32) for _ in range(3)]

    def finish(value, start, first):
        at = pl.ds(start, BLOCK)
        head = turn(value[:, :128], cos_ref[at, :], -sin_ref[at, :]).astype(BF16)
        rest = value[:, 128:].astype(BF16)
        out_ref[at, first : first + 128] = head
        out_ref[at, first + 128 : first + HS] = rest
        both = jnp.concatenate([head.astype(F32), rest.astype(F32)], 1)
        return jnp.sum(both, axis=0, keepdims=True)

    for start in range(0, rows, BLOCK):
        width = start + BLOCK
        at = pl.ds(start, BLOCK)
        query = qkv_ref[at, :HS]
        grad = grad_ref[at, :]
        scores = nt(query, qkv_ref[:width, HS : 2 * HS]) * scaling
        allowed = block_allowed(doc_col, doc_row, start, width)
        weights = jnp.where(allowed, jnp.exp(scores - log_ref[at, :]), 0.0)
        probabilities = weights.astype(BF16)
        d_probs = nt(grad, qkv_ref[:width, 2 * HS :])
        inner = jnp.sum(weights * d_probs, axis=1, keepdims=True)
        d_scores = (weights * (d_probs - inner)).astype(BF16)
        d_values = tn(probabilities, grad)
        d_keys = tn(d_scores, query) * scaling
        if start:
            dv_ref[:start, :] += d_values[:start]
            dk_ref[:start, :] += d_keys[:start]
        dv_ref[start:width, :] = d_values[start:]
        dk_ref[start:width, :] = d_keys[start:]
        d_query = nn(d_scores, qkv_ref[:width, HS : 2 * HS]) * scaling
        sums[0] = sums[0] + finish(d_query, start, 0)
    for start in range(0, rows, BLOCK):
        at = pl.ds(start, BLOCK)
        sums[1] = sums[1] + finish(dk_ref[at, :], start, HS)
        values = dv_ref[at, :].astype(BF16)
        out_ref[at, 2 * HS :] = values
        sums[2] = sums[2] + jnp.sum(values.astype(F32), axis=0, keepdims=True)
    for part in range(3):
        sum_ref[:, part * HS : (part + 1) * HS] = sums[part]


PART = 256


def whole_spec(array):
    return pl.BlockSpec(array.shape, lambda i: (0,) * array.ndim)


def columns_spec(rows, first=0, last=None):
    if last is None:
        return pl.BlockSpec((rows, PART), lambda i: (0, i + first))
    return pl.BlockSpec((rows, PART), lambda i: (0, jnp.clip(i + first, 0, last)))


def grid_call(kernel, steps, outs, out_specs, args, in_specs, scratch=()):
    return pl.pallas_call(
        kernel,
        grid=(steps,),
        out_shape=tuple(outs),
        in_specs=in_specs,
        out_specs=tuple(out_specs),
        scratch_shapes=scratch,
        compiler_params=pltpu.CompilerParams(vmem_limit_bytes=48 * 1024 * 1024),
        cost_estimate=light(),
    )(*args)


def quarter_spec(weights, width):
    block = (weights.shape[0] // 2, 1, weights.shape[2], width)
    return pl.BlockSpec(block, lambda i: (i % 2, i // 2, 0, 0))


def project_kernel(steps, z_ref, one_ref, two_ref, weight_ref, *refs):
    *out_refs, both_ref = refs
    part = one_ref.shape[0] // 4

    @pl.when(pl.program_id(0) == 0)
    def _():
        for number, step in enumerate(steps):
            rows = pl.ds(pl.multiple_of((z_ref[0] + step) % 4 * part, part), part)
            at = slice(number * part, (number + 1) * part)
            both_ref[at, : one_ref.shape[1]] = one_ref[rows, :]
            both_ref[at, one_ref.shape[1] :] = two_ref[rows, :]

    block = weight_ref[...].reshape(-1, weight_ref.shape[-1])
    total = nt(both_ref[...], block).astype(BF16)
    first = 0
    for out_ref in out_refs:
        out_ref[...] = total[first : first + out_ref.shape[0]]
        first += out_ref.shape[0]


def project(one, two, weights, steps, counts):
    width = one.shape[1] + two.shape[1]
    features = math.prod(weights.shape[:3])
    step = features // 4
    weight_spec = quarter_spec(weights, width)
    z = lax.axis_index("z").astype(jnp.int32)[None]
    return grid_call(
        functools.partial(project_kernel, steps),
        4,
        [shape(count, features, BF16) for count in counts],
        [pl.BlockSpec((count, step), lambda i: (0, i)) for count in counts],
        (z, one, two, weights),
        [pl.BlockSpec(memory_space=pltpu.SMEM), whole_spec(one), whole_spec(two), weight_spec],
        scratch=[pltpu.VMEM((sum(counts), width), BF16)],
    )


def project_far(one, two, weights):
    eighth = one.shape[0] // 8
    return project(one, two, weights, (2,), (eighth, eighth))


def project_near(one, two, weights):
    quarter = one.shape[0] // 4
    return project(one, two, weights, (1, 3, 0), (quarter, quarter, quarter))


def project_near_halves(one, two, weights):
    eighth = one.shape[0] // 8
    return project(one, two, weights, (1, 3, 0), (eighth,) * 4 + (2 * eighth,))


def back_grads_kernel(left_ref, one_ref, two_ref, out_ref):
    block = out_ref.shape[:-1]
    first = 0
    for right_ref in (one_ref, two_ref):
        width = right_ref.shape[1]
        values = tn(left_ref[...], right_ref[...]).astype(BF16)
        out_ref[..., first : first + width] = values.reshape(*block, width)
        first += width


def in_grads_kernel(left_ref, one_ref, two_ref, norm_ref, weight_ref, bias_ref, out_ref, sums_ref):
    block = out_ref.shape[:-1]
    first = 0
    rows = []
    for number, right_ref in enumerate((one_ref, two_ref)):
        gain_sum = shift_sum = jnp.zeros((left_ref.shape[1], 128), F32)
        for part in range(0, right_ref.shape[1], PART):
            at = slice(first + part, first + part + PART)
            raw = tn(left_ref[...], right_ref[:, part : part + PART])
            wide = weight_ref[..., at].astype(F32).reshape(raw.shape)
            gain_part, shift_part = wide * raw, wide * bias_ref[:, at]
            gain_sum = gain_sum + gain_part[:, :128] + gain_part[:, 128:]
            shift_sum = shift_sum + shift_part[:, :128] + shift_part[:, 128:]
            out_ref[..., at] = raw.astype(BF16).reshape(*block, PART)
        gain = norm_ref[2 * number : 2 * number + 1, :]
        rows += [jnp.sum(part.T, axis=0, keepdims=True) / gain for part in (gain_sum, shift_sum)]
        first += right_ref.shape[1]
    sums_ref[...] = jnp.concatenate([*rows, jnp.zeros((4, left_ref.shape[1]), F32)], 0)


def weight_grads(left, one, two, extra=None):
    rows, features = left.shape
    count = features // 16
    step = 4 * count
    width = one.shape[1] + two.shape[1]
    args = [left, one, two]
    in_specs = [pl.BlockSpec((rows, step), lambda i: (0, i)), whole_spec(one), whole_spec(two)]
    outs = [jax.ShapeDtypeStruct((4, 2, 2, count, width), BF16)]
    out_specs = [pl.BlockSpec((2, 2, 1, count, width), lambda i: (i % 2, 0, i // 2, 0, 0))]
    kernel = back_grads_kernel
    if extra is not None:
        kernel = in_grads_kernel
        vectors, weights, bias = extra
        args += [vectors, weights, bias]
        in_specs += [
            pl.BlockSpec((vectors.shape[0], step), lambda i: (0, i)),
            quarter_spec(weights, width),
            whole_spec(bias),
        ]
        outs.append(shape(8, features, F32))
        out_specs.append(pl.BlockSpec((8, step), lambda i: (0, i)))
    return grid_call(kernel, features // step, outs, out_specs, args, in_specs)


def gelu_pair(hidden):
    normal = 0.5 * (1.0 + lax.erf(hidden * (1.0 / math.sqrt(2.0))))
    density = jnp.exp(-0.5 * hidden * hidden) * (1.0 / math.sqrt(2.0 * math.pi))
    return (hidden * normal, normal + hidden * density)


def natural(ref):
    return jnp.concatenate([ref[:, xh].reshape(-1, ref.shape[-1]) for xh in range(2)], 0)


def forward_kernel(split, normal_ref, weight_ref, extra_ref, cos_ref, sin_ref, doc_col_ref, doc_row_ref, qkv_ref, att_ref, log_ref, active_ref, slope_ref, bias_ref, mix_ref):
    step = pl.program_id(0)
    weight = natural(weight_ref)

    @pl.when(step == 0)
    def _():
        total = jnp.zeros((32, 128), F32)
        for place in range(extra_ref.shape[0]):
            for xh in range(2):
                total = total + extra_ref[place, xh, :32, :].astype(F32)
        lines = 14
        for line in range(lines):
            both = total[line : line + 1] + total[lines + line : lines + line + 1]
            bias_ref[line // 2 : line // 2 + 1, 128 * (line % 2) : 128 * (line % 2 + 1)] = both

    bias = bias_ref[pl.ds(step, 1), :]

    @pl.when(step < split)
    def _():
        mix_ref[step] = nn(normal_ref[...], weight) + bias

    @pl.when(step == split)
    def _():
        attend(mix_ref, cos_ref, sin_ref, doc_col_ref, doc_row_ref, qkv_ref, att_ref, log_ref)

    @pl.when(step >= split)
    def _():
        rows = normal_ref.shape[0]
        for start in range(0, rows, 256):
            at = slice(start, start + 256)
            active, slope = gelu_pair(nn(normal_ref[at, :], weight) + bias)
            active_ref[at, :] = active.astype(BF16)
            slope_ref[at, :] = slope.astype(BF16)


def forward(normal, weights, qkv_cols, up_cols, tables):
    rows, features = normal.shape
    split, steps = qkv_cols // PART, (qkv_cols + up_cols) // PART
    early = [shape(rows, qkv_cols, BF16), shape(rows, HS, BF16), shape(rows, 1, F32)]
    late = columns_spec(rows, -split, steps - split - 1)
    extra_place = weights.shape[-1] // 128 - 1
    return grid_call(
        functools.partial(forward_kernel, split),
        steps,
        early + [shape(rows, up_cols, BF16)] * 2,
        [whole_spec(out) for out in early] + [late, late],
        (normal, weights, weights, *tables),
        [
            whole_spec(normal),
            pl.BlockSpec((*weights.shape[:3], PART), lambda i: (0, 0, 0, i)),
            pl.BlockSpec((*weights.shape[:3], 128), lambda i: (0, 0, 0, extra_place)),
            *[whole_spec(table) for table in tables],
        ],
        scratch=[pltpu.VMEM((8, PART), F32), pltpu.VMEM((split, rows, PART), F32)],
    )


def backward_kernel(split, cot_ref, weight_ref, slope_ref, att_ref, hid_ref, sum_ref):
    def product():
        return nn(cot_ref[...], natural(weight_ref))

    @pl.when(pl.program_id(0) < split)
    def _():
        att_ref[...] = product().astype(BF16)

    @pl.when(pl.program_id(0) >= split)
    def _():
        value = (product() * slope_ref[...].astype(F32)).astype(BF16)
        hid_ref[...] = value
        sum_ref[...] = jnp.sum(value.astype(F32), axis=0, keepdims=True)


def backward(cot, weights, slope, dense_cols, down_cols):
    rows, features = cot.shape
    split, steps = dense_cols // PART, (dense_cols + down_cols) // PART
    outs = [shape(rows, dense_cols, BF16), shape(rows, down_cols, BF16), shape(1, down_cols, F32)]
    return grid_call(
        functools.partial(backward_kernel, split),
        steps,
        outs,
        [
            columns_spec(rows, 0, split - 1),
            columns_spec(rows, -split, steps - split - 1),
            columns_spec(1, -split, steps - split - 1),
        ],
        (cot, weights, slope),
        [
            whole_spec(cot),
            pl.BlockSpec((*weights.shape[:3], PART), lambda i: (0, 0, 0, i)),
            columns_spec(rows, -split, steps - split - 1),
        ],
    )


def finish_back_kernel(kept_ref, got_ref, dense_ref, down_ref):
    total = kept_ref[...].astype(F32) + got_ref[...].astype(F32)
    first = dense_ref.shape[0]
    dense_ref[...] = total[:, :first].T
    down_ref[...] = total[:, first:].T


def finish_in_kernel(row_ref, kept_ref, got_ref, norm_ref, bias_ref, qkv_ref, up_ref):
    total = kept_ref[...].astype(F32) + got_ref[...].astype(F32)

    def column(which):
        return own_column(row_ref, norm_ref, which, total.shape[0])

    first = 0
    for number, out_ref in enumerate((qkv_ref, up_ref)):
        at = slice(first, first + out_ref.shape[1])
        out_ref[...] = total[:, at] * column(2 * number) + column(2 * number + 1) * bias_ref[:, at]
        first += out_ref.shape[1]


def input_grad_kernel(tok_ref, cot_ref, kept_ref, got_ref, out_ref):
    tok_rows = tok_ref[...].astype(F32)
    center = jnp.mean(tok_rows, axis=-1, keepdims=True)
    centered = tok_rows - center
    variance = jnp.mean(centered * centered, axis=-1, keepdims=True)
    inverse = lax.rsqrt(variance + 1e-05)
    normal = centered * inverse
    u_rows = kept_ref[...] + got_ref[...].astype(F32)
    u_mean = jnp.mean(u_rows, axis=-1, keepdims=True)
    un_mean = jnp.mean(u_rows * normal, axis=-1, keepdims=True)
    d_rows = (u_rows - u_mean - normal * un_mean) * inverse
    out_ref[...] = (cot_ref[...].astype(F32) + d_rows).astype(BF16)


def own_column(row_ref, norm_ref, which, count):
    start = pl.multiple_of(row_ref[0] * count, count)
    square = (count, count)
    diagonal = lax.broadcasted_iota(jnp.int32, square, 0) == lax.broadcasted_iota(jnp.int32, square, 1)
    lanes = norm_ref[which : which + 1, pl.ds(start, count)].astype(F32)
    return jnp.sum(jnp.where(diagonal, jnp.broadcast_to(lanes, square), 0.0), axis=1, keepdims=True)


def prepare_kernel(row_ref, tok_ref, norm_ref, qkv_ref, up_ref, dense_ref, down_ref, qkv_bias_ref, up_bias_ref, normal_ref, out_ref, back_ref):
    tok_rows = tok_ref[...].astype(F32)
    center = jnp.mean(tok_rows, axis=-1, keepdims=True)
    centered = tok_rows - center
    variance = jnp.mean(centered * centered, axis=-1, keepdims=True)
    normal_ref[...] = (centered * lax.rsqrt(variance + 1e-05)).astype(BF16)
    count = qkv_ref.shape[0]

    def placed(bias_ref, width):
        own = bias_ref[...].astype(F32)
        rest = jnp.zeros((1, width - own.shape[1]), F32)
        wide = jnp.broadcast_to(jnp.concatenate([own, rest], 1), (8, width))
        return pltpu.roll(wide, row_ref[0] * own.shape[1], 1)[:1]

    lines = []
    first = 0
    for number, weight, bias in ((0, qkv_ref, qkv_bias_ref), (2, up_ref, up_bias_ref)):
        width = weight.shape[1]
        wide = weight[...].astype(F32)
        out_ref[:, first : first + width] = (wide * own_column(row_ref, norm_ref, number, count)).astype(BF16)
        shifted = jnp.sum(wide * own_column(row_ref, norm_ref, number + 1, count), axis=0, keepdims=True)
        shifted = shifted + placed(bias, width)
        lines += [shifted[:, 128 * i : 128 * (i + 1)] for i in range(width // 128)]
        first += width
    first_back = 0
    for weight in (dense_ref, down_ref):
        width = weight.shape[0]
        back_ref[:, first_back : first_back + width] = weight[...].astype(F32).T.astype(BF16)
        first_back += width
    high = [line.astype(BF16).astype(F32) for line in lines]
    low = [line - part for line, part in zip(lines, high)]
    rest = jnp.zeros((count - 2 * len(lines), 128), F32)
    out_ref[:, first:] = jnp.concatenate([*high, *low, rest], 0).astype(BF16)


def vmem_call(kernel, outs, args, scratch=(), scalars=0, limit=40):
    spec = pl.BlockSpec()
    scalar = pl.BlockSpec(memory_space=pltpu.SMEM)
    return pl.pallas_call(
        kernel,
        out_shape=outs,
        in_specs=[scalar] * scalars + [spec] * (len(args) - scalars),
        out_specs=[spec] * len(outs),
        scratch_shapes=scratch,
        compiler_params=pltpu.CompilerParams(vmem_limit_bytes=limit * 1024 * 1024),
        cost_estimate=light(),
    )(*args)


def shape(rows, columns, dtype):
    return jax.ShapeDtypeStruct((rows, columns), dtype)


def attend_back(qkv, grad, logs, cosine, sine, doc_col, doc_row):
    rows = qkv.shape[0]
    outs = (shape(rows, 3 * HS, BF16), shape(1, 3 * HS, F32))
    return vmem_call(
        attend_back_kernel,
        outs,
        (qkv, grad, logs, cosine, sine, doc_col, doc_row),
        scratch=[pltpu.VMEM((rows, HS), F32), pltpu.VMEM((rows, HS), F32)],
    )


def doc_layout(lengths, places):
    first, second = lengths[0], lengths[0] + lengths[1]
    third = second + lengths[2]
    passed = [(places >= end).astype(jnp.int32) for end in (first, second, third)]
    doc_ids = passed[0] + passed[1] + passed[2]
    begins = passed[0] * lengths[0] + passed[1] * lengths[1] + passed[2] * lengths[2]
    return (doc_ids, places - begins)


def rotary_tables(positions):
    half = ROT // 2
    lane = jnp.arange(128, dtype=jnp.int32)
    frequency = 1.0 / 10000.0 ** ((lane % half).astype(F32) * (2.0 / ROT))
    frequency = jnp.where(lane < ROT, frequency, 0.0)
    angles = positions.astype(F32) * frequency[None, :]
    sign = jnp.where(lane < half, -1.0, 1.0)
    return (jnp.cos(angles), jnp.sin(angles) * sign[None, :])


def shards(
    tokens,
    doc_lengths,
    input_gain,
    input_shift,
    post_gain,
    post_shift,
    qkv_weight,
    qkv_bias,
    dense_weight,
    dense_bias,
    up_weight,
    up_bias,
    down_weight,
    down_bias,
    cotangent,
):
    row_index = (lax.axis_index("xh") * 4 + lax.axis_index("y")) * 2 + lax.axis_index("c")
    slice_rows = qkv_weight.shape[0]
    qkv_cols, up_cols = qkv_weight.shape[1], up_weight.shape[1]

    tok_count, width = tokens.shape
    vectors = jnp.concatenate([input_gain, input_shift, post_gain, post_shift]).astype(F32).reshape(4, width)
    back_cols = (dense_weight.shape[0], down_weight.shape[0])
    own_normal, block, block_back = vmem_call(
        prepare_kernel,
        (
            shape(tok_count, width, BF16),
            shape(slice_rows, qkv_cols + up_cols + 128, BF16),
            shape(slice_rows, sum(back_cols), BF16),
        ),
        (
            row_index.astype(jnp.int32)[None],
            tokens,
            vectors,
            qkv_weight,
            up_weight,
            dense_weight,
            down_weight,
            qkv_bias[None],
            up_bias[None],
        ),
        scalars=1,
        limit=60,
    )
    xh = lax.axis_index("xh")

    def pair_of(own, other):
        return jnp.stack([jnp.where(xh == first, own, other) for first in range(2)])

    row_count = 8 * tok_count
    doc_col, positions = doc_layout(doc_lengths[0], jnp.arange(row_count, dtype=jnp.int32)[:, None])
    doc_row, _ = doc_layout(doc_lengths[0], jnp.arange(row_count, dtype=jnp.int32)[None, :])
    tables = (*rotary_tables(positions), doc_col, doc_row)

    normal = {("at", "own"): own_normal}
    cot = {("at", "own"): cotangent}
    block_other = hop(block, xh=1)
    normal["back", "own"], normal["ahead", "own"] = ring_near(own_normal, "z")
    block_own, block_other, near_back, own_normal, own_cot, own_back, *tables = all_after(
        [block, block_other, normal["back", "own"], own_normal, cotangent, block_back, *tables],
        [normal["ahead", "own"]],
    )
    weights = gather_row_near(pair_of(block_own, block_other))
    normal["at", "other"] = hop(own_normal, xl=1)
    normal["far", "own"] = hop(near_back, z=1)
    cot["ahead", "own"] = hop(own_cot, z=3)
    normal_other, own_cot, own_back = all_after(
        [normal["at", "other"], own_cot, own_back], [normal["far", "own"], cot["ahead", "own"]]
    )
    normal["back", "other"], normal["ahead", "other"] = ring_near(normal_other, "z")
    cot["at", "other"] = hop(own_cot, xl=1)
    back_other = hop(own_back, xh=1)
    ahead_other, own_cot, cot_ahead = all_after(
        [normal["ahead", "other"], own_cot, cot["ahead", "own"]], [normal["back", "other"]]
    )
    normal["far", "other"] = hop(ahead_other, z=3)
    cot["back", "own"] = hop(own_cot, z=1)
    cot["ahead", "other"] = hop(cot_ahead, xl=1)
    far_other, own_back, back_other, cot_back, cot_other = all_after(
        [normal["far", "other"], own_back, back_other, cot["back", "own"], cot["at", "other"]], []
    )
    normal["far", "other"] = far_other
    back_weights = gather_row_near(pair_of(own_back, back_other))
    normal_all = rows_of_group(normal)
    cot["far", "own"] = hop(cot_back, z=1)
    cot["far", "other"] = hop(cot_other, z=2)
    cot["back", "other"] = hop(cot_back, xl=1)

    qkv, attended, logs, active, slope = forward(normal_all, weights, qkv_cols, up_cols, tables)
    late = (("far", "own"), ("far", "other"), ("back", "other"))
    qkv, *held = all_after([qkv, *[cot[place] for place in late]], [])
    cot_all = rows_of_group(cot | dict(zip(late, held)))
    (back_grads,) = weight_grads(cot_all, attended, active)
    back_pair = scatter_row_near(back_grads)
    attended, active = all_after([attended, active], [back_grads])
    out_far = project_far(attended, active, back_weights)
    out_first = scatter_col_first(out_far)
    attended, active = all_after([attended, active], [out_far[0]])
    out_near = project_near_halves(attended, active, back_weights)
    out_early = scatter_col_early(out_near)

    cot_all = after(cot_all, out_near[0])
    d_attended, d_hidden, up_bias_part = backward(cot_all, back_weights, slope, *back_cols)
    d_attended, d_hidden, *out_first = all_after([d_attended, d_hidden, *out_first], [])
    out_late = scatter_col_late(out_near, out_first)
    d_mixture, qkv_bias_part = attend_back(qkv, d_attended, logs, *tables)
    biases = jnp.concatenate([qkv_bias_part, up_bias_part], 1)
    in_grads, sums = weight_grads(normal_all, d_mixture, d_hidden, (vectors, weights, biases))
    in_grads, sums, d_mixture, d_hidden, *out_got = all_after(
        [in_grads, sums, d_mixture, d_hidden, *out_early, *out_late], []
    )
    in_pair = scatter_row_near(in_grads)

    cot_sum = jnp.sum(cotangent.astype(F32), axis=0, keepdims=True)
    biases = jnp.pad(biases, ((0, 0), (0, width - biases.shape[1])))
    line = jnp.arange(8)[:, None]
    packed = jnp.where(line == 4, cot_sum, jnp.where(line == 5, biases, sums))
    packed = packed + hop(packed, c=1)
    u_far = project_far(d_mixture, d_hidden, weights)
    packed, d_mixture, d_hidden, back_pair, *u_far = all_after(
        [packed, d_mixture, d_hidden, back_pair, *u_far], []
    )
    u_first = scatter_col_first(u_far)
    packed = packed + hop(packed, xh=1)
    back_kept, back_got = scatter_row_far(back_pair)
    back_early, ahead_early, back_late, ahead_late = out_got
    out_parts = ((back_late, ahead_early), (back_early, ahead_late))
    out_kept, out_got = scatter_col_third(out_near[4], out_parts)
    u_near = project_near(d_mixture, d_hidden, weights)
    packed, back_got, out_got, *held = all_after([packed, back_got, out_got, *u_near, *u_first], [])
    u_near, u_first = held[:3], held[3:]
    u_second = scatter_col_second(u_near, u_first)
    packed = packed + jnp.where(line == 5, 0.0, hop(packed, xl=1))
    layer_out = (
        tokens.astype(F32)
        + (out_kept + out_got.astype(F32))
        + dense_bias.astype(F32)
        + down_bias.astype(F32)
    ).astype(BF16)
    packed = packed + swap(packed, "y")
    packed = packed + hop(packed, y=2)
    bias_total = packed[5:6]
    qkv_bias_total = lax.dynamic_slice_in_dim(
        packed[5], row_index * qkv_bias.shape[0], qkv_bias.shape[0], 0
    )
    up_bias_total = lax.dynamic_slice_in_dim(
        packed[5], qkv_cols + row_index * up_bias.shape[0], up_bias.shape[0], 0
    )
    in_kept, in_got = scatter_row_far(after(in_pair, packed))
    packed, in_got, *u_second = all_after([packed, in_got, *u_second], [layer_out])
    half = tok_count
    u_parts = [[part[place * half : (place + 1) * half] for part in u_second] for place in range(2)]
    u_kept, u_got = scatter_col_third(u_near[2], u_parts)
    packed = packed + swap(packed, "z")
    packed = packed + hop(packed, z=2)

    def flat(kept, got):
        return (kept.reshape(slice_rows, -1), got.reshape(slice_rows, -1))

    dense_total, down_total = vmem_call(
        finish_back_kernel,
        tuple(shape(cols, slice_rows, F32) for cols in back_cols),
        flat(back_kept, back_got),
    )
    qkv_total, up_total = vmem_call(
        finish_in_kernel,
        tuple(shape(slice_rows, cols, F32) for cols in (qkv_cols, up_cols)),
        (row_index.astype(jnp.int32)[None], *flat(in_kept, in_got), vectors, bias_total),
        scalars=1,
    )
    (input_grad,) = vmem_call(
        input_grad_kernel,
        (shape(tok_count, width, BF16),),
        (tokens, cotangent, u_kept, u_got),
    )

    return (
        layer_out,
        input_grad,
        packed[0],
        packed[1],
        packed[2],
        packed[3],
        qkv_total,
        qkv_bias_total,
        dense_total,
        packed[4],
        up_total,
        up_bias_total,
        down_total,
        packed[4],
    )


def solution(mesh):
    fine = Mesh(mesh.devices.reshape(tuple(SIZES.values())), NAMES)
    everywhere = P(ROW + COL, None)
    return jax.shard_map(
        shards,
        mesh=fine,
        in_specs=(
            everywhere,
            P(ROW, None),
            P(),
            P(),
            P(),
            P(),
            P(ROW, COL),
            P(COL + ROW),
            P(COL, ROW),
            P(),
            P(ROW, COL),
            P(COL + ROW),
            P(COL, ROW),
            P(),
            everywhere,
        ),
        out_specs=(
            everywhere,
            everywhere,
            P(),
            P(),
            P(),
            P(),
            P(ROW, COL),
            P(COL + ROW),
            P(COL, ROW),
            P(),
            P(ROW, COL),
            P(COL + ROW),
            P(COL, ROW),
            P(),
        ),
        check_vma=False,
    )
```

```python
import functools
import itertools
import math

import jax
import jax.numpy as jnp
from jax import lax
from jax.experimental import pallas as pl
from jax.experimental.pallas import tpu as pltpu
from jax.sharding import Mesh
from jax.sharding import PartitionSpec as P

HS = 256
ROT = 64
BLOCK = 256
SIZES = {"xh": 2, "y": 4, "c": 2, "z": 4, "xl": 2}
NAMES = tuple(SIZES)
ROW = ("xh", "y", "c")
COL = ("z", "xl")
F32 = jnp.float32
BF16 = jnp.bfloat16


def light():
    return pl.CostEstimate(flops=1, bytes_accessed=1, transcendentals=0)


def hop(value, **deltas):
    return send(value, tuple(deltas), lambda coords: [c + deltas[name] for name, c in coords.items()])


def swap(value, axis):
    return send(value, (axis,), lambda coords: [coords[axis] ^ 1])


def send(value, names, target):
    axes = tuple(name for name in NAMES if name in names)

    def flat(coords):
        index = 0
        for name, place in zip(axes, coords):
            index = index * SIZES[name] + place % SIZES[name]
        return index

    pairs = []
    for coords in itertools.product(*[range(SIZES[name]) for name in axes]):
        pairs.append((flat(coords), flat(target(dict(zip(axes, coords))))))
    return lax.ppermute(value, axes if len(axes) > 1 else axes[0], pairs)


def rows_at(value, start, count):
    return lax.dynamic_slice_in_dim(value, start, count, 0)


def after(value, *others):
    return lax.optimization_barrier((value, *others))[0]


def all_after(values, others):
    return list(lax.optimization_barrier((*values, *others))[: len(values)])


def ring_near(pair, axis):
    return [hop(pair, **{axis: 1}), hop(pair, **{axis: 3})]


def places(axis, pair):
    at, own = lax.axis_index(axis), lax.axis_index(pair)
    return {
        "at": at,
        "back": (at + 3) % 4,
        "ahead": (at + 1) % 4,
        "far": (at + 2) % 4,
        "own": own,
        "other": 1 - own,
    }


def group_kernel(count, places_ref, *refs):
    *sources, out_ref = refs
    for number, source in enumerate(sources):
        start = pl.multiple_of(places_ref[number] * count, count)
        out_ref[pl.ds(start, count), :] = source[...]


def rows_of_group(blocks):
    count, width = blocks["at", "own"].shape
    at = places("z", "xl")
    index = jnp.stack([at[place] * 2 + at[pair] for place, pair in blocks]).astype(jnp.int32)
    outs = (shape(8 * count, width, BF16),)
    kernel = functools.partial(group_kernel, count)
    (whole,) = vmem_call(kernel, outs, (index, *blocks.values()), scalars=1, limit=60)
    return whole


def gather_row_near(pair):
    return lax.all_gather(pair, ("y", "c"), axis=0)


def scatter_col_first(far):
    return [hop(far[0], z=1), hop(far[1], z=3)]


def scatter_col_second(near, first):
    low, high = first
    up, down = near[:2]
    count = low.shape[0]
    up = jnp.concatenate([up[:count] + low, up[count:]], 0)
    down = jnp.concatenate([down[:count], down[count:] + high], 0)
    return [hop(up, z=1), hop(down, z=3)]


def scatter_col_early(near):
    return [hop(near[1], z=1), hop(near[2], z=3)]


def scatter_col_late(near, first):
    return [hop(near[0] + first[0], z=1), hop(near[3] + first[1], z=3)]


def scatter_col_third(own, parts):
    mine = lax.axis_index("xl") == 0
    count = own.shape[0] // 2
    halves = [
        sum(part.astype(F32) for part in (own[place * count : (place + 1) * count], *got))
        for place, got in enumerate(parts)
    ]
    kept, sent = jnp.where(mine, halves[0], halves[1]), jnp.where(mine, halves[1], halves[0])
    return kept, hop(sent.astype(BF16), xl=1)


def scatter_row_near(blocks):
    return lax.psum_scatter(blocks.reshape(8, *blocks.shape[2:]), ("y", "c"), scatter_dimension=0)


def scatter_row_far(pair):
    xh = lax.axis_index("xh")
    kept = lax.dynamic_index_in_dim(pair, xh, 0, keepdims=False)
    sent = lax.dynamic_index_in_dim(pair, 1 - xh, 0, keepdims=False)
    return kept, hop(sent, xh=1)


def nt(left, right):
    return lax.dot_general(left, right, (((1,), (1,)), ((), ())), preferred_element_type=F32)


def tn(left, right):
    return lax.dot_general(left, right, (((0,), (0,)), ((), ())), preferred_element_type=F32)


def nn(left, right):
    return jnp.dot(left, right, preferred_element_type=F32)


def turn(part, cosine, sine):
    lane = lax.broadcasted_iota(jnp.int32, part.shape, 1)
    ahead = pltpu.roll(part, 128 - ROT // 2, 1)
    behind = pltpu.roll(part, ROT // 2, 1)
    return part * cosine + jnp.where(lane < ROT // 2, ahead, behind) * sine


def block_allowed(doc_col, doc_row, start, width):
    docs = doc_col[start : start + BLOCK] == doc_row[:, :width]
    row = start + lax.broadcasted_iota(jnp.int32, (BLOCK, width), 0)
    column = lax.broadcasted_iota(jnp.int32, (BLOCK, width), 1)
    return docs & (column <= row)


def attend(mix_ref, cos_ref, sin_ref, doc_col_ref, doc_row_ref, qkv_ref, out_ref, log_ref):
    rows = mix_ref.shape[1]
    for start in range(0, rows, BLOCK):
        at = pl.ds(start, BLOCK)
        cosine, sine = cos_ref[at, :], sin_ref[at, :]
        for part in range(2):
            first = part * HS
            qkv_ref[at, first : first + 128] = turn(mix_ref[part, at, :128], cosine, sine).astype(BF16)
            qkv_ref[at, first + 128 : first + HS] = mix_ref[part, at, 128:].astype(BF16)
        qkv_ref[at, 2 * HS :] = mix_ref[2, at, :].astype(BF16)
    doc_row = doc_row_ref[...]
    doc_col = doc_col_ref[...]
    for start in range(0, rows, BLOCK):
        width = start + BLOCK
        at = pl.ds(start, BLOCK)
        scores = nt(qkv_ref[at, :HS], qkv_ref[:width, HS : 2 * HS]) * HS ** (-0.5)
        scores = jnp.where(block_allowed(doc_col, doc_row, start, width), scores, -1e30)
        top = jnp.max(scores, axis=1, keepdims=True)
        raised = jnp.exp(scores - top)
        total = jnp.sum(raised, axis=1, keepdims=True)
        probabilities = (raised * (1.0 / total)).astype(BF16)
        out_ref[at, :] = nn(probabilities, qkv_ref[:width, 2 * HS :]).astype(BF16)
        log_ref[at, :] = top + jnp.log(total)


def attend_back_kernel(qkv_ref, grad_ref, log_ref, cos_ref, sin_ref, doc_col_ref, doc_row_ref, out_ref, sum_ref, dk_ref, dv_ref):
    rows = qkv_ref.shape[0]
    scaling = HS ** (-0.5)
    doc_row = doc_row_ref[...]
    doc_col = doc_col_ref[...]
    sums = [jnp.zeros((1, HS), F32) for _ in range(3)]

    def finish(value, start, first):
        at = pl.ds(start, BLOCK)
        head = turn(value[:, :128], cos_ref[at, :], -sin_ref[at, :]).astype(BF16)
        rest = value[:, 128:].astype(BF16)
        out_ref[at, first : first + 128] = head
        out_ref[at, first + 128 : first + HS] = rest
        both = jnp.concatenate([head.astype(F32), rest.astype(F32)], 1)
        return jnp.sum(both, axis=0, keepdims=True)

    for start in range(0, rows, BLOCK):
        width = start + BLOCK
        at = pl.ds(start, BLOCK)
        query = qkv_ref[at, :HS]
        grad = grad_ref[at, :]
        scores = nt(query, qkv_ref[:width, HS : 2 * HS]) * scaling
        allowed = block_allowed(doc_col, doc_row, start, width)
        weights = jnp.where(allowed, jnp.exp(scores - log_ref[at, :]), 0.0)
        probabilities = weights.astype(BF16)
        d_probs = nt(grad, qkv_ref[:width, 2 * HS :])
        inner = jnp.sum(weights * d_probs, axis=1, keepdims=True)
        d_scores = (weights * (d_probs - inner)).astype(BF16)
        d_values = tn(probabilities, grad)
        d_keys = tn(d_scores, query) * scaling
        if start:
            dv_ref[:start, :] += d_values[:start]
            dk_ref[:start, :] += d_keys[:start]
        dv_ref[start:width, :] = d_values[start:]
        dk_ref[start:width, :] = d_keys[start:]
        d_query = nn(d_scores, qkv_ref[:width, HS : 2 * HS]) * scaling
        sums[0] = sums[0] + finish(d_query, start, 0)
    for start in range(0, rows, BLOCK):
        at = pl.ds(start, BLOCK)
        sums[1] = sums[1] + finish(dk_ref[at, :], start, HS)
        values = dv_ref[at, :].astype(BF16)
        out_ref[at, 2 * HS :] = values
        sums[2] = sums[2] + jnp.sum(values.astype(F32), axis=0, keepdims=True)
    for part in range(3):
        sum_ref[:, part * HS : (part + 1) * HS] = sums[part]


PART = 256


def whole_spec(array):
    return pl.BlockSpec(array.shape, lambda i: (0,) * array.ndim)


def columns_spec(rows, first=0, last=None):
    if last is None:
        return pl.BlockSpec((rows, PART), lambda i: (0, i + first))
    return pl.BlockSpec((rows, PART), lambda i: (0, jnp.clip(i + first, 0, last)))


def grid_call(kernel, steps, outs, out_specs, args, in_specs, scratch=()):
    return pl.pallas_call(
        kernel,
        grid=(steps,),
        out_shape=tuple(outs),
        in_specs=in_specs,
        out_specs=tuple(out_specs),
        scratch_shapes=scratch,
        compiler_params=pltpu.CompilerParams(vmem_limit_bytes=48 * 1024 * 1024),
        cost_estimate=light(),
    )(*args)


def quarter_spec(weights, width):
    block = (weights.shape[0] // 2, 1, weights.shape[2], width)
    return pl.BlockSpec(block, lambda i: (i % 2, i // 2, 0, 0))


def project_kernel(steps, z_ref, one_ref, two_ref, weight_ref, *refs):
    *out_refs, both_ref = refs
    part = one_ref.shape[0] // 4

    @pl.when(pl.program_id(0) == 0)
    def _():
        for number, step in enumerate(steps):
            rows = pl.ds(pl.multiple_of((z_ref[0] + step) % 4 * part, part), part)
            at = slice(number * part, (number + 1) * part)
            both_ref[at, : one_ref.shape[1]] = one_ref[rows, :]
            both_ref[at, one_ref.shape[1] :] = two_ref[rows, :]

    block = weight_ref[...].reshape(-1, weight_ref.shape[-1])
    total = nt(both_ref[...], block).astype(BF16)
    first = 0
    for out_ref in out_refs:
        out_ref[...] = total[first : first + out_ref.shape[0]]
        first += out_ref.shape[0]


def project(one, two, weights, steps, counts):
    width = one.shape[1] + two.shape[1]
    features = math.prod(weights.shape[:3])
    step = features // 4
    weight_spec = quarter_spec(weights, width)
    z = lax.axis_index("z").astype(jnp.int32)[None]
    return grid_call(
        functools.partial(project_kernel, steps),
        4,
        [shape(count, features, BF16) for count in counts],
        [pl.BlockSpec((count, step), lambda i: (0, i)) for count in counts],
        (z, one, two, weights),
        [pl.BlockSpec(memory_space=pltpu.SMEM), whole_spec(one), whole_spec(two), weight_spec],
        scratch=[pltpu.VMEM((sum(counts), width), BF16)],
    )


def project_far(one, two, weights):
    eighth = one.shape[0] // 8
    return project(one, two, weights, (2,), (eighth, eighth))


def project_near(one, two, weights):
    quarter = one.shape[0] // 4
    return project(one, two, weights, (1, 3, 0), (quarter, quarter, quarter))


def project_near_halves(one, two, weights):
    eighth = one.shape[0] // 8
    return project(one, two, weights, (1, 3, 0), (eighth,) * 4 + (2 * eighth,))


def back_grads_kernel(left_ref, one_ref, two_ref, out_ref):
    block = out_ref.shape[:-1]
    first = 0
    for right_ref in (one_ref, two_ref):
        width = right_ref.shape[1]
        values = tn(left_ref[...], right_ref[...]).astype(BF16)
        out_ref[..., first : first + width] = values.reshape(*block, width)
        first += width


def in_grads_kernel(left_ref, one_ref, two_ref, norm_ref, weight_ref, bias_ref, out_ref, sums_ref):
    block = out_ref.shape[:-1]
    first = 0
    rows = []
    for number, right_ref in enumerate((one_ref, two_ref)):
        gain_sum = shift_sum = jnp.zeros((left_ref.shape[1], 128), F32)
        for part in range(0, right_ref.shape[1], PART):
            at = slice(first + part, first + part + PART)
            raw = tn(left_ref[...], right_ref[:, part : part + PART])
            wide = weight_ref[..., at].astype(F32).reshape(raw.shape)
            gain_part, shift_part = wide * raw, wide * bias_ref[:, at]
            gain_sum = gain_sum + gain_part[:, :128] + gain_part[:, 128:]
            shift_sum = shift_sum + shift_part[:, :128] + shift_part[:, 128:]
            out_ref[..., at] = raw.astype(BF16).reshape(*block, PART)
        gain = norm_ref[2 * number : 2 * number + 1, :]
        rows += [jnp.sum(part.T, axis=0, keepdims=True) / gain for part in (gain_sum, shift_sum)]
        first += right_ref.shape[1]
    sums_ref[...] = jnp.concatenate([*rows, jnp.zeros((4, left_ref.shape[1]), F32)], 0)


def weight_grads(left, one, two, extra=None):
    rows, features = left.shape
    count = features // 16
    step = 4 * count
    width = one.shape[1] + two.shape[1]
    args = [left, one, two]
    in_specs = [pl.BlockSpec((rows, step), lambda i: (0, i)), whole_spec(one), whole_spec(two)]
    outs = [jax.ShapeDtypeStruct((4, 2, 2, count, width), BF16)]
    out_specs = [pl.BlockSpec((2, 2, 1, count, width), lambda i: (i % 2, 0, i // 2, 0, 0))]
    kernel = back_grads_kernel
    if extra is not None:
        kernel = in_grads_kernel
        vectors, weights, bias = extra
        args += [vectors, weights, bias]
        in_specs += [
            pl.BlockSpec((vectors.shape[0], step), lambda i: (0, i)),
            quarter_spec(weights, width),
            whole_spec(bias),
        ]
        outs.append(shape(8, features, F32))
        out_specs.append(pl.BlockSpec((8, step), lambda i: (0, i)))
    return grid_call(kernel, features // step, outs, out_specs, args, in_specs)


def gelu_pair(hidden):
    normal = 0.5 * (1.0 + lax.erf(hidden * (1.0 / math.sqrt(2.0))))
    density = jnp.exp(-0.5 * hidden * hidden) * (1.0 / math.sqrt(2.0 * math.pi))
    return (hidden * normal, normal + hidden * density)


def natural(ref):
    return jnp.concatenate([ref[:, xh].reshape(-1, ref.shape[-1]) for xh in range(2)], 0)


def forward_kernel(split, normal_ref, weight_ref, extra_ref, cos_ref, sin_ref, doc_col_ref, doc_row_ref, qkv_ref, att_ref, log_ref, active_ref, slope_ref, bias_ref, mix_ref):
    step = pl.program_id(0)
    weight = natural(weight_ref)

    @pl.when(step == 0)
    def _():
        total = jnp.zeros((32, 128), F32)
        for place in range(extra_ref.shape[0]):
            for xh in range(2):
                total = total + extra_ref[place, xh, :32, :].astype(F32)
        lines = 14
        for line in range(lines):
            both = total[line : line + 1] + total[lines + line : lines + line + 1]
            bias_ref[line // 2 : line // 2 + 1, 128 * (line % 2) : 128 * (line % 2 + 1)] = both

    bias = bias_ref[pl.ds(step, 1), :]

    @pl.when(step < split)
    def _():
        mix_ref[step] = nn(normal_ref[...], weight) + bias

    @pl.when(step == split)
    def _():
        attend(mix_ref, cos_ref, sin_ref, doc_col_ref, doc_row_ref, qkv_ref, att_ref, log_ref)

    @pl.when(step >= split)
    def _():
        rows = normal_ref.shape[0]
        for start in range(0, rows, 256):
            at = slice(start, start + 256)
            active, slope = gelu_pair(nn(normal_ref[at, :], weight) + bias)
            active_ref[at, :] = active.astype(BF16)
            slope_ref[at, :] = slope.astype(BF16)


def forward(normal, weights, qkv_cols, up_cols, tables):
    rows, features = normal.shape
    split, steps = qkv_cols // PART, (qkv_cols + up_cols) // PART
    early = [shape(rows, qkv_cols, BF16), shape(rows, HS, BF16), shape(rows, 1, F32)]
    late = columns_spec(rows, -split, steps - split - 1)
    extra_place = weights.shape[-1] // 128 - 1
    return grid_call(
        functools.partial(forward_kernel, split),
        steps,
        early + [shape(rows, up_cols, BF16)] * 2,
        [whole_spec(out) for out in early] + [late, late],
        (normal, weights, weights, *tables),
        [
            whole_spec(normal),
            pl.BlockSpec((*weights.shape[:3], PART), lambda i: (0, 0, 0, i)),
            pl.BlockSpec((*weights.shape[:3], 128), lambda i: (0, 0, 0, extra_place)),
            *[whole_spec(table) for table in tables],
        ],
        scratch=[pltpu.VMEM((8, PART), F32), pltpu.VMEM((split, rows, PART), F32)],
    )


def backward_kernel(split, cot_ref, weight_ref, slope_ref, att_ref, hid_ref, sum_ref):
    def product():
        return nn(cot_ref[...], natural(weight_ref))

    @pl.when(pl.program_id(0) < split)
    def _():
        att_ref[...] = product().astype(BF16)

    @pl.when(pl.program_id(0) >= split)
    def _():
        value = (product() * slope_ref[...].astype(F32)).astype(BF16)
        hid_ref[...] = value
        sum_ref[...] = jnp.sum(value.astype(F32), axis=0, keepdims=True)


def backward(cot, weights, slope, dense_cols, down_cols):
    rows, features = cot.shape
    split, steps = dense_cols // PART, (dense_cols + down_cols) // PART
    outs = [shape(rows, dense_cols, BF16), shape(rows, down_cols, BF16), shape(1, down_cols, F32)]
    return grid_call(
        functools.partial(backward_kernel, split),
        steps,
        outs,
        [
            columns_spec(rows, 0, split - 1),
            columns_spec(rows, -split, steps - split - 1),
            columns_spec(1, -split, steps - split - 1),
        ],
        (cot, weights, slope),
        [
            whole_spec(cot),
            pl.BlockSpec((*weights.shape[:3], PART), lambda i: (0, 0, 0, i)),
            columns_spec(rows, -split, steps - split - 1),
        ],
    )


def finish_back_kernel(kept_ref, got_ref, dense_ref, down_ref):
    total = kept_ref[...].astype(F32) + got_ref[...].astype(F32)
    first = dense_ref.shape[0]
    dense_ref[...] = total[:, :first].T
    down_ref[...] = total[:, first:].T


def finish_in_kernel(row_ref, kept_ref, got_ref, norm_ref, bias_ref, qkv_ref, up_ref):
    total = kept_ref[...].astype(F32) + got_ref[...].astype(F32)

    def column(which):
        return own_column(row_ref, norm_ref, which, total.shape[0])

    first = 0
    for number, out_ref in enumerate((qkv_ref, up_ref)):
        at = slice(first, first + out_ref.shape[1])
        out_ref[...] = total[:, at] * column(2 * number) + column(2 * number + 1) * bias_ref[:, at]
        first += out_ref.shape[1]


def input_grad_kernel(tok_ref, cot_ref, kept_ref, got_ref, out_ref):
    tok_rows = tok_ref[...].astype(F32)
    center = jnp.mean(tok_rows, axis=-1, keepdims=True)
    centered = tok_rows - center
    variance = jnp.mean(centered * centered, axis=-1, keepdims=True)
    inverse = lax.rsqrt(variance + 1e-05)
    normal = centered * inverse
    u_rows = kept_ref[...] + got_ref[...].astype(F32)
    u_mean = jnp.mean(u_rows, axis=-1, keepdims=True)
    un_mean = jnp.mean(u_rows * normal, axis=-1, keepdims=True)
    d_rows = (u_rows - u_mean - normal * un_mean) * inverse
    out_ref[...] = (cot_ref[...].astype(F32) + d_rows).astype(BF16)


def own_column(row_ref, norm_ref, which, count):
    start = pl.multiple_of(row_ref[0] * count, count)
    square = (count, count)
    diagonal = lax.broadcasted_iota(jnp.int32, square, 0) == lax.broadcasted_iota(jnp.int32, square, 1)
    lanes = norm_ref[which : which + 1, pl.ds(start, count)].astype(F32)
    return jnp.sum(jnp.where(diagonal, jnp.broadcast_to(lanes, square), 0.0), axis=1, keepdims=True)


def prepare_kernel(row_ref, tok_ref, norm_ref, qkv_ref, up_ref, dense_ref, down_ref, qkv_bias_ref, up_bias_ref, normal_ref, out_ref, back_ref):
    tok_rows = tok_ref[...].astype(F32)
    center = jnp.mean(tok_rows, axis=-1, keepdims=True)
    centered = tok_rows - center
    variance = jnp.mean(centered * centered, axis=-1, keepdims=True)
    normal_ref[...] = (centered * lax.rsqrt(variance + 1e-05)).astype(BF16)
    count = qkv_ref.shape[0]

    def placed(bias_ref, width):
        own = bias_ref[...].astype(F32)
        rest = jnp.zeros((1, width - own.shape[1]), F32)
        wide = jnp.broadcast_to(jnp.concatenate([own, rest], 1), (8, width))
        return pltpu.roll(wide, row_ref[0] * own.shape[1], 1)[:1]

    lines = []
    first = 0
    for number, weight, bias in ((0, qkv_ref, qkv_bias_ref), (2, up_ref, up_bias_ref)):
        width = weight.shape[1]
        wide = weight[...].astype(F32)
        out_ref[:, first : first + width] = (wide * own_column(row_ref, norm_ref, number, count)).astype(BF16)
        shifted = jnp.sum(wide * own_column(row_ref, norm_ref, number + 1, count), axis=0, keepdims=True)
        shifted = shifted + placed(bias, width)
        lines += [shifted[:, 128 * i : 128 * (i + 1)] for i in range(width // 128)]
        first += width
    first_back = 0
    for weight in (dense_ref, down_ref):
        width = weight.shape[0]
        back_ref[:, first_back : first_back + width] = weight[...].astype(F32).T.astype(BF16)
        first_back += width
    high = [line.astype(BF16).astype(F32) for line in lines]
    low = [line - part for line, part in zip(lines, high)]
    rest = jnp.zeros((count - 2 * len(lines), 128), F32)
    out_ref[:, first:] = jnp.concatenate([*high, *low, rest], 0).astype(BF16)


def vmem_call(kernel, outs, args, scratch=(), scalars=0, limit=40):
    spec = pl.BlockSpec()
    scalar = pl.BlockSpec(memory_space=pltpu.SMEM)
    return pl.pallas_call(
        kernel,
        out_shape=outs,
        in_specs=[scalar] * scalars + [spec] * (len(args) - scalars),
        out_specs=[spec] * len(outs),
        scratch_shapes=scratch,
        compiler_params=pltpu.CompilerParams(vmem_limit_bytes=limit * 1024 * 1024),
        cost_estimate=light(),
    )(*args)


def shape(rows, columns, dtype):
    return jax.ShapeDtypeStruct((rows, columns), dtype)


def attend_back(qkv, grad, logs, cosine, sine, doc_col, doc_row):
    rows = qkv.shape[0]
    outs = (shape(rows, 3 * HS, BF16), shape(1, 3 * HS, F32))
    return vmem_call(
        attend_back_kernel,
        outs,
        (qkv, grad, logs, cosine, sine, doc_col, doc_row),
        scratch=[pltpu.VMEM((rows, HS), F32), pltpu.VMEM((rows, HS), F32)],
    )


def doc_layout(lengths, places):
    first, second = lengths[0], lengths[0] + lengths[1]
    third = second + lengths[2]
    passed = [(places >= end).astype(jnp.int32) for end in (first, second, third)]
    doc_ids = passed[0] + passed[1] + passed[2]
    begins = passed[0] * lengths[0] + passed[1] * lengths[1] + passed[2] * lengths[2]
    return (doc_ids, places - begins)


def rotary_tables(positions):
    half = ROT // 2
    lane = jnp.arange(128, dtype=jnp.int32)
    frequency = 1.0 / 10000.0 ** ((lane % half).astype(F32) * (2.0 / ROT))
    frequency = jnp.where(lane < ROT, frequency, 0.0)
    angles = positions.astype(F32) * frequency[None, :]
    sign = jnp.where(lane < half, -1.0, 1.0)
    return (jnp.cos(angles), jnp.sin(angles) * sign[None, :])


def shards(
    tokens,
    doc_lengths,
    input_gain,
    input_shift,
    post_gain,
    post_shift,
    qkv_weight,
    qkv_bias,
    dense_weight,
    dense_bias,
    up_weight,
    up_bias,
    down_weight,
    down_bias,
    cotangent,
):
    row_index = (lax.axis_index("xh") * 4 + lax.axis_index("y")) * 2 + lax.axis_index("c")
    slice_rows = qkv_weight.shape[0]
    qkv_cols, up_cols = qkv_weight.shape[1], up_weight.shape[1]

    tok_count, width = tokens.shape
    vectors = jnp.concatenate([input_gain, input_shift, post_gain, post_shift]).astype(F32).reshape(4, width)
    back_cols = (dense_weight.shape[0], down_weight.shape[0])
    own_normal, block, block_back = vmem_call(
        prepare_kernel,
        (
            shape(tok_count, width, BF16),
            shape(slice_rows, qkv_cols + up_cols + 128, BF16),
            shape(slice_rows, sum(back_cols), BF16),
        ),
        (
            row_index.astype(jnp.int32)[None],
            tokens,
            vectors,
            qkv_weight,
            up_weight,
            dense_weight,
            down_weight,
            qkv_bias[None],
            up_bias[None],
        ),
        scalars=1,
        limit=60,
    )
    xh = lax.axis_index("xh")

    def pair_of(own, other):
        return jnp.stack([jnp.where(xh == first, own, other) for first in range(2)])

    row_count = 8 * tok_count
    doc_col, positions = doc_layout(doc_lengths[0], jnp.arange(row_count, dtype=jnp.int32)[:, None])
    doc_row, _ = doc_layout(doc_lengths[0], jnp.arange(row_count, dtype=jnp.int32)[None, :])
    tables = (*rotary_tables(positions), doc_col, doc_row)

    normal = {("at", "own"): own_normal}
    cot = {("at", "own"): cotangent}
    block_other = hop(block, xh=1)
    normal["back", "own"], normal["ahead", "own"] = ring_near(own_normal, "z")
    block_own, block_other, near_back, own_normal, own_cot, own_back, *tables = all_after(
        [block, block_other, normal["back", "own"], own_normal, cotangent, block_back, *tables],
        [normal["ahead", "own"]],
    )
    weights = gather_row_near(pair_of(block_own, block_other))
    normal["at", "other"] = hop(own_normal, xl=1)
    normal["far", "own"] = hop(near_back, z=1)
    cot["ahead", "own"] = hop(own_cot, z=3)
    normal_other, own_cot, own_back = all_after(
        [normal["at", "other"], own_cot, own_back], [normal["far", "own"], cot["ahead", "own"]]
    )
    normal["back", "other"], normal["ahead", "other"] = ring_near(normal_other, "z")
    cot["at", "other"] = hop(own_cot, xl=1)
    back_other = hop(own_back, xh=1)
    ahead_other, own_cot, cot_ahead = all_after(
        [normal["ahead", "other"], own_cot, cot["ahead", "own"]], [normal["back", "other"]]
    )
    normal["far", "other"] = hop(ahead_other, z=3)
    cot["back", "own"] = hop(own_cot, z=1)
    cot["ahead", "other"] = hop(cot_ahead, xl=1)
    far_other, own_back, back_other, cot_back, cot_other = all_after(
        [normal["far", "other"], own_back, back_other, cot["back", "own"], cot["at", "other"]], []
    )
    normal["far", "other"] = far_other
    back_weights = gather_row_near(pair_of(own_back, back_other))
    normal_all = rows_of_group(normal)
    cot["far", "own"] = hop(cot_back, z=1)
    cot["far", "other"] = hop(cot_other, z=2)
    cot["back", "other"] = hop(cot_back, xl=1)

    qkv, attended, logs, active, slope = forward(normal_all, weights, qkv_cols, up_cols, tables)
    late = (("far", "own"), ("far", "other"), ("back", "other"))
    qkv, *held = all_after([qkv, *[cot[place] for place in late]], [])
    cot_all = rows_of_group(cot | dict(zip(late, held)))
    (back_grads,) = weight_grads(cot_all, attended, active)
    back_pair = scatter_row_near(back_grads)
    attended, active = all_after([attended, active], [back_grads])
    out_far = project_far(attended, active, back_weights)
    out_first = scatter_col_first(out_far)
    attended, active = all_after([attended, active], [out_far[0]])
    out_near = project_near_halves(attended, active, back_weights)
    out_early = scatter_col_early(out_near)

    cot_all = after(cot_all, out_near[0])
    d_attended, d_hidden, up_bias_part = backward(cot_all, back_weights, slope, *back_cols)
    d_attended, d_hidden, *out_first = all_after([d_attended, d_hidden, *out_first], [])
    out_late = scatter_col_late(out_near, out_first)
    d_mixture, qkv_bias_part = attend_back(qkv, d_attended, logs, *tables)
    biases = jnp.concatenate([qkv_bias_part, up_bias_part], 1)
    in_grads, sums = weight_grads(normal_all, d_mixture, d_hidden, (vectors, weights, biases))
    in_grads, sums, d_mixture, d_hidden, *out_got = all_after(
        [in_grads, sums, d_mixture, d_hidden, *out_early, *out_late], []
    )
    in_pair = scatter_row_near(in_grads)

    cot_sum = jnp.sum(cotangent.astype(F32), axis=0, keepdims=True)
    biases = jnp.pad(biases, ((0, 0), (0, width - biases.shape[1])))
    line = jnp.arange(8)[:, None]
    packed = jnp.where(line == 4, cot_sum, jnp.where(line == 5, biases, sums))
    packed = packed + hop(packed, c=1)
    u_far = project_far(d_mixture, d_hidden, weights)
    packed, d_mixture, d_hidden, back_pair, *u_far = all_after(
        [packed, d_mixture, d_hidden, back_pair, *u_far], []
    )
    u_first = scatter_col_first(u_far)
    packed = packed + hop(packed, xh=1)
    back_kept, back_got = scatter_row_far(back_pair)
    back_early, ahead_early, back_late, ahead_late = out_got
    out_parts = ((back_late, ahead_early), (back_early, ahead_late))
    out_kept, out_got = scatter_col_third(out_near[4], out_parts)
    u_near = project_near(d_mixture, d_hidden, weights)
    packed, back_got, out_got, *held = all_after([packed, back_got, out_got, *u_near, *u_first], [])
    u_near, u_first = held[:3], held[3:]
    u_second = scatter_col_second(u_near, u_first)
    packed = packed + jnp.where(line == 5, 0.0, hop(packed, xl=1))
    layer_out = (
        tokens.astype(F32)
        + (out_kept + out_got.astype(F32))
        + dense_bias.astype(F32)
        + down_bias.astype(F32)
    ).astype(BF16)
    packed = packed + hop(packed, y=1) + hop(packed, y=2) + hop(packed, y=3)
    bias_total = packed[5:6]
    qkv_bias_total = lax.dynamic_slice_in_dim(
        packed[5], row_index * qkv_bias.shape[0], qkv_bias.shape[0], 0
    )
    up_bias_total = lax.dynamic_slice_in_dim(
        packed[5], qkv_cols + row_index * up_bias.shape[0], up_bias.shape[0], 0
    )
    in_kept, in_got = scatter_row_far(in_pair)
    packed, in_got, *u_second = all_after([packed, in_got, *u_second], [layer_out])
    half = tok_count
    u_parts = [[part[place * half : (place + 1) * half] for part in u_second] for place in range(2)]
    u_kept, u_got = scatter_col_third(u_near[2], u_parts)
    packed = packed + swap(packed, "z")
    packed = packed + hop(packed, z=2)

    def flat(kept, got):
        return (kept.reshape(slice_rows, -1), got.reshape(slice_rows, -1))

    dense_total, down_total = vmem_call(
        finish_back_kernel,
        tuple(shape(cols, slice_rows, F32) for cols in back_cols),
        flat(back_kept, back_got),
    )
    qkv_total, up_total = vmem_call(
        finish_in_kernel,
        tuple(shape(slice_rows, cols, F32) for cols in (qkv_cols, up_cols)),
        (row_index.astype(jnp.int32)[None], *flat(in_kept, in_got), vectors, bias_total),
        scalars=1,
    )
    (input_grad,) = vmem_call(
        input_grad_kernel,
        (shape(tok_count, width, BF16),),
        (tokens, cotangent, u_kept, u_got),
    )

    return (
        layer_out,
        input_grad,
        packed[0],
        packed[1],
        packed[2],
        packed[3],
        qkv_total,
        qkv_bias_total,
        dense_total,
        packed[4],
        up_total,
        up_bias_total,
        down_total,
        packed[4],
    )


def solution(mesh):
    fine = Mesh(mesh.devices.reshape(tuple(SIZES.values())), NAMES)
    everywhere = P(ROW + COL, None)
    return jax.shard_map(
        shards,
        mesh=fine,
        in_specs=(
            everywhere,
            P(ROW, None),
            P(),
            P(),
            P(),
            P(),
            P(ROW, COL),
            P(COL + ROW),
            P(COL, ROW),
            P(),
            P(ROW, COL),
            P(COL + ROW),
            P(COL, ROW),
            P(),
            everywhere,
        ),
        out_specs=(
            everywhere,
            everywhere,
            P(),
            P(),
            P(),
            P(),
            P(ROW, COL),
            P(COL + ROW),
            P(COL, ROW),
            P(),
            P(ROW, COL),
            P(COL + ROW),
            P(COL, ROW),
            P(),
        ),
        check_vma=False,
    )
```

```python
import functools
import itertools
import math

import jax
import jax.numpy as jnp
from jax import lax
from jax.experimental import pallas as pl
from jax.experimental.pallas import tpu as pltpu
from jax.sharding import Mesh
from jax.sharding import PartitionSpec as P

HS = 256
ROT = 64
BLOCK = 256
SIZES = {"xh": 2, "y": 4, "c": 2, "z": 4, "xl": 2}
NAMES = tuple(SIZES)
ROW = ("xh", "y", "c")
COL = ("z", "xl")
F32 = jnp.float32
BF16 = jnp.bfloat16


def light():
    return pl.CostEstimate(flops=1, bytes_accessed=1, transcendentals=0)


def hop(value, **deltas):
    return send(value, tuple(deltas), lambda coords: [c + deltas[name] for name, c in coords.items()])


def swap(value, axis):
    return send(value, (axis,), lambda coords: [coords[axis] ^ 1])


def send(value, names, target):
    axes = tuple(name for name in NAMES if name in names)

    def flat(coords):
        index = 0
        for name, place in zip(axes, coords):
            index = index * SIZES[name] + place % SIZES[name]
        return index

    pairs = []
    for coords in itertools.product(*[range(SIZES[name]) for name in axes]):
        pairs.append((flat(coords), flat(target(dict(zip(axes, coords))))))
    return lax.ppermute(value, axes if len(axes) > 1 else axes[0], pairs)


def rows_at(value, start, count):
    return lax.dynamic_slice_in_dim(value, start, count, 0)


def after(value, *others):
    return lax.optimization_barrier((value, *others))[0]


def all_after(values, others):
    return list(lax.optimization_barrier((*values, *others))[: len(values)])


def ring_near(pair, axis):
    return [hop(pair, **{axis: 1}), hop(pair, **{axis: 3})]


def places(axis, pair):
    at, own = lax.axis_index(axis), lax.axis_index(pair)
    return {
        "at": at,
        "back": (at + 3) % 4,
        "ahead": (at + 1) % 4,
        "far": (at + 2) % 4,
        "own": own,
        "other": 1 - own,
    }


def group_kernel(count, places_ref, *refs):
    *sources, out_ref = refs
    for number, source in enumerate(sources):
        start = pl.multiple_of(places_ref[number] * count, count)
        out_ref[pl.ds(start, count), :] = source[...]


def rows_of_group(blocks):
    count, width = blocks["at", "own"].shape
    at = places("z", "xl")
    index = jnp.stack([at[place] * 2 + at[pair] for place, pair in blocks]).astype(jnp.int32)
    part = width // 4
    (whole,) = grid_call(
        functools.partial(group_kernel, count),
        4,
        [shape(8 * count, width, BF16)],
        [pl.BlockSpec((8 * count, part), lambda i: (0, i))],
        (index, *blocks.values()),
        [pl.BlockSpec(memory_space=pltpu.SMEM)]
        + [pl.BlockSpec((count, part), lambda i: (0, i)) for _ in blocks],
        limit=60,
    )
    return whole


def gather_row_near(pair):
    return lax.all_gather(pair, ("y", "c"), axis=0)


def scatter_col_first(far):
    return [hop(far[0], z=1), hop(far[1], z=3)]


def scatter_col_second(near, first):
    low, high = first
    up, down = near[:2]
    count = low.shape[0]
    up = jnp.concatenate([up[:count] + low, up[count:]], 0)
    down = jnp.concatenate([down[:count], down[count:] + high], 0)
    return [hop(up, z=1), hop(down, z=3)]


def scatter_col_early(near):
    return [hop(near[1], z=1), hop(near[2], z=3)]


def scatter_col_late(near, first):
    return [hop(near[0] + first[0], z=1), hop(near[3] + first[1], z=3)]


def scatter_col_third(own, parts):
    mine = lax.axis_index("xl") == 0
    count = own.shape[0] // 2
    halves = [
        sum(part.astype(F32) for part in (own[place * count : (place + 1) * count], *got))
        for place, got in enumerate(parts)
    ]
    kept, sent = jnp.where(mine, halves[0], halves[1]), jnp.where(mine, halves[1], halves[0])
    return kept, hop(sent.astype(BF16), xl=1)


def scatter_row_near(blocks):
    return lax.psum_scatter(blocks.reshape(8, *blocks.shape[2:]), ("y", "c"), scatter_dimension=0)


def scatter_row_far(pair):
    xh = lax.axis_index("xh")
    kept = lax.dynamic_index_in_dim(pair, xh, 0, keepdims=False)
    sent = lax.dynamic_index_in_dim(pair, 1 - xh, 0, keepdims=False)
    return kept, hop(sent, xh=1)


def nt(left, right):
    return lax.dot_general(left, right, (((1,), (1,)), ((), ())), preferred_element_type=F32)


def tn(left, right):
    return lax.dot_general(left, right, (((0,), (0,)), ((), ())), preferred_element_type=F32)


def nn(left, right):
    return jnp.dot(left, right, preferred_element_type=F32)


def turn(part, cosine, sine):
    lane = lax.broadcasted_iota(jnp.int32, part.shape, 1)
    ahead = pltpu.roll(part, 128 - ROT // 2, 1)
    behind = pltpu.roll(part, ROT // 2, 1)
    return part * cosine + jnp.where(lane < ROT // 2, ahead, behind) * sine


def block_allowed(doc_col, doc_row, start, width):
    docs = doc_col[start : start + BLOCK] == doc_row[:, :width]
    row = start + lax.broadcasted_iota(jnp.int32, (BLOCK, width), 0)
    column = lax.broadcasted_iota(jnp.int32, (BLOCK, width), 1)
    return docs & (column <= row)


def attend(mix_ref, cos_ref, sin_ref, doc_col_ref, doc_row_ref, qkv_ref, out_ref, log_ref):
    rows = mix_ref.shape[1]
    for start in range(0, rows, BLOCK):
        at = pl.ds(start, BLOCK)
        cosine, sine = cos_ref[at, :], sin_ref[at, :]
        for part in range(2):
            first = part * HS
            qkv_ref[at, first : first + 128] = turn(mix_ref[part, at, :128], cosine, sine).astype(BF16)
            qkv_ref[at, first + 128 : first + HS] = mix_ref[part, at, 128:].astype(BF16)
        qkv_ref[at, 2 * HS :] = mix_ref[2, at, :].astype(BF16)
    doc_row = doc_row_ref[...]
    doc_col = doc_col_ref[...]
    for start in range(0, rows, BLOCK):
        width = start + BLOCK
        at = pl.ds(start, BLOCK)
        scores = nt(qkv_ref[at, :HS], qkv_ref[:width, HS : 2 * HS]) * HS ** (-0.5)
        scores = jnp.where(block_allowed(doc_col, doc_row, start, width), scores, -1e30)
        top = jnp.max(scores, axis=1, keepdims=True)
        raised = jnp.exp(scores - top)
        total = jnp.sum(raised, axis=1, keepdims=True)
        probabilities = (raised * (1.0 / total)).astype(BF16)
        out_ref[at, :] = nn(probabilities, qkv_ref[:width, 2 * HS :]).astype(BF16)
        log_ref[at, :] = top + jnp.log(total)


def attend_back_kernel(qkv_ref, grad_ref, log_ref, cos_ref, sin_ref, doc_col_ref, doc_row_ref, out_ref, sum_ref, dk_ref, dv_ref):
    rows = qkv_ref.shape[0]
    scaling = HS ** (-0.5)
    doc_row = doc_row_ref[...]
    doc_col = doc_col_ref[...]
    sums = [jnp.zeros((1, HS), F32) for _ in range(3)]

    def finish(value, start, first):
        at = pl.ds(start, BLOCK)
        head = turn(value[:, :128], cos_ref[at, :], -sin_ref[at, :]).astype(BF16)
        rest = value[:, 128:].astype(BF16)
        out_ref[at, first : first + 128] = head
        out_ref[at, first + 128 : first + HS] = rest
        both = jnp.concatenate([head.astype(F32), rest.astype(F32)], 1)
        return jnp.sum(both, axis=0, keepdims=True)

    for start in range(0, rows, BLOCK):
        width = start + BLOCK
        at = pl.ds(start, BLOCK)
        query = qkv_ref[at, :HS]
        grad = grad_ref[at, :]
        scores = nt(query, qkv_ref[:width, HS : 2 * HS]) * scaling
        allowed = block_allowed(doc_col, doc_row, start, width)
        weights = jnp.where(allowed, jnp.exp(scores - log_ref[at, :]), 0.0)
        probabilities = weights.astype(BF16)
        d_probs = nt(grad, qkv_ref[:width, 2 * HS :])
        inner = jnp.sum(weights * d_probs, axis=1, keepdims=True)
        d_scores = (weights * (d_probs - inner)).astype(BF16)
        d_values = tn(probabilities, grad)
        d_keys = tn(d_scores, query) * scaling
        if start:
            dv_ref[:start, :] += d_values[:start]
            dk_ref[:start, :] += d_keys[:start]
        dv_ref[start:width, :] = d_values[start:]
        dk_ref[start:width, :] = d_keys[start:]
        d_query = nn(d_scores, qkv_ref[:width, HS : 2 * HS]) * scaling
        sums[0] = sums[0] + finish(d_query, start, 0)
    for start in range(0, rows, BLOCK):
        at = pl.ds(start, BLOCK)
        sums[1] = sums[1] + finish(dk_ref[at, :], start, HS)
        values = dv_ref[at, :].astype(BF16)
        out_ref[at, 2 * HS :] = values
        sums[2] = sums[2] + jnp.sum(values.astype(F32), axis=0, keepdims=True)
    for part in range(3):
        sum_ref[:, part * HS : (part + 1) * HS] = sums[part]


PART = 256


def whole_spec(array):
    return pl.BlockSpec(array.shape, lambda i: (0,) * array.ndim)


def columns_spec(rows, first=0, last=None):
    if last is None:
        return pl.BlockSpec((rows, PART), lambda i: (0, i + first))
    return pl.BlockSpec((rows, PART), lambda i: (0, jnp.clip(i + first, 0, last)))


def grid_call(kernel, steps, outs, out_specs, args, in_specs, scratch=(), limit=48):
    return pl.pallas_call(
        kernel,
        grid=(steps,),
        out_shape=tuple(outs),
        in_specs=in_specs,
        out_specs=tuple(out_specs),
        scratch_shapes=scratch,
        compiler_params=pltpu.CompilerParams(vmem_limit_bytes=limit * 1024 * 1024),
        cost_estimate=light(),
    )(*args)


def quarter_spec(weights, width):
    block = (weights.shape[0] // 2, 1, weights.shape[2], width)
    return pl.BlockSpec(block, lambda i: (i % 2, i // 2, 0, 0))


def project_kernel(count, z_ref, *refs):
    row_refs, weight_ref, out_refs, both_ref = refs[: 2 * count], refs[2 * count], refs[2 * count + 1 : -1], refs[-1]

    @pl.when(pl.program_id(0) == 0)
    def _():
        for number in range(count):
            one_ref, two_ref = row_refs[2 * number : 2 * number + 2]
            part, split = one_ref.shape
            at = slice(number * part, (number + 1) * part)
            both_ref[at, :split] = one_ref[...]
            both_ref[at, split:] = two_ref[...]

    block = weight_ref[...].reshape(-1, weight_ref.shape[-1])
    total = nt(both_ref[...], block).astype(BF16)
    first = 0
    for out_ref in out_refs:
        out_ref[...] = total[first : first + out_ref.shape[0]]
        first += out_ref.shape[0]


def project(one, two, weights, steps, counts):
    width = one.shape[1] + two.shape[1]
    features = math.prod(weights.shape[:3])
    step = features // 4
    part = one.shape[0] // 4
    block = (weights.shape[0] // 2, 1, weights.shape[2], width)
    row_specs = [
        pl.BlockSpec((part, side.shape[1]), lambda i, z, ahead=ahead: ((z[0] + ahead) % 4, 0))
        for ahead in steps
        for side in (one, two)
    ]
    z = lax.axis_index("z").astype(jnp.int32)[None]
    return pl.pallas_call(
        functools.partial(project_kernel, len(steps)),
        grid_spec=pltpu.PrefetchScalarGridSpec(
            num_scalar_prefetch=1,
            grid=(4,),
            in_specs=[*row_specs, pl.BlockSpec(block, lambda i, z: (i % 2, i // 2, 0, 0))],
            out_specs=tuple(pl.BlockSpec((count, step), lambda i, z: (0, i)) for count in counts),
            scratch_shapes=[pltpu.VMEM((sum(counts), width), BF16)],
        ),
        out_shape=tuple(shape(count, features, BF16) for count in counts),
        compiler_params=pltpu.CompilerParams(vmem_limit_bytes=48 * 1024 * 1024),
        cost_estimate=light(),
    )(z, *([one, two] * len(steps)), weights)


def project_far(one, two, weights):
    eighth = one.shape[0] // 8
    return project(one, two, weights, (2,), (eighth, eighth))


def project_near(one, two, weights):
    quarter = one.shape[0] // 4
    return project(one, two, weights, (1, 3, 0), (quarter, quarter, quarter))


def project_near_halves(one, two, weights):
    eighth = one.shape[0] // 8
    return project(one, two, weights, (1, 3, 0), (eighth,) * 4 + (2 * eighth,))


def back_grads_kernel(left_ref, one_ref, two_ref, out_ref):
    block = out_ref.shape[:-1]
    first = 0
    for right_ref in (one_ref, two_ref):
        width = right_ref.shape[1]
        values = tn(left_ref[...], right_ref[...]).astype(BF16)
        out_ref[..., first : first + width] = values.reshape(*block, width)
        first += width


def in_grads_kernel(left_ref, one_ref, two_ref, norm_ref, weight_ref, bias_ref, out_ref, sums_ref):
    block = out_ref.shape[:-1]
    first = 0
    rows = []
    for number, right_ref in enumerate((one_ref, two_ref)):
        gain_sum = shift_sum = jnp.zeros((left_ref.shape[1], 128), F32)
        for part in range(0, right_ref.shape[1], PART):
            at = slice(first + part, first + part + PART)
            raw = tn(left_ref[...], right_ref[:, part : part + PART])
            wide = weight_ref[..., at].astype(F32).reshape(raw.shape)
            gain_part, shift_part = wide * raw, wide * bias_ref[:, at]
            gain_sum = gain_sum + gain_part[:, :128] + gain_part[:, 128:]
            shift_sum = shift_sum + shift_part[:, :128] + shift_part[:, 128:]
            out_ref[..., at] = raw.astype(BF16).reshape(*block, PART)
        gain = norm_ref[2 * number : 2 * number + 1, :]
        rows += [jnp.sum(part.T, axis=0, keepdims=True) / gain for part in (gain_sum, shift_sum)]
        first += right_ref.shape[1]
    sums_ref[...] = jnp.concatenate([*rows, jnp.zeros((4, left_ref.shape[1]), F32)], 0)


def weight_grads(left, one, two, extra=None):
    rows, features = left.shape
    count = features // 16
    step = 4 * count
    width = one.shape[1] + two.shape[1]
    args = [left, one, two]
    in_specs = [pl.BlockSpec((rows, step), lambda i: (0, i)), whole_spec(one), whole_spec(two)]
    outs = [jax.ShapeDtypeStruct((4, 2, 2, count, width), BF16)]
    out_specs = [pl.BlockSpec((2, 2, 1, count, width), lambda i: (i % 2, 0, i // 2, 0, 0))]
    kernel = back_grads_kernel
    if extra is not None:
        kernel = in_grads_kernel
        vectors, weights, bias = extra
        args += [vectors, weights, bias]
        in_specs += [
            pl.BlockSpec((vectors.shape[0], step), lambda i: (0, i)),
            quarter_spec(weights, width),
            whole_spec(bias),
        ]
        outs.append(shape(8, features, F32))
        out_specs.append(pl.BlockSpec((8, step), lambda i: (0, i)))
    return grid_call(kernel, features // step, outs, out_specs, args, in_specs)


def gelu_pair(hidden):
    normal = 0.5 * (1.0 + lax.erf(hidden * (1.0 / math.sqrt(2.0))))
    density = jnp.exp(-0.5 * hidden * hidden) * (1.0 / math.sqrt(2.0 * math.pi))
    return (hidden * normal, normal + hidden * density)


def natural(ref):
    return jnp.concatenate([ref[:, xh].reshape(-1, ref.shape[-1]) for xh in range(2)], 0)


def forward_kernel(split, normal_ref, weight_ref, extra_ref, cos_ref, sin_ref, doc_col_ref, doc_row_ref, qkv_ref, att_ref, log_ref, active_ref, slope_ref, bias_ref, mix_ref):
    step = pl.program_id(0)
    weight = natural(weight_ref)

    @pl.when(step == 0)
    def _():
        total = jnp.zeros((32, 128), F32)
        for place in range(extra_ref.shape[0]):
            for xh in range(2):
                total = total + extra_ref[place, xh, :32, :].astype(F32)
        lines = 14
        for line in range(lines):
            both = total[line : line + 1] + total[lines + line : lines + line + 1]
            bias_ref[line // 2 : line // 2 + 1, 128 * (line % 2) : 128 * (line % 2 + 1)] = both

    bias = bias_ref[pl.ds(step, 1), :]

    @pl.when(step < split)
    def _():
        mix_ref[step] = nn(normal_ref[...], weight) + bias

    @pl.when(step == split)
    def _():
        attend(mix_ref, cos_ref, sin_ref, doc_col_ref, doc_row_ref, qkv_ref, att_ref, log_ref)

    @pl.when(step >= split)
    def _():
        rows = normal_ref.shape[0]
        for start in range(0, rows, 256):
            at = slice(start, start + 256)
            active, slope = gelu_pair(nn(normal_ref[at, :], weight) + bias)
            active_ref[at, :] = active.astype(BF16)
            slope_ref[at, :] = slope.astype(BF16)


def forward(normal, weights, qkv_cols, up_cols, tables):
    rows, features = normal.shape
    split, steps = qkv_cols // PART, (qkv_cols + up_cols) // PART
    early = [shape(rows, qkv_cols, BF16), shape(rows, HS, BF16), shape(rows, 1, F32)]
    late = columns_spec(rows, -split, steps - split - 1)
    extra_place = weights.shape[-1] // 128 - 1
    return grid_call(
        functools.partial(forward_kernel, split),
        steps,
        early + [shape(rows, up_cols, BF16)] * 2,
        [whole_spec(out) for out in early] + [late, late],
        (normal, weights, weights, *tables),
        [
            whole_spec(normal),
            pl.BlockSpec((*weights.shape[:3], PART), lambda i: (0, 0, 0, i)),
            pl.BlockSpec((*weights.shape[:3], 128), lambda i: (0, 0, 0, extra_place)),
            *[whole_spec(table) for table in tables],
        ],
        scratch=[pltpu.VMEM((8, PART), F32), pltpu.VMEM((split, rows, PART), F32)],
    )


def backward_kernel(split, cot_ref, weight_ref, slope_ref, att_ref, hid_ref, sum_ref):
    def product():
        return nn(cot_ref[...], natural(weight_ref))

    @pl.when(pl.program_id(0) < split)
    def _():
        att_ref[...] = product().astype(BF16)

    @pl.when(pl.program_id(0) >= split)
    def _():
        value = (product() * slope_ref[...].astype(F32)).astype(BF16)
        hid_ref[...] = value
        sum_ref[...] = jnp.sum(value.astype(F32), axis=0, keepdims=True)


def backward(cot, weights, slope, dense_cols, down_cols):
    rows, features = cot.shape
    split, steps = dense_cols // PART, (dense_cols + down_cols) // PART
    outs = [shape(rows, dense_cols, BF16), shape(rows, down_cols, BF16), shape(1, down_cols, F32)]
    return grid_call(
        functools.partial(backward_kernel, split),
        steps,
        outs,
        [
            columns_spec(rows, 0, split - 1),
            columns_spec(rows, -split, steps - split - 1),
            columns_spec(1, -split, steps - split - 1),
        ],
        (cot, weights, slope),
        [
            whole_spec(cot),
            pl.BlockSpec((*weights.shape[:3], PART), lambda i: (0, 0, 0, i)),
            columns_spec(rows, -split, steps - split - 1),
        ],
    )


def finish_back_kernel(kept_ref, got_ref, dense_ref, down_ref):
    total = kept_ref[...].astype(F32) + got_ref[...].astype(F32)
    first = dense_ref.shape[0]
    dense_ref[...] = total[:, :first].T
    down_ref[...] = total[:, first:].T


def finish_in_kernel(row_ref, kept_ref, got_ref, norm_ref, bias_ref, qkv_ref, up_ref):
    total = kept_ref[...].astype(F32) + got_ref[...].astype(F32)

    def column(which):
        return own_column(row_ref, norm_ref, which, total.shape[0])

    first = 0
    for number, out_ref in enumerate((qkv_ref, up_ref)):
        at = slice(first, first + out_ref.shape[1])
        out_ref[...] = total[:, at] * column(2 * number) + column(2 * number + 1) * bias_ref[:, at]
        first += out_ref.shape[1]


def input_grad_kernel(tok_ref, cot_ref, kept_ref, got_ref, out_ref):
    tok_rows = tok_ref[...].astype(F32)
    center = jnp.mean(tok_rows, axis=-1, keepdims=True)
    centered = tok_rows - center
    variance = jnp.mean(centered * centered, axis=-1, keepdims=True)
    inverse = lax.rsqrt(variance + 1e-05)
    normal = centered * inverse
    u_rows = kept_ref[...] + got_ref[...].astype(F32)
    u_mean = jnp.mean(u_rows, axis=-1, keepdims=True)
    un_mean = jnp.mean(u_rows * normal, axis=-1, keepdims=True)
    d_rows = (u_rows - u_mean - normal * un_mean) * inverse
    out_ref[...] = (cot_ref[...].astype(F32) + d_rows).astype(BF16)


def own_column(row_ref, norm_ref, which, count):
    start = pl.multiple_of(row_ref[0] * count, count)
    square = (count, count)
    diagonal = lax.broadcasted_iota(jnp.int32, square, 0) == lax.broadcasted_iota(jnp.int32, square, 1)
    lanes = norm_ref[which : which + 1, pl.ds(start, count)].astype(F32)
    return jnp.sum(jnp.where(diagonal, jnp.broadcast_to(lanes, square), 0.0), axis=1, keepdims=True)


def prepare_kernel(row_ref, tok_ref, norm_ref, qkv_ref, up_ref, dense_ref, down_ref, qkv_bias_ref, up_bias_ref, normal_ref, out_ref, back_ref):
    tok_rows = tok_ref[...].astype(F32)
    center = jnp.mean(tok_rows, axis=-1, keepdims=True)
    centered = tok_rows - center
    variance = jnp.mean(centered * centered, axis=-1, keepdims=True)
    normal_ref[...] = (centered * lax.rsqrt(variance + 1e-05)).astype(BF16)
    count = qkv_ref.shape[0]

    def placed(bias_ref, width):
        own = bias_ref[...].astype(F32)
        rest = jnp.zeros((1, width - own.shape[1]), F32)
        wide = jnp.broadcast_to(jnp.concatenate([own, rest], 1), (8, width))
        return pltpu.roll(wide, row_ref[0] * own.shape[1], 1)[:1]

    lines = []
    first = 0
    for number, weight, bias in ((0, qkv_ref, qkv_bias_ref), (2, up_ref, up_bias_ref)):
        width = weight.shape[1]
        wide = weight[...].astype(F32)
        out_ref[:, first : first + width] = (wide * own_column(row_ref, norm_ref, number, count)).astype(BF16)
        shifted = jnp.sum(wide * own_column(row_ref, norm_ref, number + 1, count), axis=0, keepdims=True)
        shifted = shifted + placed(bias, width)
        lines += [shifted[:, 128 * i : 128 * (i + 1)] for i in range(width // 128)]
        first += width
    first_back = 0
    for weight in (dense_ref, down_ref):
        width = weight.shape[0]
        back_ref[:, first_back : first_back + width] = weight[...].astype(F32).T.astype(BF16)
        first_back += width
    high = [line.astype(BF16).astype(F32) for line in lines]
    low = [line - part for line, part in zip(lines, high)]
    rest = jnp.zeros((count - 2 * len(lines), 128), F32)
    out_ref[:, first:] = jnp.concatenate([*high, *low, rest], 0).astype(BF16)


def vmem_call(kernel, outs, args, scratch=(), scalars=0, limit=40):
    spec = pl.BlockSpec()
    scalar = pl.BlockSpec(memory_space=pltpu.SMEM)
    return pl.pallas_call(
        kernel,
        out_shape=outs,
        in_specs=[scalar] * scalars + [spec] * (len(args) - scalars),
        out_specs=[spec] * len(outs),
        scratch_shapes=scratch,
        compiler_params=pltpu.CompilerParams(vmem_limit_bytes=limit * 1024 * 1024),
        cost_estimate=light(),
    )(*args)


def shape(rows, columns, dtype):
    return jax.ShapeDtypeStruct((rows, columns), dtype)


def attend_back(qkv, grad, logs, cosine, sine, doc_col, doc_row):
    rows = qkv.shape[0]
    outs = (shape(rows, 3 * HS, BF16), shape(1, 3 * HS, F32))
    return vmem_call(
        attend_back_kernel,
        outs,
        (qkv, grad, logs, cosine, sine, doc_col, doc_row),
        scratch=[pltpu.VMEM((rows, HS), F32), pltpu.VMEM((rows, HS), F32)],
    )


def doc_layout(lengths, places):
    first, second = lengths[0], lengths[0] + lengths[1]
    third = second + lengths[2]
    passed = [(places >= end).astype(jnp.int32) for end in (first, second, third)]
    doc_ids = passed[0] + passed[1] + passed[2]
    begins = passed[0] * lengths[0] + passed[1] * lengths[1] + passed[2] * lengths[2]
    return (doc_ids, places - begins)


def rotary_tables(positions):
    half = ROT // 2
    lane = jnp.arange(128, dtype=jnp.int32)
    frequency = 1.0 / 10000.0 ** ((lane % half).astype(F32) * (2.0 / ROT))
    frequency = jnp.where(lane < ROT, frequency, 0.0)
    angles = positions.astype(F32) * frequency[None, :]
    sign = jnp.where(lane < half, -1.0, 1.0)
    return (jnp.cos(angles), jnp.sin(angles) * sign[None, :])


def shards(
    tokens,
    doc_lengths,
    input_gain,
    input_shift,
    post_gain,
    post_shift,
    qkv_weight,
    qkv_bias,
    dense_weight,
    dense_bias,
    up_weight,
    up_bias,
    down_weight,
    down_bias,
    cotangent,
):
    row_index = (lax.axis_index("xh") * 4 + lax.axis_index("y")) * 2 + lax.axis_index("c")
    slice_rows = qkv_weight.shape[0]
    qkv_cols, up_cols = qkv_weight.shape[1], up_weight.shape[1]

    tok_count, width = tokens.shape
    vectors = jnp.concatenate([input_gain, input_shift, post_gain, post_shift]).astype(F32).reshape(4, width)
    back_cols = (dense_weight.shape[0], down_weight.shape[0])
    own_normal, block, block_back = vmem_call(
        prepare_kernel,
        (
            shape(tok_count, width, BF16),
            shape(slice_rows, qkv_cols + up_cols + 128, BF16),
            shape(slice_rows, sum(back_cols), BF16),
        ),
        (
            row_index.astype(jnp.int32)[None],
            tokens,
            vectors,
            qkv_weight,
            up_weight,
            dense_weight,
            down_weight,
            qkv_bias[None],
            up_bias[None],
        ),
        scalars=1,
        limit=60,
    )
    xh = lax.axis_index("xh")

    def pair_of(own, other):
        return jnp.stack([jnp.where(xh == first, own, other) for first in range(2)])

    row_count = 8 * tok_count
    doc_col, positions = doc_layout(doc_lengths[0], jnp.arange(row_count, dtype=jnp.int32)[:, None])
    doc_row, _ = doc_layout(doc_lengths[0], jnp.arange(row_count, dtype=jnp.int32)[None, :])
    tables = (*rotary_tables(positions), doc_col, doc_row)

    normal = {("at", "own"): own_normal}
    cot = {("at", "own"): cotangent}
    block_other = hop(block, xh=1)
    normal["back", "own"], normal["ahead", "own"] = ring_near(own_normal, "z")
    block_own, block_other, near_back, own_normal, own_cot, own_back, *tables = all_after(
        [block, block_other, normal["back", "own"], own_normal, cotangent, block_back, *tables],
        [normal["ahead", "own"]],
    )
    weights = gather_row_near(pair_of(block_own, block_other))
    normal["at", "other"] = hop(own_normal, xl=1)
    normal["far", "own"] = hop(near_back, z=1)
    cot["ahead", "own"] = hop(own_cot, z=3)
    normal_other, own_cot, own_back = all_after(
        [normal["at", "other"], own_cot, own_back], [normal["far", "own"], cot["ahead", "own"]]
    )
    normal["back", "other"], normal["ahead", "other"] = ring_near(normal_other, "z")
    cot["at", "other"] = hop(own_cot, xl=1)
    back_other = hop(own_back, xh=1)
    ahead_other, own_cot, cot_ahead = all_after(
        [normal["ahead", "other"], own_cot, cot["ahead", "own"]], [normal["back", "other"]]
    )
    normal["far", "other"] = hop(ahead_other, z=3)
    cot["back", "own"] = hop(own_cot, z=1)
    cot["ahead", "other"] = hop(cot_ahead, xl=1)
    far_other, own_back, back_other, cot_back, cot_other = all_after(
        [normal["far", "other"], own_back, back_other, cot["back", "own"], cot["at", "other"]], []
    )
    normal["far", "other"] = far_other
    back_weights = gather_row_near(pair_of(own_back, back_other))
    normal_all = rows_of_group(normal)
    cot["far", "own"] = hop(cot_back, z=1)
    cot["far", "other"] = hop(cot_other, z=2)
    cot["back", "other"] = hop(cot_back, xl=1)

    qkv, attended, logs, active, slope = forward(normal_all, weights, qkv_cols, up_cols, tables)
    late = (("far", "own"), ("far", "other"), ("back", "other"))
    qkv, *held = all_after([qkv, *[cot[place] for place in late]], [])
    cot_all = rows_of_group(cot | dict(zip(late, held)))
    (back_grads,) = weight_grads(cot_all, attended, active)
    back_pair = scatter_row_near(back_grads)
    attended, active = all_after([attended, active], [back_grads])
    out_far = project_far(attended, active, back_weights)
    out_first = scatter_col_first(out_far)
    attended, active = all_after([attended, active], [out_far[0]])
    out_near = project_near_halves(attended, active, back_weights)
    out_early = scatter_col_early(out_near)

    cot_all = after(cot_all, out_near[0])
    d_attended, d_hidden, up_bias_part = backward(cot_all, back_weights, slope, *back_cols)
    d_attended, d_hidden, *out_first = all_after([d_attended, d_hidden, *out_first], [])
    out_late = scatter_col_late(out_near, out_first)
    d_mixture, qkv_bias_part = attend_back(qkv, d_attended, logs, *tables)
    biases = jnp.concatenate([qkv_bias_part, up_bias_part], 1)
    in_grads, sums = weight_grads(normal_all, d_mixture, d_hidden, (vectors, weights, biases))
    in_grads, sums, d_mixture, d_hidden, *out_got = all_after(
        [in_grads, sums, d_mixture, d_hidden, *out_early, *out_late], []
    )
    in_pair = scatter_row_near(in_grads)

    cot_sum = jnp.sum(cotangent.astype(F32), axis=0, keepdims=True)
    biases = jnp.pad(biases, ((0, 0), (0, width - biases.shape[1])))
    line = jnp.arange(8)[:, None]
    packed = jnp.where(line == 4, cot_sum, jnp.where(line == 5, biases, sums))
    packed = packed + hop(packed, c=1)
    u_far = project_far(d_mixture, d_hidden, weights)
    packed, d_mixture, d_hidden, back_pair, *u_far = all_after(
        [packed, d_mixture, d_hidden, back_pair, *u_far], []
    )
    u_first = scatter_col_first(u_far)
    packed = packed + hop(packed, xh=1)
    back_kept, back_got = scatter_row_far(back_pair)
    back_early, ahead_early, back_late, ahead_late = out_got
    out_parts = ((back_late, ahead_early), (back_early, ahead_late))
    out_kept, out_got = scatter_col_third(out_near[4], out_parts)
    u_near = project_near(d_mixture, d_hidden, weights)
    packed, back_got, out_got, *held = all_after([packed, back_got, out_got, *u_near, *u_first], [])
    u_near, u_first = held[:3], held[3:]
    u_second = scatter_col_second(u_near, u_first)
    packed = packed + jnp.where(line == 5, 0.0, hop(packed, xl=1))
    layer_out = (
        tokens.astype(F32)
        + (out_kept + out_got.astype(F32))
        + dense_bias.astype(F32)
        + down_bias.astype(F32)
    ).astype(BF16)
    packed = packed + hop(packed, y=1) + hop(packed, y=2) + hop(packed, y=3)
    bias_total = packed[5:6]
    qkv_bias_total = lax.dynamic_slice_in_dim(
        packed[5], row_index * qkv_bias.shape[0], qkv_bias.shape[0], 0
    )
    up_bias_total = lax.dynamic_slice_in_dim(
        packed[5], qkv_cols + row_index * up_bias.shape[0], up_bias.shape[0], 0
    )
    in_kept, in_got = scatter_row_far(in_pair)
    packed, in_got, *u_second = all_after([packed, in_got, *u_second], [layer_out])
    half = tok_count
    u_parts = [[part[place * half : (place + 1) * half] for part in u_second] for place in range(2)]
    u_kept, u_got = scatter_col_third(u_near[2], u_parts)
    packed = packed + swap(packed, "z")
    packed = packed + hop(packed, z=2)

    def flat(kept, got):
        return (kept.reshape(slice_rows, -1), got.reshape(slice_rows, -1))

    dense_total, down_total = vmem_call(
        finish_back_kernel,
        tuple(shape(cols, slice_rows, F32) for cols in back_cols),
        flat(back_kept, back_got),
    )
    qkv_total, up_total = vmem_call(
        finish_in_kernel,
        tuple(shape(slice_rows, cols, F32) for cols in (qkv_cols, up_cols)),
        (row_index.astype(jnp.int32)[None], *flat(in_kept, in_got), vectors, bias_total),
        scalars=1,
    )
    (input_grad,) = vmem_call(
        input_grad_kernel,
        (shape(tok_count, width, BF16),),
        (tokens, cotangent, u_kept, u_got),
    )

    return (
        layer_out,
        input_grad,
        packed[0],
        packed[1],
        packed[2],
        packed[3],
        qkv_total,
        qkv_bias_total,
        dense_total,
        packed[4],
        up_total,
        up_bias_total,
        down_total,
        packed[4],
    )


def solution(mesh):
    fine = Mesh(mesh.devices.reshape(tuple(SIZES.values())), NAMES)
    everywhere = P(ROW + COL, None)
    return jax.shard_map(
        shards,
        mesh=fine,
        in_specs=(
            everywhere,
            P(ROW, None),
            P(),
            P(),
            P(),
            P(),
            P(ROW, COL),
            P(COL + ROW),
            P(COL, ROW),
            P(),
            P(ROW, COL),
            P(COL + ROW),
            P(COL, ROW),
            P(),
            everywhere,
        ),
        out_specs=(
            everywhere,
            everywhere,
            P(),
            P(),
            P(),
            P(),
            P(ROW, COL),
            P(COL + ROW),
            P(COL, ROW),
            P(),
            P(ROW, COL),
            P(COL + ROW),
            P(COL, ROW),
            P(),
        ),
        check_vma=False,
    )
```

```python
import functools
import itertools
import math

import jax
import jax.numpy as jnp
from jax import lax
from jax.experimental import pallas as pl
from jax.experimental.pallas import tpu as pltpu
from jax.sharding import Mesh
from jax.sharding import PartitionSpec as P

HS = 256
ROT = 64
BLOCK = 256
SIZES = {"xh": 2, "y": 4, "c": 2, "z": 4, "xl": 2}
NAMES = tuple(SIZES)
ROW = ("xh", "y", "c")
COL = ("z", "xl")
F32 = jnp.float32
BF16 = jnp.bfloat16


def light():
    return pl.CostEstimate(flops=1, bytes_accessed=1, transcendentals=0)


def hop(value, **deltas):
    return send(value, tuple(deltas), lambda coords: [c + deltas[name] for name, c in coords.items()])


def swap(value, axis):
    return send(value, (axis,), lambda coords: [coords[axis] ^ 1])


def send(value, names, target):
    axes = tuple(name for name in NAMES if name in names)

    def flat(coords):
        index = 0
        for name, place in zip(axes, coords):
            index = index * SIZES[name] + place % SIZES[name]
        return index

    pairs = []
    for coords in itertools.product(*[range(SIZES[name]) for name in axes]):
        pairs.append((flat(coords), flat(target(dict(zip(axes, coords))))))
    return lax.ppermute(value, axes if len(axes) > 1 else axes[0], pairs)


def rows_at(value, start, count):
    return lax.dynamic_slice_in_dim(value, start, count, 0)


def after(value, *others):
    return lax.optimization_barrier((value, *others))[0]


def all_after(values, others):
    return list(lax.optimization_barrier((*values, *others))[: len(values)])


def ring_near(pair, axis):
    return [hop(pair, **{axis: 1}), hop(pair, **{axis: 3})]


def places(axis, pair):
    at, own = lax.axis_index(axis), lax.axis_index(pair)
    return {
        "at": at,
        "back": (at + 3) % 4,
        "ahead": (at + 1) % 4,
        "far": (at + 2) % 4,
        "own": own,
        "other": 1 - own,
    }


def group_kernel(count, places_ref, *refs):
    *sources, out_ref = refs
    for number, source in enumerate(sources):
        start = pl.multiple_of(places_ref[number] * count, count)
        out_ref[pl.ds(start, count), :] = source[...]


def rows_of_group(blocks):
    count, width = blocks["at", "own"].shape
    at = places("z", "xl")
    index = jnp.stack([at[place] * 2 + at[pair] for place, pair in blocks]).astype(jnp.int32)
    part = width // 4
    (whole,) = grid_call(
        functools.partial(group_kernel, count),
        4,
        [shape(8 * count, width, BF16)],
        [pl.BlockSpec((8 * count, part), lambda i: (0, i))],
        (index, *blocks.values()),
        [pl.BlockSpec(memory_space=pltpu.SMEM)]
        + [pl.BlockSpec((count, part), lambda i: (0, i)) for _ in blocks],
        limit=60,
    )
    return whole


def gather_row_near(pair):
    return lax.all_gather(pair, ("y", "c"), axis=0)


def scatter_col_first(far):
    return [hop(far[0], z=1), hop(far[1], z=3)]


def scatter_col_second(near, first):
    low, high = first
    up, down = near[:2]
    count = low.shape[0]
    up = jnp.concatenate([up[:count] + low, up[count:]], 0)
    down = jnp.concatenate([down[:count], down[count:] + high], 0)
    return [hop(up, z=1), hop(down, z=3)]


def scatter_col_early(near):
    return [hop(near[1], z=1), hop(near[2], z=3)]


def scatter_col_late(near, first):
    return [hop(near[0] + first[0], z=1), hop(near[3] + first[1], z=3)]


def scatter_col_third(own, parts):
    mine = lax.axis_index("xl") == 0
    count = own.shape[0] // 2
    halves = [
        sum(part.astype(F32) for part in (own[place * count : (place + 1) * count], *got))
        for place, got in enumerate(parts)
    ]
    kept, sent = jnp.where(mine, halves[0], halves[1]), jnp.where(mine, halves[1], halves[0])
    return kept, hop(sent.astype(BF16), xl=1)


def scatter_row_near(blocks):
    return lax.psum_scatter(blocks.reshape(8, *blocks.shape[2:]), ("y", "c"), scatter_dimension=0)


def scatter_row_far(pair):
    xh = lax.axis_index("xh")
    kept = lax.dynamic_index_in_dim(pair, xh, 0, keepdims=False)
    sent = lax.dynamic_index_in_dim(pair, 1 - xh, 0, keepdims=False)
    return kept, hop(sent, xh=1)


def nt(left, right):
    return lax.dot_general(left, right, (((1,), (1,)), ((), ())), preferred_element_type=F32)


def tn(left, right):
    return lax.dot_general(left, right, (((0,), (0,)), ((), ())), preferred_element_type=F32)


def nn(left, right):
    return jnp.dot(left, right, preferred_element_type=F32)


def turn(part, cosine, sine):
    lane = lax.broadcasted_iota(jnp.int32, part.shape, 1)
    ahead = pltpu.roll(part, 128 - ROT // 2, 1)
    behind = pltpu.roll(part, ROT // 2, 1)
    return part * cosine + jnp.where(lane < ROT // 2, ahead, behind) * sine


def block_allowed(doc_col, doc_row, start, width):
    docs = doc_col[start : start + BLOCK] == doc_row[:, :width]
    row = start + lax.broadcasted_iota(jnp.int32, (BLOCK, width), 0)
    column = lax.broadcasted_iota(jnp.int32, (BLOCK, width), 1)
    return docs & (column <= row)


def attend(mix_ref, cos_ref, sin_ref, doc_col_ref, doc_row_ref, qkv_ref, out_ref, log_ref):
    rows = mix_ref.shape[1]
    for start in range(0, rows, BLOCK):
        at = pl.ds(start, BLOCK)
        cosine, sine = cos_ref[at, :], sin_ref[at, :]
        for part in range(2):
            first = part * HS
            qkv_ref[at, first : first + 128] = turn(mix_ref[part, at, :128], cosine, sine).astype(BF16)
            qkv_ref[at, first + 128 : first + HS] = mix_ref[part, at, 128:].astype(BF16)
        qkv_ref[at, 2 * HS :] = mix_ref[2, at, :].astype(BF16)
    doc_row = doc_row_ref[...]
    doc_col = doc_col_ref[...]
    for start in range(0, rows, BLOCK):
        width = start + BLOCK
        at = pl.ds(start, BLOCK)
        scores = nt(qkv_ref[at, :HS], qkv_ref[:width, HS : 2 * HS]) * HS ** (-0.5)
        scores = jnp.where(block_allowed(doc_col, doc_row, start, width), scores, -1e30)
        top = jnp.max(scores, axis=1, keepdims=True)
        raised = jnp.exp(scores - top)
        total = jnp.sum(raised, axis=1, keepdims=True)
        probabilities = (raised * (1.0 / total)).astype(BF16)
        out_ref[at, :] = nn(probabilities, qkv_ref[:width, 2 * HS :]).astype(BF16)
        log_ref[at, :] = top + jnp.log(total)


def attend_back_kernel(qkv_ref, grad_ref, log_ref, cos_ref, sin_ref, doc_col_ref, doc_row_ref, out_ref, sum_ref, dk_ref, dv_ref):
    rows = qkv_ref.shape[0]
    scaling = HS ** (-0.5)
    doc_row = doc_row_ref[...]
    doc_col = doc_col_ref[...]
    sums = [jnp.zeros((1, HS), F32) for _ in range(3)]

    def finish(value, start, first):
        at = pl.ds(start, BLOCK)
        head = turn(value[:, :128], cos_ref[at, :], -sin_ref[at, :]).astype(BF16)
        rest = value[:, 128:].astype(BF16)
        out_ref[at, first : first + 128] = head
        out_ref[at, first + 128 : first + HS] = rest
        both = jnp.concatenate([head.astype(F32), rest.astype(F32)], 1)
        return jnp.sum(both, axis=0, keepdims=True)

    for start in range(0, rows, BLOCK):
        width = start + BLOCK
        at = pl.ds(start, BLOCK)
        query = qkv_ref[at, :HS]
        grad = grad_ref[at, :]
        scores = nt(query, qkv_ref[:width, HS : 2 * HS]) * scaling
        allowed = block_allowed(doc_col, doc_row, start, width)
        weights = jnp.where(allowed, jnp.exp(scores - log_ref[at, :]), 0.0)
        probabilities = weights.astype(BF16)
        d_probs = nt(grad, qkv_ref[:width, 2 * HS :])
        inner = jnp.sum(weights * d_probs, axis=1, keepdims=True)
        d_scores = (weights * (d_probs - inner)).astype(BF16)
        d_values = tn(probabilities, grad)
        d_keys = tn(d_scores, query) * scaling
        if start:
            dv_ref[:start, :] += d_values[:start]
            dk_ref[:start, :] += d_keys[:start]
        dv_ref[start:width, :] = d_values[start:]
        dk_ref[start:width, :] = d_keys[start:]
        d_query = nn(d_scores, qkv_ref[:width, HS : 2 * HS]) * scaling
        sums[0] = sums[0] + finish(d_query, start, 0)
    for start in range(0, rows, BLOCK):
        at = pl.ds(start, BLOCK)
        sums[1] = sums[1] + finish(dk_ref[at, :], start, HS)
        values = dv_ref[at, :].astype(BF16)
        out_ref[at, 2 * HS :] = values
        sums[2] = sums[2] + jnp.sum(values.astype(F32), axis=0, keepdims=True)
    for part in range(3):
        sum_ref[:, part * HS : (part + 1) * HS] = sums[part]


PART = 256


def whole_spec(array):
    return pl.BlockSpec(array.shape, lambda i: (0,) * array.ndim)


def columns_spec(rows, first=0, last=None):
    if last is None:
        return pl.BlockSpec((rows, PART), lambda i: (0, i + first))
    return pl.BlockSpec((rows, PART), lambda i: (0, jnp.clip(i + first, 0, last)))


def grid_call(kernel, steps, outs, out_specs, args, in_specs, scratch=(), limit=48):
    return pl.pallas_call(
        kernel,
        grid=(steps,),
        out_shape=tuple(outs),
        in_specs=in_specs,
        out_specs=tuple(out_specs),
        scratch_shapes=scratch,
        compiler_params=pltpu.CompilerParams(vmem_limit_bytes=limit * 1024 * 1024),
        cost_estimate=light(),
    )(*args)


def quarter_spec(weights, width):
    block = (weights.shape[0] // 2, 1, weights.shape[2], width)
    return pl.BlockSpec(block, lambda i: (i % 2, i // 2, 0, 0))


def project_kernel(count, z_ref, *refs):
    row_refs, weight_ref, out_refs, both_ref = refs[: 2 * count], refs[2 * count], refs[2 * count + 1 : -1], refs[-1]

    @pl.when(pl.program_id(0) == 0)
    def _():
        for number in range(count):
            one_ref, two_ref = row_refs[2 * number : 2 * number + 2]
            part, split = one_ref.shape
            at = slice(number * part, (number + 1) * part)
            both_ref[at, :split] = one_ref[...]
            both_ref[at, split:] = two_ref[...]

    block = weight_ref[...].reshape(-1, weight_ref.shape[-1])
    total = nt(both_ref[...], block).astype(BF16)
    first = 0
    for out_ref in out_refs:
        out_ref[...] = total[first : first + out_ref.shape[0]]
        first += out_ref.shape[0]


def project(one, two, weights, steps, counts):
    width = one.shape[1] + two.shape[1]
    features = math.prod(weights.shape[:3])
    step = features // 4
    part = one.shape[0] // 4
    block = (weights.shape[0] // 2, 1, weights.shape[2], width)
    row_specs = [
        pl.BlockSpec((part, side.shape[1]), lambda i, z, ahead=ahead: ((z[0] + ahead) % 4, 0))
        for ahead in steps
        for side in (one, two)
    ]
    z = lax.axis_index("z").astype(jnp.int32)[None]
    return pl.pallas_call(
        functools.partial(project_kernel, len(steps)),
        grid_spec=pltpu.PrefetchScalarGridSpec(
            num_scalar_prefetch=1,
            grid=(4,),
            in_specs=[*row_specs, pl.BlockSpec(block, lambda i, z: (i % 2, i // 2, 0, 0))],
            out_specs=tuple(pl.BlockSpec((count, step), lambda i, z: (0, i)) for count in counts),
            scratch_shapes=[pltpu.VMEM((sum(counts), width), BF16)],
        ),
        out_shape=tuple(shape(count, features, BF16) for count in counts),
        compiler_params=pltpu.CompilerParams(vmem_limit_bytes=48 * 1024 * 1024),
        cost_estimate=light(),
    )(z, *([one, two] * len(steps)), weights)


def project_far(one, two, weights):
    eighth = one.shape[0] // 8
    return project(one, two, weights, (2,), (eighth, eighth))


def project_near(one, two, weights):
    quarter = one.shape[0] // 4
    return project(one, two, weights, (1, 3, 0), (quarter, quarter, quarter))


def project_near_halves(one, two, weights):
    eighth = one.shape[0] // 8
    return project(one, two, weights, (1, 3, 0), (eighth,) * 4 + (2 * eighth,))


def back_grads_kernel(left_ref, one_ref, two_ref, out_ref):
    block = out_ref.shape[:-1]
    first = 0
    for right_ref in (one_ref, two_ref):
        width = right_ref.shape[1]
        values = tn(left_ref[...], right_ref[...]).astype(BF16)
        out_ref[..., first : first + width] = values.reshape(*block, width)
        first += width


def in_grads_kernel(left_ref, one_ref, two_ref, norm_ref, weight_ref, bias_ref, out_ref, sums_ref):
    block = out_ref.shape[:-1]
    first = 0
    rows = []
    for number, right_ref in enumerate((one_ref, two_ref)):
        gain_sum = shift_sum = jnp.zeros((left_ref.shape[1], 128), F32)
        for part in range(0, right_ref.shape[1], PART):
            at = slice(first + part, first + part + PART)
            raw = tn(left_ref[...], right_ref[:, part : part + PART])
            wide = weight_ref[..., at].astype(F32).reshape(raw.shape)
            gain_part, shift_part = wide * raw, wide * bias_ref[:, at]
            gain_sum = gain_sum + gain_part[:, :128] + gain_part[:, 128:]
            shift_sum = shift_sum + shift_part[:, :128] + shift_part[:, 128:]
            out_ref[..., at] = raw.astype(BF16).reshape(*block, PART)
        gain = norm_ref[2 * number : 2 * number + 1, :]
        rows += [jnp.sum(part.T, axis=0, keepdims=True) / gain for part in (gain_sum, shift_sum)]
        first += right_ref.shape[1]
    sums_ref[...] = jnp.concatenate([*rows, jnp.zeros((4, left_ref.shape[1]), F32)], 0)


def weight_grads(left, one, two, extra=None):
    rows, features = left.shape
    count = features // 16
    step = 4 * count
    width = one.shape[1] + two.shape[1]
    args = [left, one, two]
    in_specs = [pl.BlockSpec((rows, step), lambda i: (0, i)), whole_spec(one), whole_spec(two)]
    outs = [jax.ShapeDtypeStruct((4, 2, 2, count, width), BF16)]
    out_specs = [pl.BlockSpec((2, 2, 1, count, width), lambda i: (i % 2, 0, i // 2, 0, 0))]
    kernel = back_grads_kernel
    if extra is not None:
        kernel = in_grads_kernel
        vectors, weights, bias = extra
        args += [vectors, weights, bias]
        in_specs += [
            pl.BlockSpec((vectors.shape[0], step), lambda i: (0, i)),
            quarter_spec(weights, width),
            whole_spec(bias),
        ]
        outs.append(shape(8, features, F32))
        out_specs.append(pl.BlockSpec((8, step), lambda i: (0, i)))
    return grid_call(kernel, features // step, outs, out_specs, args, in_specs)


def gelu_pair(hidden):
    normal = 0.5 * (1.0 + lax.erf(hidden * (1.0 / math.sqrt(2.0))))
    density = jnp.exp(-0.5 * hidden * hidden) * (1.0 / math.sqrt(2.0 * math.pi))
    return (hidden * normal, normal + hidden * density)


def natural(ref):
    return jnp.concatenate([ref[:, xh].reshape(-1, ref.shape[-1]) for xh in range(2)], 0)


def forward_kernel(split, normal_ref, weight_ref, extra_ref, cos_ref, sin_ref, doc_col_ref, doc_row_ref, qkv_ref, att_ref, log_ref, active_ref, slope_ref, bias_ref, mix_ref):
    step = pl.program_id(0)
    weight = natural(weight_ref)

    @pl.when(step == 0)
    def _():
        total = jnp.zeros((32, 128), F32)
        for place in range(extra_ref.shape[0]):
            for xh in range(2):
                total = total + extra_ref[place, xh, :32, :].astype(F32)
        lines = 14
        for line in range(lines):
            both = total[line : line + 1] + total[lines + line : lines + line + 1]
            bias_ref[line // 2 : line // 2 + 1, 128 * (line % 2) : 128 * (line % 2 + 1)] = both

    bias = bias_ref[pl.ds(step, 1), :]

    @pl.when(step < split)
    def _():
        mix_ref[step] = nn(normal_ref[...], weight) + bias

    @pl.when(step == split)
    def _():
        attend(mix_ref, cos_ref, sin_ref, doc_col_ref, doc_row_ref, qkv_ref, att_ref, log_ref)

    @pl.when(step >= split)
    def _():
        rows = normal_ref.shape[0]
        for start in range(0, rows, 256):
            at = slice(start, start + 256)
            active, slope = gelu_pair(nn(normal_ref[at, :], weight) + bias)
            active_ref[at, :] = active.astype(BF16)
            slope_ref[at, :] = slope.astype(BF16)


def forward(normal, weights, qkv_cols, up_cols, tables):
    rows, features = normal.shape
    split, steps = qkv_cols // PART, (qkv_cols + up_cols) // PART
    early = [shape(rows, qkv_cols, BF16), shape(rows, HS, BF16), shape(rows, 1, F32)]
    late = columns_spec(rows, -split, steps - split - 1)
    extra_place = weights.shape[-1] // 128 - 1
    return grid_call(
        functools.partial(forward_kernel, split),
        steps,
        early + [shape(rows, up_cols, BF16)] * 2,
        [whole_spec(out) for out in early] + [late, late],
        (normal, weights, weights, *tables),
        [
            whole_spec(normal),
            pl.BlockSpec((*weights.shape[:3], PART), lambda i: (0, 0, 0, i)),
            pl.BlockSpec((*weights.shape[:3], 128), lambda i: (0, 0, 0, extra_place)),
            *[whole_spec(table) for table in tables],
        ],
        scratch=[pltpu.VMEM((8, PART), F32), pltpu.VMEM((split, rows, PART), F32)],
    )


def backward_kernel(split, cot_ref, weight_ref, slope_ref, att_ref, hid_ref, sum_ref):
    def product():
        return nn(cot_ref[...], natural(weight_ref))

    @pl.when(pl.program_id(0) < split)
    def _():
        att_ref[...] = product().astype(BF16)

    @pl.when(pl.program_id(0) >= split)
    def _():
        value = (product() * slope_ref[...].astype(F32)).astype(BF16)
        hid_ref[...] = value
        sum_ref[...] = jnp.sum(value.astype(F32), axis=0, keepdims=True)


def backward(cot, weights, slope, dense_cols, down_cols):
    rows, features = cot.shape
    split, steps = dense_cols // PART, (dense_cols + down_cols) // PART
    outs = [shape(rows, dense_cols, BF16), shape(rows, down_cols, BF16), shape(1, down_cols, F32)]
    return grid_call(
        functools.partial(backward_kernel, split),
        steps,
        outs,
        [
            columns_spec(rows, 0, split - 1),
            columns_spec(rows, -split, steps - split - 1),
            columns_spec(1, -split, steps - split - 1),
        ],
        (cot, weights, slope),
        [
            whole_spec(cot),
            pl.BlockSpec((*weights.shape[:3], PART), lambda i: (0, 0, 0, i)),
            columns_spec(rows, -split, steps - split - 1),
        ],
    )


def finish_back_kernel(kept_ref, got_ref, dense_ref, down_ref):
    total = kept_ref[...].astype(F32) + got_ref[...].astype(F32)
    first = dense_ref.shape[0]
    dense_ref[...] = total[:, :first].T
    down_ref[...] = total[:, first:].T


def finish_in_kernel(row_ref, kept_ref, got_ref, norm_ref, bias_ref, qkv_ref, up_ref):
    total = kept_ref[...].astype(F32) + got_ref[...].astype(F32)

    def column(which):
        return own_column(row_ref, norm_ref, which, total.shape[0])

    first = 0
    for number, out_ref in enumerate((qkv_ref, up_ref)):
        at = slice(first, first + out_ref.shape[1])
        out_ref[...] = total[:, at] * column(2 * number) + column(2 * number + 1) * bias_ref[:, at]
        first += out_ref.shape[1]


def input_grad_kernel(tok_ref, cot_ref, kept_ref, got_ref, out_ref):
    tok_rows = tok_ref[...].astype(F32)
    center = jnp.mean(tok_rows, axis=-1, keepdims=True)
    centered = tok_rows - center
    variance = jnp.mean(centered * centered, axis=-1, keepdims=True)
    inverse = lax.rsqrt(variance + 1e-05)
    normal = centered * inverse
    u_rows = kept_ref[...] + got_ref[...].astype(F32)
    u_mean = jnp.mean(u_rows, axis=-1, keepdims=True)
    un_mean = jnp.mean(u_rows * normal, axis=-1, keepdims=True)
    d_rows = (u_rows - u_mean - normal * un_mean) * inverse
    out_ref[...] = (cot_ref[...].astype(F32) + d_rows).astype(BF16)


def own_column(row_ref, norm_ref, which, count):
    start = pl.multiple_of(row_ref[0] * count, count)
    square = (count, count)
    diagonal = lax.broadcasted_iota(jnp.int32, square, 0) == lax.broadcasted_iota(jnp.int32, square, 1)
    lanes = norm_ref[which : which + 1, pl.ds(start, count)].astype(F32)
    return jnp.sum(jnp.where(diagonal, jnp.broadcast_to(lanes, square), 0.0), axis=1, keepdims=True)


def prepare_kernel(row_ref, tok_ref, norm_ref, qkv_ref, up_ref, dense_ref, down_ref, qkv_bias_ref, up_bias_ref, normal_ref, out_ref, back_ref):
    tok_rows = tok_ref[...].astype(F32)
    center = jnp.mean(tok_rows, axis=-1, keepdims=True)
    centered = tok_rows - center
    variance = jnp.mean(centered * centered, axis=-1, keepdims=True)
    normal_ref[...] = (centered * lax.rsqrt(variance + 1e-05)).astype(BF16)
    count = qkv_ref.shape[0]

    def placed(bias_ref, width):
        own = bias_ref[...].astype(F32)
        rest = jnp.zeros((1, width - own.shape[1]), F32)
        wide = jnp.broadcast_to(jnp.concatenate([own, rest], 1), (8, width))
        return pltpu.roll(wide, row_ref[0] * own.shape[1], 1)[:1]

    lines = []
    first = 0
    for number, weight, bias in ((0, qkv_ref, qkv_bias_ref), (2, up_ref, up_bias_ref)):
        width = weight.shape[1]
        wide = weight[...].astype(F32)
        out_ref[:, first : first + width] = (wide * own_column(row_ref, norm_ref, number, count)).astype(BF16)
        shifted = jnp.sum(wide * own_column(row_ref, norm_ref, number + 1, count), axis=0, keepdims=True)
        shifted = shifted + placed(bias, width)
        lines += [shifted[:, 128 * i : 128 * (i + 1)] for i in range(width // 128)]
        first += width
    first_back = 0
    for weight in (dense_ref, down_ref):
        width = weight.shape[0]
        back_ref[:, first_back : first_back + width] = weight[...].astype(F32).T.astype(BF16)
        first_back += width
    high = [line.astype(BF16).astype(F32) for line in lines]
    low = [line - part for line, part in zip(lines, high)]
    rest = jnp.zeros((count - 2 * len(lines), 128), F32)
    out_ref[:, first:] = jnp.concatenate([*high, *low, rest], 0).astype(BF16)


def vmem_call(kernel, outs, args, scratch=(), scalars=0, limit=40):
    spec = pl.BlockSpec()
    scalar = pl.BlockSpec(memory_space=pltpu.SMEM)
    return pl.pallas_call(
        kernel,
        out_shape=outs,
        in_specs=[scalar] * scalars + [spec] * (len(args) - scalars),
        out_specs=[spec] * len(outs),
        scratch_shapes=scratch,
        compiler_params=pltpu.CompilerParams(vmem_limit_bytes=limit * 1024 * 1024),
        cost_estimate=light(),
    )(*args)


def shape(rows, columns, dtype):
    return jax.ShapeDtypeStruct((rows, columns), dtype)


def attend_back(qkv, grad, logs, cosine, sine, doc_col, doc_row):
    rows = qkv.shape[0]
    outs = (shape(rows, 3 * HS, BF16), shape(1, 3 * HS, F32))
    return vmem_call(
        attend_back_kernel,
        outs,
        (qkv, grad, logs, cosine, sine, doc_col, doc_row),
        scratch=[pltpu.VMEM((rows, HS), F32), pltpu.VMEM((rows, HS), F32)],
    )


def doc_layout(lengths, places):
    first, second = lengths[0], lengths[0] + lengths[1]
    third = second + lengths[2]
    passed = [(places >= end).astype(jnp.int32) for end in (first, second, third)]
    doc_ids = passed[0] + passed[1] + passed[2]
    begins = passed[0] * lengths[0] + passed[1] * lengths[1] + passed[2] * lengths[2]
    return (doc_ids, places - begins)


def rotary_tables(positions):
    half = ROT // 2
    lane = jnp.arange(128, dtype=jnp.int32)
    frequency = 1.0 / 10000.0 ** ((lane % half).astype(F32) * (2.0 / ROT))
    frequency = jnp.where(lane < ROT, frequency, 0.0)
    angles = positions.astype(F32) * frequency[None, :]
    sign = jnp.where(lane < half, -1.0, 1.0)
    return (jnp.cos(angles), jnp.sin(angles) * sign[None, :])


def shards(
    tokens,
    doc_lengths,
    input_gain,
    input_shift,
    post_gain,
    post_shift,
    qkv_weight,
    qkv_bias,
    dense_weight,
    dense_bias,
    up_weight,
    up_bias,
    down_weight,
    down_bias,
    cotangent,
):
    row_index = (lax.axis_index("xh") * 4 + lax.axis_index("y")) * 2 + lax.axis_index("c")
    slice_rows = qkv_weight.shape[0]
    qkv_cols, up_cols = qkv_weight.shape[1], up_weight.shape[1]

    tok_count, width = tokens.shape
    vectors = jnp.concatenate([input_gain, input_shift, post_gain, post_shift]).astype(F32).reshape(4, width)
    back_cols = (dense_weight.shape[0], down_weight.shape[0])
    own_normal, block, block_back = vmem_call(
        prepare_kernel,
        (
            shape(tok_count, width, BF16),
            shape(slice_rows, qkv_cols + up_cols + 128, BF16),
            shape(slice_rows, sum(back_cols), BF16),
        ),
        (
            row_index.astype(jnp.int32)[None],
            tokens,
            vectors,
            qkv_weight,
            up_weight,
            dense_weight,
            down_weight,
            qkv_bias[None],
            up_bias[None],
        ),
        scalars=1,
        limit=60,
    )
    xh = lax.axis_index("xh")

    def pair_of(own, other):
        return jnp.stack([jnp.where(xh == first, own, other) for first in range(2)])

    row_count = 8 * tok_count
    doc_col, positions = doc_layout(doc_lengths[0], jnp.arange(row_count, dtype=jnp.int32)[:, None])
    doc_row, _ = doc_layout(doc_lengths[0], jnp.arange(row_count, dtype=jnp.int32)[None, :])
    tables = (*rotary_tables(positions), doc_col, doc_row)

    normal = {("at", "own"): own_normal}
    cot = {("at", "own"): cotangent}
    block_other = hop(block, xh=1)
    normal["back", "own"], normal["ahead", "own"] = ring_near(own_normal, "z")
    block_own, block_other, near_back, own_normal, own_cot, own_back, *tables = all_after(
        [block, block_other, normal["back", "own"], own_normal, cotangent, block_back, *tables],
        [normal["ahead", "own"]],
    )
    weights = gather_row_near(pair_of(block_own, block_other))
    normal["at", "other"] = hop(own_normal, xl=1)
    normal["far", "own"] = hop(near_back, z=1)
    cot["ahead", "own"] = hop(own_cot, z=3)
    normal_other, own_cot, own_back = all_after(
        [normal["at", "other"], own_cot, own_back], [normal["far", "own"], cot["ahead", "own"]]
    )
    normal["back", "other"], normal["ahead", "other"] = ring_near(normal_other, "z")
    cot["at", "other"] = hop(own_cot, xl=1)
    back_other = hop(own_back, xh=1)
    ahead_other, own_cot, cot_ahead = all_after(
        [normal["ahead", "other"], own_cot, cot["ahead", "own"]], [normal["back", "other"]]
    )
    normal["far", "other"] = hop(ahead_other, z=3)
    cot["back", "own"] = hop(own_cot, z=1)
    cot["ahead", "other"] = hop(cot_ahead, xl=1)
    far_other, own_back, back_other, cot_back, cot_other = all_after(
        [normal["far", "other"], own_back, back_other, cot["back", "own"], cot["at", "other"]], []
    )
    normal["far", "other"] = far_other
    back_weights = gather_row_near(pair_of(own_back, back_other))
    normal_all = rows_of_group(normal)
    cot["far", "own"] = hop(cot_back, z=1)
    cot["far", "other"] = hop(cot_other, z=2)
    cot["back", "other"] = hop(cot_back, xl=1)

    qkv, attended, logs, active, slope = forward(normal_all, weights, qkv_cols, up_cols, tables)
    late = (("far", "own"), ("far", "other"), ("back", "other"))
    qkv, *held = all_after([qkv, *[cot[place] for place in late]], [])
    cot_all = rows_of_group(cot | dict(zip(late, held)))
    (back_grads,) = weight_grads(cot_all, attended, active)
    back_pair = scatter_row_near(back_grads)
    attended, active = all_after([attended, active], [back_grads])
    out_far = project_far(attended, active, back_weights)
    out_first = scatter_col_first(out_far)
    attended, active = all_after([attended, active], [out_far[0]])
    out_near = project_near_halves(attended, active, back_weights)
    out_early = scatter_col_early(out_near)

    cot_all = after(cot_all, out_near[0])
    d_attended, d_hidden, up_bias_part = backward(cot_all, back_weights, slope, *back_cols)
    d_attended, d_hidden, *out_first = all_after([d_attended, d_hidden, *out_first], [])
    out_late = scatter_col_late(out_near, out_first)
    d_mixture, qkv_bias_part = attend_back(qkv, d_attended, logs, *tables)
    biases = jnp.concatenate([qkv_bias_part, up_bias_part], 1)
    in_grads, sums = weight_grads(normal_all, d_mixture, d_hidden, (vectors, weights, biases))
    in_grads, sums, d_mixture, d_hidden, *out_got = all_after(
        [in_grads, sums, d_mixture, d_hidden, *out_early, *out_late], []
    )
    in_pair = scatter_row_near(in_grads)

    cot_sum = jnp.sum(cotangent.astype(F32), axis=0, keepdims=True)
    biases = jnp.pad(biases, ((0, 0), (0, width - biases.shape[1])))
    line = jnp.arange(8)[:, None]
    packed = jnp.where(line == 4, cot_sum, jnp.where(line == 5, biases, sums))
    packed = packed + hop(packed, c=1)
    u_far = project_far(d_mixture, d_hidden, weights)
    packed, d_mixture, d_hidden, back_pair, *u_far = all_after(
        [packed, d_mixture, d_hidden, back_pair, *u_far], []
    )
    u_first = scatter_col_first(u_far)
    packed = packed + hop(packed, xh=1)
    back_kept, back_got = scatter_row_far(back_pair)
    back_early, ahead_early, back_late, ahead_late = out_got
    out_parts = ((back_late, ahead_early), (back_early, ahead_late))
    out_kept, out_got = scatter_col_third(out_near[4], out_parts)
    u_near = project_near(d_mixture, d_hidden, weights)
    packed, back_got, out_got, *held = all_after([packed, back_got, out_got, *u_near, *u_first], [])
    u_near, u_first = held[:3], held[3:]
    u_second = scatter_col_second(u_near, u_first)
    packed = packed + jnp.where(line == 5, 0.0, hop(packed, xl=1))
    layer_out = (
        tokens.astype(F32)
        + (out_kept + out_got.astype(F32))
        + dense_bias.astype(F32)
        + down_bias.astype(F32)
    ).astype(BF16)
    packed = packed + hop(packed, y=1) + hop(packed, y=2) + hop(packed, y=3)
    bias_total = packed[5:6]
    qkv_bias_total = lax.dynamic_slice_in_dim(
        packed[5], row_index * qkv_bias.shape[0], qkv_bias.shape[0], 0
    )
    up_bias_total = lax.dynamic_slice_in_dim(
        packed[5], qkv_cols + row_index * up_bias.shape[0], up_bias.shape[0], 0
    )
    in_kept, in_got = scatter_row_far(in_pair)
    packed, in_got, *u_second = all_after([packed, in_got, *u_second], [layer_out])
    half = tok_count
    u_parts = [[part[place * half : (place + 1) * half] for part in u_second] for place in range(2)]
    u_kept, u_got = scatter_col_third(u_near[2], u_parts)
    packed = packed + swap(packed, "z")
    packed = packed + hop(packed, z=2)

    def flat(kept, got):
        return (kept.reshape(slice_rows, -1), got.reshape(slice_rows, -1))

    dense_total, down_total = vmem_call(
        finish_back_kernel,
        tuple(shape(cols, slice_rows, F32) for cols in back_cols),
        flat(back_kept, back_got),
    )
    qkv_total, up_total = vmem_call(
        finish_in_kernel,
        tuple(shape(slice_rows, cols, F32) for cols in (qkv_cols, up_cols)),
        (row_index.astype(jnp.int32)[None], *flat(in_kept, in_got), vectors, bias_total),
        scalars=1,
    )
    (input_grad,) = grid_call(
        input_grad_kernel,
        4,
        [shape(tok_count, width, BF16)],
        [pl.BlockSpec((tok_count // 4, width), lambda i: (i, 0))],
        (tokens, cotangent, u_kept, u_got),
        [pl.BlockSpec((tok_count // 4, width), lambda i: (i, 0))] * 4,
        limit=40,
    )

    return (
        layer_out,
        input_grad,
        packed[0],
        packed[1],
        packed[2],
        packed[3],
        qkv_total,
        qkv_bias_total,
        dense_total,
        packed[4],
        up_total,
        up_bias_total,
        down_total,
        packed[4],
    )


def solution(mesh):
    fine = Mesh(mesh.devices.reshape(tuple(SIZES.values())), NAMES)
    everywhere = P(ROW + COL, None)
    return jax.shard_map(
        shards,
        mesh=fine,
        in_specs=(
            everywhere,
            P(ROW, None),
            P(),
            P(),
            P(),
            P(),
            P(ROW, COL),
            P(COL + ROW),
            P(COL, ROW),
            P(),
            P(ROW, COL),
            P(COL + ROW),
            P(COL, ROW),
            P(),
            everywhere,
        ),
        out_specs=(
            everywhere,
            everywhere,
            P(),
            P(),
            P(),
            P(),
            P(ROW, COL),
            P(COL + ROW),
            P(COL, ROW),
            P(),
            P(ROW, COL),
            P(COL + ROW),
            P(COL, ROW),
            P(),
        ),
        check_vma=False,
    )
```
